32 devices in a mesh: pipe: 2 (over x), dp: 4 (over z), tensor: 4 (over y, core).
Axes of the slice: x: 2, y: 2, z: 4, core: 2. Of those that a mesh axis runs over, the one named last changes fastest.
Arguments:
- inputs: bfloat16 [2, 12, 1024, 512], P('pipe', 'dp', 'tensor'), may hold values from -6 to 6
- cotangent: bfloat16 [2, 12, 1024, 512], P('pipe', 'dp', 'tensor'), may hold values from -6 to 6
- segments: int32 [2, 12, 1024], P(None, 'dp'), may hold values from 0 to 7, never falling along the last dimension, each value on 1 to 256 neighbouring positions
- pads: int32 [2, 12, 1024], P('pipe', 'dp'), may hold values 0 or 1
- self_qkv: bfloat16 [2, 512, 3, 512], P('pipe', None, None, 'tensor'), may hold values from -0.25 to 0.25
- self_bias: float32 [2, 2, 512], P('pipe', None, 'tensor'), may hold values from -3 to 3
- self_out: bfloat16 [2, 512, 512], P('pipe', 'tensor'), may hold values from -1 to 1
- ff_in: bfloat16 [2, 512, 2048], P('pipe', None, 'tensor'), may hold values from -0.25 to 0.25
- ff_bias: bfloat16 [2, 2048], P('pipe', 'tensor'), may hold values from -3 to 3
- ff_out: bfloat16 [2, 2048, 512], P('pipe', 'tensor'), may hold values from -0.125 to 0.125
- vectors: float32 [2, 6, 512], P('pipe'), may hold values from -2 to 2, as said below
- cross_q: bfloat16 [512, 512], P('pipe', 'tensor'), may hold values from -0.25 to 0.25
- cross_kv: bfloat16 [512, 2, 512], P('pipe', None, 'tensor'), may hold values from -0.25 to 0.25
- cross_out: bfloat16 [512, 512], P('tensor', 'pipe'), may hold values from -1 to 1
- cross_small: bfloat16 [4, 512], P('pipe'), may hold values from -3 to 3
- cross_gain: bfloat16 [512], P('pipe'), may hold values from 0.099609375 to 1.8984375
Outputs:
- section_out: bfloat16 [2, 12, 1024, 512], P('pipe', 'dp', 'tensor')
- input_grad: float32 [2, 12, 1024, 512], P('pipe', 'dp', 'tensor')
- qkv_grad: float32 [2, 512, 3, 512], P('pipe', None, None, 'tensor')
- self_bias_grad: float32 [2, 2, 512], P('pipe', None, 'tensor')
- self_out_grad: float32 [2, 512, 512], P('pipe', 'tensor')
- ff_in_grad: float32 [2, 512, 2048], P('pipe', None, 'tensor')
- ff_bias_grad: float32 [2, 2048], P('pipe', 'tensor')
- ff_out_grad: float32 [2, 2048, 512], P('pipe', 'tensor')
- vectors_grad: float32 [2, 6, 512], P('pipe')
- cross_q_grad: float32 [512, 512], P('pipe', 'tensor')
- cross_kv_grad: float32 [512, 2, 512], P('pipe', None, 'tensor')
- cross_out_grad: float32 [512, 512], P('tensor', 'pipe')
- cross_small_grad: float32 [4, 512], P('pipe')
- cross_gain_grad: float32 [512], P('pipe')
The draws below stay inside these ranges and needn't reach their ends.
Inputs may be any that keep to these rules, and one draw needn't show every extreme that they name: `segments`: in each row the ids never fall and each of the 8 ids covers 1 to 256 slots, one of them exactly 256. `vectors`: rows 2 and 4 of each section, the norms' gains, lie in 0.4 to 1.6.
All inputs are finite; a program needn't handle non-finite values. No bound on the sum of `pads` on one device may be relied on, other than what follows from the above.
Results may differ from the reference program's by a relative error of at most 0.028.
Values may be sent and summed in bfloat16 or wider, within the bound.
No kernel may reach another device: no remote copies, remote signals or barrier semaphores. Data moves between devices by JAX's collectives and lax.ppermute only.
A program may use at most 256 MiB of HBM per device.

```python
import math
import jax
import jax.numpy as jnp
import numpy as np
from jax import lax

D = 512
HEADS = 8
HEAD_DIM = 64
FF = 2048
LEN = 1024
SEGS = 8
MOST = 256
ROWS = 12


def draw_vectors(key, part):
    key = jax.random.fold_in(key, 7)
    first_key, second_key = jax.random.split(key)
    row_index = jnp.arange(6)[None, :, None]
    gain_rows = ((row_index == 2) | (row_index == 4)).astype(jnp.float32)
    shift_values = jnp.clip(0.5 * jax.random.normal(first_key, (2, 6, D), jnp.float32), -2.0, 2.0)
    gain_values = jnp.clip(1.0 + 0.25 * jax.random.normal(second_key, (2, 6, D), jnp.float32), 0.4, 1.6)
    return gain_rows * gain_values + (1.0 - gain_rows) * shift_values


def place_ends(values, own_key, least, high):
    dims = values.shape
    spot = [jax.random.randint(jax.random.fold_in(own_key, axis), (), 0, dims[axis]) for axis in range(len(dims))]
    values = values.at[tuple(spot)].set(least)
    longest = dims.index(max(dims))
    spot[longest] = (spot[longest] + 1) % dims[longest]
    return values.at[tuple(spot)].set(high)


def steps_of(own_key, extent, shards, smallest, top_value):
    loudness = 1.0
    for position, parts in shards:
        steps = jax.random.uniform(jax.random.fold_in(jax.random.fold_in(own_key, 6), position), (parts,), jnp.float32, smallest / len(shards), top_value / len(shards))
        loudness = loudness * jnp.repeat(jnp.exp(steps), extent[position] // parts).reshape((-1,) + (1,) * (len(extent) - 1 - position))
    return loudness


def split_up(count, total, limit, skew):
    loads = [(1 << 20) // math.isqrt(rank ** skew) + 1 for rank in range(2, count + 1)]
    rest, given = total - limit - (count - 1), [1] * (count - 1)
    while rest > 0:
        candidates = [i for i in range(count - 1) if given[i] < limit]
        whole, budget = sum([loads[i] for i in candidates]), rest
        for i in candidates:
            addition = min(limit - given[i], max(1, budget * loads[i] // whole), rest)
            given[i] = given[i] + addition
            rest = rest - addition
    return np.array([limit] + given)


def ragged_sizes(stream_key, count, total, reach, lean):
    if count == 2:
        one = jax.random.randint(stream_key, (), max(1, total - reach), min(reach, total - 1) + 1)
        return jnp.stack([one, total - one])
    sizes = jnp.asarray(split_up(count, total, reach, lean), jnp.int32)
    couples = (count - 1) // 2
    donor, taker = sizes[1:1 + 2 * couples:2], sizes[2:2 + 2 * couples:2]
    room = jnp.minimum(donor - 1, reach - taker)
    passed = jax.random.randint(jax.random.fold_in(stream_key, 1), (couples,), 0, 1 << 20) % (room + 1)
    sizes = sizes.at[1:1 + 2 * couples:2].set(donor - passed).at[2:2 + 2 * couples:2].set(taker + passed)
    return sizes[jax.random.permutation(jax.random.fold_in(stream_key, 2), count)]


def scatter_about(stream_key, shape, scale, limit, cuts=(), dtype=jnp.bfloat16):
    entries = jax.random.normal(stream_key, shape, jnp.float32) * scale
    if len(cuts) > 0:
        entries = steps_of(stream_key, shape, cuts, -0.22, 0.18) * entries
    return jnp.clip(entries, min=-limit, max=limit).astype(dtype)


def setup_inputs(seed: int = 0) -> dict:
    seeds = jax.random.split(jax.random.key(seed), 17)
    return {
        "inputs": scatter_about(seeds[0], (2, ROWS, LEN, D), 1.0, 6.0, ((0, 2), (1, 4), (2, 4))),
        "cotangent": scatter_about(seeds[1], (2, ROWS, LEN, D), 1.0, 6.0, ((0, 2), (1, 4), (2, 4))),
        "segments": jax.vmap(lambda own: jnp.searchsorted(jnp.cumsum(ragged_sizes(own, SEGS, LEN, MOST, 1)), jnp.arange(LEN), side="right"))(jax.random.split(seeds[2], 2 * ROWS)).reshape((2, ROWS, LEN)).astype(jnp.int32),
        "pads": place_ends((jax.random.randint(seeds[3], (2, ROWS, LEN), 0, 8) < 1).astype(jnp.int32), jax.random.fold_in(seeds[3], 1), 0, 1),
        "self_qkv": scatter_about(seeds[4], (2, D, 3, D), D ** -0.5, 0.25, ((0, 2), (3, 4))),
        "self_bias": scatter_about(seeds[5], (2, 2, D), 0.5, 3.0, ((0, 2), (2, 4)), jnp.float32),
        "self_out": scatter_about(seeds[6], (2, D, D), (D // 16) ** -0.5, 1.0, ((0, 2), (1, 4))),
        "ff_in": scatter_about(seeds[7], (2, D, FF), D ** -0.5, 0.25, ((0, 2), (2, 4))),
        "ff_bias": scatter_about(seeds[8], (2, FF), 0.5, 3.0, ((0, 2), (1, 4))),
        "ff_out": scatter_about(seeds[9], (2, FF, D), FF ** -0.5, 0.125, ((0, 2), (1, 4))),
        "vectors": draw_vectors(jax.random.fold_in(seeds[16], 71), 0),
        "cross_q": scatter_about(seeds[11], (D, D), D ** -0.5, 0.25, ((0, 2), (1, 4))),
        "cross_kv": scatter_about(seeds[12], (D, 2, D), D ** -0.5, 0.25, ((0, 2), (2, 4))),
        "cross_out": scatter_about(seeds[13], (D, D), (D // 16) ** -0.5, 1.0, ((0, 4), (1, 2))),
        "cross_small": scatter_about(seeds[14], (4, D), 0.5, 3.0, ((0, 2),)),
        "cross_gain": jnp.clip(1.0 + 0.18 * jax.random.normal(seeds[15], (D,), jnp.float32), 0.099609375, 1.8984375).astype(jnp.bfloat16),
    }


EPSILON = 1e-05
MASKED = -1e+30

@jax.custom_vjp
def low(v):
    return lax.optimization_barrier(v.astype(jnp.bfloat16)).astype(jnp.float32)

@jax.custom_vjp
def low_back(v):
    return v

def low_keep(v):
    return (low(v), None)

def low_pass(kept, grad):
    return (grad,)

def back_keep(v):
    return (v, None)

def back_low(kept, grad):
    return (low(grad),)
low.defvjp(low_keep, low_pass)
low_back.defvjp(back_keep, back_low)

def matmul(left, right):
    return jnp.dot(left, right, precision=lax.Precision.HIGHEST)

def both_ways(values):
    return low(low_back(values))

def layer_norm(values, norm_gain, norm_shift):
    center = values - lax.optimization_barrier(jnp.mean(values, -1, keepdims=True))
    inverse = lax.rsqrt(lax.optimization_barrier(jnp.mean(center * center, -1, keepdims=True)) + EPSILON)
    return center * inverse * norm_gain + norm_shift

def attention(query_in, key_in, query_weight, query_bias, key_weight, value_weight, value_bias, allowed):
    query_rows = query_in.shape[0]
    key_rows = key_in.shape[0]
    queries = both_ways(matmul(query_in, query_weight) + query_bias).reshape(query_rows, HEADS, HEAD_DIM)
    key_heads = both_ways(matmul(key_in, key_weight)).reshape(key_rows, HEADS, HEAD_DIM)
    value_heads = both_ways(matmul(key_in, value_weight) + value_bias).reshape(key_rows, HEADS, HEAD_DIM)
    scores = jnp.einsum('qhd,khd->hqk', queries, key_heads, precision=lax.Precision.HIGHEST) * HEAD_DIM ** (-0.5)
    scores = low_back(scores)
    scores = jnp.where(allowed[None], scores, MASKED)
    largest = lax.optimization_barrier(jnp.max(scores, -1, keepdims=True))
    exponent = jnp.exp(scores - largest)
    probabilities = exponent / lax.optimization_barrier(jnp.sum(exponent, -1, keepdims=True))
    mixed = jnp.einsum('hqk,khd->qhd', low(probabilities), value_heads, precision=lax.Precision.HIGHEST)
    return both_ways(mixed).reshape(query_rows, HEADS * HEAD_DIM)

def run_section(stream, own_segments, own_pads, causal, qkv_weight, self_vec, out_weight, hidden_weight, hidden_bias, back_weight, vector_rows, cross):
    length = stream.shape[0]
    positions = jnp.arange(length)
    allowed = (own_segments[:, None] == own_segments[None, :]) & ((own_pads[None, :] == 0) | (positions[:, None] == positions[None, :]))
    if causal:
        allowed = allowed & (positions[None, :] <= positions[:, None])
    mixed = attention(stream, stream, qkv_weight[:, 0], self_vec[0], qkv_weight[:, 1], qkv_weight[:, 2], self_vec[1], allowed)
    attended = low_back(matmul(mixed, out_weight) + vector_rows[0])
    current = layer_norm(stream + attended, vector_rows[2], vector_rows[3])
    if cross is not None:
        memory, source_segments, query_cross, kv_cross, out_cross, small_cross, gain_cross = cross
        cross_allowed = own_segments[:, None] == source_segments[None, :]
        cross_mixed = attention(low(current), memory, query_cross, small_cross[0], kv_cross[:, 0], kv_cross[:, 1], small_cross[1], cross_allowed)
        crossed = low_back(matmul(cross_mixed, out_cross) + small_cross[2])
        current = layer_norm(current + crossed, gain_cross, small_cross[3])
    pre_act = low_back(matmul(low(current), hidden_weight) + hidden_bias)
    activated = low(jax.nn.gelu(pre_act, approximate=True))
    ffn_out = low_back(matmul(activated, back_weight) + vector_rows[1])
    return layer_norm(current + ffn_out + stream, vector_rows[4], vector_rows[5])

def reference(inputs, cotangent, segments, pads, self_qkv, self_bias, self_out, ff_in, ff_bias, ff_out, vectors, cross_q, cross_kv, cross_out, cross_small, cross_gain):
    weight_list = tuple((leaf_array.astype(jnp.float32) for leaf_array in (self_qkv, self_bias, self_out, ff_in, ff_bias, ff_out, vectors, cross_q, cross_kv, cross_out, cross_small, cross_gain)))
    sources = inputs[0].astype(jnp.float32)
    targets = inputs[1].astype(jnp.float32)

    def whole(weight_tuple, source_rows, target_rows):

        def row_pair(row_items):
            source, target, source_seg, target_seg, source_pad, target_pad = row_items
            qkv_weight, self_vec, out_weight, hidden_weight, hidden_bias, back_weight, vector_rows, query_cross, kv_cross, out_cross, small_cross, gain_cross = weight_tuple
            encoded = run_section(source, source_seg, source_pad, False, qkv_weight[0], self_vec[0], out_weight[0], hidden_weight[0], hidden_bias[0], back_weight[0], vector_rows[0], None)
            memory = low(encoded)
            decoded = run_section(target, target_seg, target_pad, True, qkv_weight[1], self_vec[1], out_weight[1], hidden_weight[1], hidden_bias[1], back_weight[1], vector_rows[1], (low_back(memory), source_seg, query_cross, kv_cross, out_cross, small_cross, gain_cross))
            return (memory, decoded)
        return lax.map(jax.checkpoint(row_pair), (source_rows, target_rows, segments[0], segments[1], pads[0], pads[1]))
    results, pullback = jax.vjp(whole, weight_list, sources, targets)
    gradients, source_grad, target_grad = pullback((cotangent[0].astype(jnp.float32), cotangent[1].astype(jnp.float32)))
    section_out = jnp.stack([results[0], results[1]]).astype(jnp.bfloat16)
    input_grad = jnp.stack([source_grad, target_grad])
    return (section_out, input_grad, gradients[0], gradients[1], gradients[2], gradients[3], gradients[4], gradients[5], gradients[6], gradients[7], gradients[8], gradients[9], gradients[10], gradients[11])
```

```python
import functools

import jax
import jax.numpy as jnp
from jax import lax
from jax.experimental import pallas as pl
from jax.experimental.pallas import tpu as pltpu
from jax.sharding import PartitionSpec as P

HEAD_DIM = 64
EPSILON = 1e-05
MASKED = -1e30
SEGS = 8
QF = 256
QB = 256
TB = 512
PAIR = 2 * HEAD_DIM
GELU_C = 0.7978845608028654
GELU_A = 0.044715
VMEM_LIMIT = 56 * 1024 * 1024
F32 = jnp.float32
BF16 = jnp.bfloat16


def dot(left, right):
    return jnp.dot(left, right, preferred_element_type=F32)


def dot_t(left, right):
    return lax.dot_general(left, right, (((1,), (1,)), ((), ())), preferred_element_type=F32)


def dot_tl(left, right):
    return lax.dot_general(left, right, (((0,), (0,)), ((), ())), preferred_element_type=F32)


def normed_of(values):
    center = values - jnp.mean(values, -1, keepdims=True)
    inverse = lax.rsqrt(jnp.mean(center * center, -1, keepdims=True) + EPSILON)
    return center * inverse, inverse


def norm_back(grad, normed, inverse, gain):
    scaled = grad * gain
    mean_scaled = jnp.mean(scaled, -1, keepdims=True)
    mean_both = jnp.mean(scaled * normed, -1, keepdims=True)
    return (scaled - mean_scaled - normed * mean_both) * inverse


def column_sum(values):
    return jnp.sum(values.astype(F32), 0, keepdims=True)


def gelu_parts(pre):
    squared = pre * pre
    half = 0.5 * jnp.tanh(pre * (GELU_C + (GELU_C * GELU_A) * squared)) + 0.5
    slope = half + (pre * (half - half * half)) * (2.0 * GELU_C + (6.0 * GELU_C * GELU_A) * squared)
    return pre * half, slope


def cost(flops, moved):
    return pl.CostEstimate(flops=int(flops) // 64, bytes_accessed=int(moved) // 64, transcendentals=0)


def params(axes=1):
    return pltpu.CompilerParams(
        dimension_semantics=("arbitrary",) * axes, vmem_limit_bytes=VMEM_LIMIT
    )


def find_segments(section, slots_ref, own_ref, key_ref, target_ref, source_ref, self_ref, cross_ref):
    length = slots_ref.shape[1]
    source = slots_ref[0:1, :].astype(F32)
    target = slots_ref[1:2, :].astype(F32)
    own = jnp.where(section == 1, target, source)
    own_ref[...] = own
    key_ref[...] = jnp.where(slots_ref[2:3, :] == 0, own, -1.0)
    target_ref[...] = target
    source_ref[...] = source

    def starts(segments):
        found = [jnp.int32(0)]
        for index in range(1, SEGS):
            found.append(jnp.sum(jnp.where(segments < float(index), 1.0, 0.0)).astype(jnp.int32))
        return found + [jnp.int32(length)]

    source_starts, target_starts = starts(source), starts(target)
    for index in range(SEGS):
        own_start = jnp.where(section == 1, target_starts[index], source_starts[index])
        own_end = jnp.where(section == 1, target_starts[index + 1], source_starts[index + 1])
        self_ref[index] = own_start
        self_ref[16 + index] = own_start
        self_ref[32 + index] = own_end
        cross_ref[index] = target_starts[index]
        cross_ref[16 + index] = source_starts[index]
        cross_ref[32 + index] = source_starts[index + 1]
    self_ref[48] = jnp.int32(1)
    self_ref[49] = section
    self_ref[50] = jnp.int32(1)
    cross_ref[48] = jnp.int32(0)
    cross_ref[49] = jnp.int32(0)
    cross_ref[50] = section


def half_masked(values, side):
    lane = lax.broadcasted_iota(jnp.int32, values.shape, 1)
    return jnp.where((lane >= HEAD_DIM) == bool(side), values, jnp.zeros_like(values))


def key_window(bounds, block, block_rows):
    first = block * block_rows
    last = first + (block_rows - 1)
    low, high = jnp.int32(0), jnp.int32(0)
    for index in range(SEGS):
        low = jnp.where(bounds[index] <= first, bounds[16 + index], low)
        high = jnp.where(bounds[index] <= last, bounds[32 + index], high)
    high = jnp.where(bounds[49] == 1, jnp.minimum(high, last + 1), high)
    low_block = lax.shift_right_logical(low, 7)
    high_block = lax.shift_right_logical(high + 127, 7)
    return low_block, jnp.where(bounds[50] == 1, high_block - low_block, 0)


def by_size(bounds, block, block_rows, key_blocks, sizes, body):
    low_block, needed = key_window(bounds, block, block_rows)
    below = 0
    for size in sizes:
        size = min(size, key_blocks)
        if size == below:
            continue

        @pl.when((needed > below) & (needed <= size))
        def _(size=size):
            start = jnp.minimum(low_block, key_blocks - size) * 128
            body(size, pl.multiple_of(start, 128))

        below = size


def as_columns(row):
    parts = []
    for at in range(0, row.shape[1], 128):
        parts.append(jnp.broadcast_to(row[:, at:at + 128], (128, 128)).T)
    return jnp.concatenate(parts, 0)


def window_bias(bounds, block, block_rows, start, key_code, qcode_ref):
    key_at = start + lax.broadcasted_iota(jnp.int32, key_code.shape, 0)
    tiles = []
    for at in range(0, block_rows, 128):
        query_at = block * block_rows + at + lax.broadcasted_iota(jnp.int32, (1, 128), 1)
        limit = jnp.where(bounds[49] == 1, query_at, jnp.int32(1 << 30))
        same_at = jnp.where(bounds[48] == 1, query_at, -1)
        opened = (key_code == qcode_ref[:, at:at + 128]) & (key_at <= limit)
        tiles.append(jnp.where(opened | (key_at == same_at), 0.0, MASKED))
    return jnp.concatenate(tiles, 1)


def attend_forward_kernel(bounds, q_ref, k_ref, v_ref, qcode_ref, kcode_ref, mixed_ref, total_ref):
    block = pl.program_id(0)
    heads = q_ref.shape[1] // HEAD_DIM
    key_blocks = k_ref.shape[0] // 128
    own_code = as_columns(qcode_ref[...])
    query_at = block * QF + lax.broadcasted_iota(jnp.int32, (QF, 128), 0)
    limit = jnp.where(bounds[49] == 1, query_at, jnp.int32(1 << 30))
    same_at = jnp.where(bounds[48] == 1, query_at, -1)
    lane = lax.broadcasted_iota(jnp.int32, (QF, 128), 1)

    def body(size, start):
        window = pl.ds(start, size * 128)
        tiles = []
        for tile in range(size):
            at = start + tile * 128
            key_at = at + lane
            opened = (own_code == kcode_ref[:, pl.ds(pl.multiple_of(at, 128), 128)]) & (key_at <= limit)
            tiles.append(jnp.where(opened | (key_at == same_at), 0.0, MASKED))
        bias = jnp.concatenate(tiles, 1)

        def two_pairs(index, columns):
            lanes = [pl.ds(pl.multiple_of((2 * index + at) * PAIR, PAIR), PAIR) for at in range(2)]
            scores = []
            for at in range(2):
                queries, keys = q_ref[:, lanes[at]], k_ref[window, lanes[at]]
                scores.append([dot_t(half_masked(queries, side), keys) + bias for side in range(2)])
            for at in range(2):
                values = v_ref[window, lanes[at]]
                out = None
                for side in range(2):
                    top = jnp.max(scores[at][side], -1, keepdims=True)
                    weights = jnp.exp(scores[at][side] - top)
                    total = jnp.sum(weights, -1, keepdims=True)
                    part = dot(weights.astype(BF16), half_masked(values, side)) * (1.0 / total)
                    out = part if out is None else out + part
                    columns = jnp.where(lane == (2 * index + at) * 2 + side, top + jnp.log(total), columns)
                mixed_ref[:, lanes[at]] = out.astype(BF16)
            return columns

        columns = lax.fori_loop(0, heads // 4, two_pairs, jnp.zeros((QF, 128), F32))
        total_ref[...] = columns.T[:heads]

    by_size(bounds, block, QF, key_blocks, (2, 3, 4, 5, 6, 8), body)


def attend_forward(bounds, codes, width, queries, keys, values):
    (q_array, q_at), (k_array, k_at), (v_array, v_at) = queries, keys, values
    rows = q_array.shape[0]
    heads = width // HEAD_DIM
    whole = lambda at: (lambda i, *_: (0, at))
    return pl.pallas_call(
        attend_forward_kernel,
        grid_spec=pltpu.PrefetchScalarGridSpec(
            num_scalar_prefetch=1,
            grid=(rows // QF,),
            in_specs=[
                pl.BlockSpec((QF, width), lambda i, *_: (i, q_at)),
                pl.BlockSpec((rows, width), whole(k_at)),
                pl.BlockSpec((rows, width), whole(v_at)),
                pl.BlockSpec((1, QF), lambda i, *_: (0, i)),
                pl.BlockSpec((1, rows), whole(0)),
            ],
            out_specs=[
                pl.BlockSpec((QF, width), lambda i, *_: (i, 0)),
                pl.BlockSpec((heads, QF), lambda i, *_: (0, i)),
            ],
        ),
        out_shape=[
            jax.ShapeDtypeStruct((rows, width), BF16),
            jax.ShapeDtypeStruct((heads, rows), F32),
        ],
        compiler_params=params(),
        cost_estimate=cost(4 * rows * 512 * width * 2, 8 * rows * width),
        name="attend_forward",
    )(bounds, q_array, k_array, v_array, *codes)


def attend_backward_kernel(has_weight, first_head, bounds, q_ref, k_ref, v_ref, grad_ref, total_ref, qcode_ref, kcode_ref, *refs):
    if has_weight:
        weight_ref, dq_ref, dk_ref, dv_ref, dmem_ref, kcol_ref, dkacc_ref, dvacc_ref = refs
    else:
        dq_ref, dk_ref, dv_ref, kcol_ref, dkacc_ref, dvacc_ref = refs
    block = pl.program_id(0)
    width = q_ref.shape[1]
    heads = width // HEAD_DIM
    key_blocks = k_ref.shape[0] // 128

    @pl.when(block == 0)
    def _():
        dkacc_ref[...] = jnp.zeros(dkacc_ref.shape, F32)
        dvacc_ref[...] = jnp.zeros(dvacc_ref.shape, F32)
        kcol_ref[...] = as_columns(kcode_ref[...])

    def body(size, start):
        window = pl.ds(start, size * 128)
        bias = window_bias(bounds, block, QB, start, kcol_ref[window, :], qcode_ref)

        def pair_step(pair, carry):
            lanes = pl.ds(pl.multiple_of(pair * PAIR, PAIR), PAIR)
            queries, grads = q_ref[:, lanes], grad_ref[:, lanes]
            keys, values = k_ref[window, lanes], v_ref[window, lanes]
            query_halves = [half_masked(queries, side) for side in range(2)]
            grad_halves = [half_masked(grads, side) for side in range(2)]
            products = [
                (dot_t(keys, query_halves[side]) + bias, dot_t(values, grad_halves[side])) for side in range(2)
            ]
            dq = dk = dv = None
            for side in range(2):
                scores, grad_weights = products[side]
                weights = jnp.exp(scores - total_ref[pl.ds(first_head + pair * 2 + side, 1), :])
                delta = jnp.sum(weights * grad_weights, 0, keepdims=True)
                grad_scores = (weights * (grad_weights - delta)).astype(BF16)
                made = (
                    dot_tl(grad_scores, half_masked(keys, side)),
                    dot(grad_scores, query_halves[side]),
                    dot(weights.astype(BF16), grad_halves[side]),
                )
                dq, dk, dv = made if dq is None else (dq + made[0], dk + made[1], dv + made[2])
            dkacc_ref[window, lanes] = dkacc_ref[window, lanes] + dk
            dvacc_ref[window, lanes] = dvacc_ref[window, lanes] + dv
            dq_ref[:, lanes] = (dq * HEAD_DIM ** (-0.5)).astype(BF16)
            return carry

        lax.fori_loop(0, heads // 2, pair_step, 0)

    by_size(bounds, block, QB, key_blocks, (2, 3, 4, 5, 6, 8), body)

    @pl.when(block == pl.num_programs(0) - 1)
    def _():
        dk_ref[...] = dkacc_ref[...].astype(BF16)
        dv_ref[...] = dvacc_ref[...].astype(BF16)
        if has_weight:
            summed = dot_t(dk_ref[...], weight_ref[:, :width]) + dot_t(dv_ref[...], weight_ref[:, width:])
            dmem_ref[...] = summed.astype(BF16)


def attend_backward(bounds, codes, queries, keys, values, grad, totals, weight=None, part=(0, 1)):
    (q_array, q_at), (k_array, k_at), (v_array, v_at) = queries, keys, values
    index, count = part
    rows = grad.shape[0]
    heads = totals.shape[0]
    width = grad.shape[1] // count
    whole = lambda at: pl.BlockSpec((rows, width), lambda i, *_: (0, at * count + index))
    block = lambda at: pl.BlockSpec((QB, width), lambda i, *_: (i, at * count + index))
    extra = [] if weight is None else [weight]
    first = pl.BlockSpec((rows, width), lambda i, *_: (0, 0))
    return pl.pallas_call(
        functools.partial(attend_backward_kernel, weight is not None, index * heads // count),
        grid_spec=pltpu.PrefetchScalarGridSpec(
            num_scalar_prefetch=1,
            grid=(rows // QB,),
            in_specs=[
                block(q_at),
                whole(k_at),
                whole(v_at),
                block(0),
                pl.BlockSpec((heads, QB), lambda i, *_: (0, i)),
                pl.BlockSpec((1, QB), lambda i, *_: (0, i)),
                pl.BlockSpec((1, rows), lambda i, *_: (0, 0)),
            ]
            + [fixed(v.shape) for v in extra],
            out_specs=[pl.BlockSpec((QB, width), lambda i, *_: (i, 0))] + [first] * (2 + len(extra)),
            scratch_shapes=[
                pltpu.VMEM((rows, 128), F32),
                pltpu.VMEM((rows, width), F32),
                pltpu.VMEM((rows, width), F32),
            ],
        ),
        out_shape=[jax.ShapeDtypeStruct((rows, width), BF16)] * (3 + len(extra)),
        compiler_params=params(),
        cost_estimate=cost(10 * rows * 512 * width * 2, 16 * rows * width),
        name="attend_backward",
    )(bounds, q_array, k_array, v_array, grad, totals, *codes, *extra)


def attention_pack_kernel(qkv_ref, out_ref, bias_ref, ffb_ref, pack_ref):
    width = qkv_ref.shape[1]
    lane = qkv_ref.shape[2]
    for index in range(3):
        pack_ref[index * width:(index + 1) * width, :] = qkv_ref[index]
    for index in range(width // lane):
        at = 3 * width + index * lane
        pack_ref[at:at + lane, :] = out_ref[:, index * lane:(index + 1) * lane]
    bias = bias_ref[...]
    high = bias.astype(BF16).astype(F32)
    middle = (bias - high).astype(BF16).astype(F32)
    least = bias - high - middle
    hidden = ffb_ref[...].astype(F32)
    hidden_rows = [hidden[:, at:at + lane] for at in range(0, hidden.shape[1], lane)]
    rest = jnp.zeros((16 - 3 * bias.shape[0] - len(hidden_rows), lane), F32)
    rows = jnp.concatenate([high, middle, least, *hidden_rows, rest], 0)
    pack_ref[4 * width:4 * width + 16, :] = rows.astype(BF16)


def attention_pack(qkv, out_weight, bias, ff_bias):
    width, lane = qkv.shape[1:]
    return pl.pallas_call(
        attention_pack_kernel,
        grid=(1,),
        in_specs=[fixed(v.shape) for v in (qkv, out_weight, bias, ff_bias)],
        out_specs=fixed((4 * width + 16, lane)),
        out_shape=jax.ShapeDtypeStruct((4 * width + 16, lane), BF16),
        compiler_params=params(),
        cost_estimate=cost(0, 16 * width * lane),
        name="attention_pack",
    )(qkv, out_weight, bias, ff_bias)


def query_key_value_kernel(
    flag_ref, x_ref, slots_ref, p0, p1, p2, p3, qkv_ref, weight_ref, out_ref, hidden_ref, *refs
):
    *found_refs, bias_ref = refs
    width = x_ref.shape[1]
    lane = p0.shape[1]

    @pl.when(pl.program_id(0) == 0)
    def _():
        find_segments(flag_ref[0], slots_ref, *found_refs)
        for index, pack in enumerate((p0, p1, p2, p3)):
            columns = slice(index * lane, (index + 1) * lane)
            for part in range(3):
                at = slice(part * width + index * lane, part * width + (index + 1) * lane)
                weight_ref[:, at] = pack[part * width:(part + 1) * width, :]
            for part in range(width // lane):
                at = 3 * width + part * lane
                out_ref[columns, part * lane:(part + 1) * lane] = pack[at:at + lane, :]
            rows = pack[4 * width:4 * width + 16, :].astype(F32)
            bias_ref[0:1, columns] = rows[0:1] + rows[2:3] + rows[4:5]
            bias_ref[1:2, columns] = rows[1:2] + rows[3:4] + rows[5:6]
            for part in range(width // lane):
                hidden_ref[index:index + 1, part * lane:(part + 1) * lane] = rows[6 + part:7 + part]

    made = dot(x_ref[...], weight_ref[...])
    scale = HEAD_DIM ** (-0.5)
    queries = (made[:, :width] + bias_ref[0:1, :]).astype(BF16).astype(F32) * scale
    qkv_ref[:, :width] = queries.astype(BF16)
    qkv_ref[:, width:2 * width] = made[:, width:2 * width].astype(BF16)
    qkv_ref[:, 2 * width:] = (made[:, 2 * width:] + bias_ref[1:2, :]).astype(BF16)


def query_key_value(flag, stream, slots, packs):
    rows, width = stream.shape
    line = jax.ShapeDtypeStruct((1, rows), F32)
    bounds = jax.ShapeDtypeStruct((64,), jnp.int32)
    return pl.pallas_call(
        query_key_value_kernel,
        grid_spec=pltpu.PrefetchScalarGridSpec(
            num_scalar_prefetch=1,
            grid=(rows // TB,),
            in_specs=[tokens(width), fixed(slots.shape)] + [fixed(pack.shape) for pack in packs],
            out_specs=[tokens(3 * width), fixed((width, 3 * width)), fixed((width, width)), fixed((len(packs), width))]
            + [fixed(line.shape)] * 4
            + [pl.BlockSpec(memory_space=pltpu.SMEM)] * 2,
            scratch_shapes=[pltpu.VMEM((8, width), F32)],
        ),
        out_shape=[
            jax.ShapeDtypeStruct((rows, 3 * width), BF16),
            jax.ShapeDtypeStruct((width, 3 * width), BF16),
            jax.ShapeDtypeStruct((width, width), BF16),
            jax.ShapeDtypeStruct((len(packs), width), F32),
        ]
        + [line] * 4
        + [bounds] * 2,
        compiler_params=params(),
        cost_estimate=cost(6 * rows * width * width, 10 * rows * width),
        name="query_key_value",
    )(flag, stream, slots, *packs)


def cross_pack_kernel(query_ref, pair_ref, out_ref, small_ref, gain_ref, pack_ref):
    half, lane = query_ref.shape
    pack_ref[0:half, :] = query_ref[...]
    pack_ref[half:2 * half, :] = pair_ref[0]
    pack_ref[2 * half:3 * half, :] = pair_ref[1]
    for index in range(half // lane):
        at = 3 * half + index * lane
        pack_ref[at:at + lane, :] = out_ref[:, index * lane:(index + 1) * lane]
    small = small_ref[...].astype(F32)
    gain = gain_ref[...].astype(F32)
    rest = jnp.zeros((16 - small.shape[0] - gain.shape[0], lane), F32)
    pack_ref[4 * half:4 * half + 16, :] = jnp.concatenate([small, gain, rest], 0).astype(BF16)


def cross_pack(query, pair, out_weight, small, gain):
    half, lane = query.shape
    return pl.pallas_call(
        cross_pack_kernel,
        grid=(1,),
        in_specs=[fixed(v.shape) for v in (query, pair, out_weight, small, gain)],
        out_specs=fixed((4 * half + 16, lane)),
        out_shape=jax.ShapeDtypeStruct((4 * half + 16, lane), BF16),
        compiler_params=params(),
        cost_estimate=cost(0, 16 * half * lane),
        name="cross_pack",
    )(query, pair, out_weight, small, gain)


def cross_unpack_kernel(place_ref, p0, p1, p2, p3, query_ref, pair_ref, out_ref, cvec_ref):
    lane = p0.shape[1]
    length = p0.shape[0] // 2
    half = (length - 16) // 4
    width = 2 * half
    count = width // lane
    for index, pack in enumerate((p0, p1, p2, p3)):
        columns = slice(index * lane, (index + 1) * lane)
        for side in range(2):
            rows = slice(side * half, (side + 1) * half)
            base = side * length
            query_ref[rows, columns] = pack[base:base + half, :]
            pair_ref[rows, columns] = pack[base + half:base + 2 * half, :]
            pair_ref[rows, width + index * lane:width + (index + 1) * lane] = pack[base + 2 * half:base + 3 * half, :]
            for part in range(half // lane):
                at = base + 3 * half + part * lane
                to = side * half + part * lane
                out_ref[columns, to:to + lane] = pack[at:at + lane, :]
    first = p0[4 * half:4 * half + 16, :].astype(F32)
    second = p0[length + 4 * half:length + 4 * half + 16, :].astype(F32)
    at_row = lax.broadcasted_iota(jnp.int32, (16, lane), 0)
    for index in range(count):
        columns = slice(index * lane, (index + 1) * lane)
        for which in range(2):
            wanted = which * count + (place_ref[0] ^ index)
            cvec_ref[which:which + 1, columns] = jnp.sum(jnp.where(at_row == wanted, first, 0.0), 0, keepdims=True)
        cvec_ref[2:3, columns] = second[index:index + 1]
        cvec_ref[4:5, columns] = second[count + index:count + index + 1]
        side, part = (first, index) if index < count // 2 else (second, index - count // 2)
        cvec_ref[3:4, columns] = side[2 * count + part:2 * count + part + 1]
    cvec_ref[5:8, :] = jnp.zeros((3, width), F32)


def cross_unpack(place, packs):
    length, lane = packs[0].shape
    width = (length // 2 - 16) // 2
    return pl.pallas_call(
        cross_unpack_kernel,
        grid_spec=pltpu.PrefetchScalarGridSpec(
            num_scalar_prefetch=1,
            grid=(1,),
            in_specs=[fixed(pack.shape) for pack in packs],
            out_specs=[fixed((width, width)), fixed((width, 2 * width)), fixed((width, width)), fixed((8, width))],
        ),
        out_shape=[
            jax.ShapeDtypeStruct((width, width), BF16),
            jax.ShapeDtypeStruct((width, 2 * width), BF16),
            jax.ShapeDtypeStruct((width, width), BF16),
            jax.ShapeDtypeStruct((8, width), F32),
        ],
        compiler_params=params(),
        cost_estimate=cost(0, 16 * width * width),
        name="cross_unpack",
    )(place, *packs)


def rows_of(vector, rows, at_row, base, order=None):
    lane = rows.shape[1]
    for index in range(vector.shape[1] // lane):
        to = base + (index if order is None else (order ^ index))
        rows = rows + jnp.where(at_row == to, vector[:, index * lane:(index + 1) * lane], 0.0)
    return rows


def attention_grads_kernel(
    is_cross, parts, place_ref, aq_ref, akv_ref, *refs
):
    width = aq_ref.shape[1]
    dq_refs, dk_refs, dv_refs = (refs[part * parts:(part + 1) * parts] for part in range(3))
    mixed_ref, da_ref, vgrad_ref, bgrad_ref, *packs, made_ref = refs[3 * parts:]
    lane = packs[0].shape[1]
    count = width // lane
    tail = packs[0].shape[0] - 4 * width
    akv = akv_ref if is_cross else aq_ref
    for part, (left, rights) in enumerate(((aq_ref, dq_refs), (akv, dk_refs), (akv, dv_refs))):
        for index, right in enumerate(rights):
            wide = width // parts
            made_ref[:, index * wide:(index + 1) * wide] = dot_tl(left[...], right[...]).astype(BF16)
        for index, pack in enumerate(packs):
            pack[part * width:(part + 1) * width, :] = made_ref[:, index * lane:(index + 1) * lane]
    made_ref[...] = dot_tl(mixed_ref[...], da_ref[...]).astype(BF16)
    for index, pack in enumerate(packs):
        for part in range(count):
            at = 3 * width + part * lane
            pack[at:at + lane, :] = made_ref[index * lane:(index + 1) * lane, part * lane:(part + 1) * lane]
    query_bias, value_bias = (
        jnp.concatenate([column_sum(ref[...]) for ref in some], 1) for some in (dq_refs, dv_refs)
    )
    at_row = lax.broadcasted_iota(jnp.int32, (tail, lane), 0)
    rows = jnp.zeros((tail, lane), F32)
    if is_cross:
        rows = rows_of(query_bias, rows, at_row, 0, place_ref[0])
        rows = rows_of(value_bias, rows, at_row, count, place_ref[0])
        for index in range(3):
            rows = rows_of(vgrad_ref[6 + index:7 + index, :], rows, at_row, (2 + index) * count)
    else:
        for index in range(6):
            rows = rows_of(vgrad_ref[index:index + 1, :], rows, at_row, 16 + index * count)
    for index, pack in enumerate(packs):
        own = rows
        if not is_cross:
            columns = slice(index * lane, (index + 1) * lane)
            own = own + jnp.where(at_row == 0, query_bias[:, columns], 0.0)
            own = own + jnp.where(at_row == 1, value_bias[:, columns], 0.0)
            own = rows_of(bgrad_ref[index:index + 1, :], own, at_row, 2)
        pack[4 * width:, :] = own.astype(BF16)


def attention_grads(is_cross, place, aq, akv, dqkv, mixed, da, vgrad, bgrad, lane):
    rows, width = aq.shape
    length = 4 * width + 64
    operands = (aq, akv, *dqkv, mixed, da, vgrad, bgrad)
    count = width // lane
    return pl.pallas_call(
        functools.partial(attention_grads_kernel, is_cross, len(dqkv) // 3),
        grid_spec=pltpu.PrefetchScalarGridSpec(
            num_scalar_prefetch=1,
            grid=(1,),
            in_specs=[fixed(v.shape) for v in operands],
            out_specs=[fixed((length, lane))] * count,
            scratch_shapes=[pltpu.VMEM((width, width), BF16)],
        ),
        out_shape=[jax.ShapeDtypeStruct((length, lane), BF16)] * count,
        compiler_params=params(),
        cost_estimate=cost(8 * rows * width * width, 14 * rows * width),
        name="cross_grads" if is_cross else "self_grads",
    )(place, *operands)


def feed_forward_grads_kernel(z_ref, du_ref, g_ref, df_ref, *packs):
    width = z_ref.shape[1]
    for index, pack in enumerate(packs):

        @pl.when(pl.program_id(0) == index)
        def _(pack=pack):
            pack[:width, :] = dot_tl(z_ref[...], du_ref[...]).astype(BF16)
            pack[width:, :] = dot_tl(g_ref[...], df_ref[...]).astype(BF16)


def feed_forward_grads(z, du, g, df, first, hidden):
    rows, width = z.shape
    quarter = pl.BlockSpec((rows, hidden), lambda i: (0, first - i))
    pack = (width + hidden, width)
    return pl.pallas_call(
        feed_forward_grads_kernel,
        grid=(2,),
        in_specs=[fixed(z.shape), quarter, quarter, fixed(df.shape)],
        out_specs=[fixed(pack)] * 2,
        out_shape=[jax.ShapeDtypeStruct(pack, BF16)] * 2,
        compiler_params=params(),
        cost_estimate=cost(8 * rows * width * hidden, 12 * rows * hidden),
        name="feed_forward_grads",
    )(z, du, g, df)


def tokens(width, section=None):
    if section is None:
        return pl.BlockSpec((TB, width), lambda i, *_: (i, 0))
    if section == 0:
        return pl.BlockSpec((TB, width), lambda i, flag: (i * (1 - flag[0]), 0))
    return pl.BlockSpec((TB, width), lambda i, flag: (i * flag[0], 0))


def anywhere():
    return pl.BlockSpec(memory_space=pl.ANY)


def ff_scratch(ff_packs):
    return [
        pltpu.VMEM((len(ff_packs),) + ff_packs[0].shape, BF16),
        pltpu.SemaphoreType.DMA((len(ff_packs),)),
    ]


def fetch_packs(packs, weights_ref, sems, wanted):
    started = (pl.program_id(0) == 0) & wanted

    @pl.when(started)
    def _():
        for index, pack in enumerate(packs):
            pltpu.make_async_copy(pack, weights_ref.at[index], sems.at[index]).start()

    def wait():
        @pl.when(started)
        def _():
            for index, pack in enumerate(packs):
                pltpu.make_async_copy(pack, weights_ref.at[index], sems.at[index]).wait()

    return wait


def over_quarters(first, then):
    made = first(0)
    for index in range(4):
        ahead = first(index + 1) if index < 3 else None
        then(index, made)
        made = ahead


def quarter_lanes(index, hidden):
    return slice(index * hidden, (index + 1) * hidden)


def fixed(shape):
    return pl.BlockSpec(shape, lambda i, *_: (0,) * len(shape))


def encoder_forward_kernel(
    flag_ref, mixed_ref, x_ref, out_ref, vec_ref, ff0, ff1, ff2, ff3, bias_ref,
    *refs,
):
    sum1_ref, h_ref, g_ref, slope_ref, sum2_ref, memory_ref, part_ref, weights_ref, sems = refs[-9:]
    width = x_ref.shape[1]
    hidden = ff0.shape[1]
    is_enc = flag_ref[0] == 0
    wait = fetch_packs((ff0, ff1, ff2, ff3), weights_ref, sems, is_enc)
    stream = x_ref[...].astype(F32)
    summed = stream + (dot(mixed_ref[...], out_ref[...]) + vec_ref[0:1, :])
    sum1_ref[...] = summed
    first = normed_of(summed)[0] * vec_ref[2:3, :] + vec_ref[3:4, :]
    h_ref[...] = first.astype(BF16)
    wait()

    @pl.when(is_enc)
    def _():
        sum2_ref[...] = first + stream + vec_ref[1:2, :]

        def hidden_of(index):
            return dot(h_ref[...], weights_ref[index, :width, :]) + bias_ref[index:index + 1, :]

        def quarter(index, pre):
            value, slope = gelu_parts(pre)
            value = value.astype(BF16)
            lanes = quarter_lanes(index, hidden)
            g_ref[:, lanes] = value
            slope_ref[:, lanes] = slope.astype(BF16)
            sum2_ref[...] = sum2_ref[...] + dot(value, weights_ref[index, width:, :])

        over_quarters(hidden_of, quarter)
        last = (normed_of(sum2_ref[...])[0] * vec_ref[4:5, :] + vec_ref[5:6, :]).astype(BF16)
        memory_ref[...] = last
        part_ref[...] = last


def encoder_forward(part, flag, mixed, stream, out_weight, vectors, ff_packs, bias, earlier=()):
    rows, width = stream.shape
    hidden = 4 * ff_packs[0].shape[1]
    here = lambda v: pl.BlockSpec((TB, v), lambda i, *_: (part, 0))
    shapes = [
        jax.ShapeDtypeStruct((rows, width), F32),
        jax.ShapeDtypeStruct((rows, width), BF16),
        jax.ShapeDtypeStruct((rows, hidden), BF16),
        jax.ShapeDtypeStruct((rows, hidden), BF16),
        jax.ShapeDtypeStruct((rows, width), F32),
        jax.ShapeDtypeStruct((rows, width), BF16),
    ]
    operands = (flag, mixed, stream, out_weight, vectors, *ff_packs, bias)
    return pl.pallas_call(
        encoder_forward_kernel,
        grid_spec=pltpu.PrefetchScalarGridSpec(
            num_scalar_prefetch=1,
            grid=(1,),
            in_specs=[here(width), here(width), fixed(out_weight.shape), fixed(vectors.shape)]
            + [anywhere()] * len(ff_packs)
            + [fixed(bias.shape)]
            + [anywhere()] * len(earlier),
            out_specs=[here(shape.shape[1]) for shape in shapes] + [fixed((TB, width))],
            scratch_shapes=ff_scratch(ff_packs),
        ),
        out_shape=shapes + [jax.ShapeDtypeStruct((TB, width), BF16)],
        input_output_aliases={len(operands) + index: index for index in range(len(earlier))},
        compiler_params=params(),
        cost_estimate=cost(rows * width * (width + 2 * hidden), 10 * rows * width),
        name="encoder_forward",
    )(*operands, *earlier)


def decoder_kernel(
    flag_ref, mixed_ref, sum1_ref, x_ref, cot_ref, g_in, h_in, memory_in,
    out_ref, vec_ref, cvec_ref, ff0, ff1, ff2, ff3, bias_ref,
    result_ref, g_ref, z_ref, du_ref, df_ref, dcross_ref, dmixed_ref, dh_ref, dlast_ref, vgrad_ref, bgrad_ref,
    weights_ref, sems, slope_ref, total_ref,
):
    width = x_ref.shape[1]
    hidden = ff0.shape[1]
    wait = fetch_packs((ff0, ff1, ff2, ff3), weights_ref, sems, flag_ref[0] == 1)

    @pl.when(pl.program_id(0) == 0)
    def _():
        vgrad_ref[...] = jnp.zeros(vgrad_ref.shape, F32)
        bgrad_ref[...] = jnp.zeros(bgrad_ref.shape, F32)

    @pl.when(flag_ref[0] == 0)
    def _():
        result_ref[...] = memory_in[...]
        g_ref[...] = g_in[...]
        z_ref[...] = h_in[...]

    @pl.when(flag_ref[0] == 1)
    def _():
        stream = x_ref[...].astype(F32)
        first = normed_of(sum1_ref[...])[0] * vec_ref[2:3, :] + vec_ref[3:4, :]
        mixed = mixed_ref[...]
        crossed = dot(mixed, out_ref[...]) + cvec_ref[2:3, :]
        normed_c, inverse_c = normed_of(first + crossed)
        second = normed_c * cvec_ref[3:4, :] + cvec_ref[4:5, :]
        second_low = second.astype(BF16)
        z_ref[...] = second_low
        total_ref[...] = second + stream + vec_ref[1:2, :]
        wait()

        def hidden_of(index):
            return dot(z_ref[...], weights_ref[index, :width, :]) + bias_ref[index:index + 1, :]

        def quarter(index, pre):
            value, slope = gelu_parts(pre)
            value = value.astype(BF16)
            lanes = quarter_lanes(index, hidden)
            g_ref[:, lanes] = value
            slope_ref[:, lanes] = slope.astype(BF16)
            total_ref[...] = total_ref[...] + dot(value, weights_ref[index, width:, :])

        over_quarters(hidden_of, quarter)
        normed, inverse = normed_of(total_ref[...])
        result_ref[...] = (normed * vec_ref[4:5, :] + vec_ref[5:6, :]).astype(BF16)
        grad = cot_ref[...].astype(F32)
        grad_last = norm_back(grad, normed, inverse, vec_ref[4:5, :])
        dlast_ref[...] = grad_last
        grad_ffn = grad_last.astype(BF16)
        df_ref[...] = grad_ffn
        total_ref[...] = grad_last

        def value_grad_of(index):
            return dot_t(df_ref[...], weights_ref[index, width:, :])

        def quarter_back(index, grad_value):
            lanes = quarter_lanes(index, hidden)
            grad_pre = (grad_value * slope_ref[:, lanes].astype(F32)).astype(BF16)
            du_ref[:, lanes] = grad_pre
            bgrad_ref[index:index + 1, :] += column_sum(grad_pre)
            total_ref[...] = total_ref[...] + dot_t(grad_pre, weights_ref[index, :width, :])

        over_quarters(value_grad_of, quarter_back)
        grad_second = total_ref[...]
        grad_cross = norm_back(grad_second, normed_c, inverse_c, cvec_ref[3:4, :])
        dh_ref[...] = grad_cross
        cross_low = grad_cross.astype(BF16)
        dcross_ref[...] = cross_low
        dmixed_ref[...] = dot_t(cross_low, out_ref[...]).astype(BF16)
        vgrad_ref[1:2, :] += column_sum(grad_ffn)
        vgrad_ref[4:5, :] += column_sum(grad * normed)
        vgrad_ref[5:6, :] += column_sum(grad)
        vgrad_ref[6:7, :] += column_sum(cross_low)
        vgrad_ref[7:8, :] += column_sum(grad_second * normed_c)
        vgrad_ref[8:9, :] += column_sum(grad_second)


def decoder_step(flag, mixed, sum1, stream, cot, g_in, h_in, memory_in, out_weight, vectors, cvec, ff_packs, bias):
    rows, width = stream.shape
    hidden = g_in.shape[1]
    return pl.pallas_call(
        decoder_kernel,
        grid_spec=pltpu.PrefetchScalarGridSpec(
            num_scalar_prefetch=1,
            grid=(rows // TB,),
            in_specs=[
                tokens(width, 1), tokens(width, 1), tokens(width, 1), tokens(width, 1), tokens(hidden, 0),
                tokens(width, 0), tokens(width, 0), fixed(out_weight.shape), fixed(vectors.shape), fixed(cvec.shape),
            ]
            + [anywhere()] * len(ff_packs)
            + [fixed(bias.shape)],
            out_specs=[
                tokens(width), tokens(hidden), tokens(width), tokens(hidden, 1), tokens(width, 1), tokens(width, 1),
                tokens(width, 1), tokens(width, 1), tokens(width, 1), fixed((16, width)), fixed(bias.shape),
            ],
            scratch_shapes=ff_scratch(ff_packs) + [pltpu.VMEM((TB, hidden), BF16), pltpu.VMEM((TB, width), F32)],
        ),
        out_shape=[
            jax.ShapeDtypeStruct((rows, width), BF16),
            jax.ShapeDtypeStruct((rows, hidden), BF16),
            jax.ShapeDtypeStruct((rows, width), BF16),
            jax.ShapeDtypeStruct((rows, hidden), BF16),
            jax.ShapeDtypeStruct((rows, width), BF16),
            jax.ShapeDtypeStruct((rows, width), BF16),
            jax.ShapeDtypeStruct((rows, width), BF16),
            jax.ShapeDtypeStruct((rows, width), F32),
            jax.ShapeDtypeStruct((rows, width), F32),
            jax.ShapeDtypeStruct((16, width), F32),
            jax.ShapeDtypeStruct(bias.shape, F32),
        ],
        compiler_params=params(),
        cost_estimate=cost(2 * rows * width * (2 * width + 4 * hidden), 40 * rows * width),
        name="decoder_step",
    )(flag, mixed, sum1, stream, cot, g_in, h_in, memory_in, out_weight, vectors, cvec, *ff_packs, bias)


def backward_kernel(
    flag_ref, cot_ref, dmem_ref, sum1_ref, sum2_ref, slope_ref,
    dh_in, dq_in, dlast_in, du_in, df_in, vgrad_in, bgrad_in,
    out_ref, cross_ref, vec_ref, ff0, ff1, ff2, ff3,
    du_ref, df_ref, da_ref, dmixed_ref, dres_ref, vgrad_ref, bgrad_ref, dfirst_ref, weights_ref, sems,
):
    width = cot_ref.shape[1]
    hidden = ff0.shape[1]
    wait = fetch_packs((ff0, ff1, ff2, ff3), weights_ref, sems, flag_ref[0] == 0)
    at_start = pl.program_id(0) == 0
    is_dec = flag_ref[0] == 1

    @pl.when(at_start & is_dec)
    def _():
        vgrad_ref[...] = vgrad_in[...]
        bgrad_ref[...] = bgrad_in[...]

    @pl.when(at_start & jnp.logical_not(is_dec))
    def _():
        vgrad_ref[...] = jnp.zeros(vgrad_ref.shape, F32)
        bgrad_ref[...] = jnp.zeros(bgrad_ref.shape, F32)

    @pl.when(is_dec)
    def _():
        du_ref[...] = du_in[...]
        df_ref[...] = df_in[...]
        dres_ref[...] = dlast_in[...]
        dfirst_ref[...] = dh_in[...] + dot_t(dq_in[...], cross_ref[...])

    @pl.when(jnp.logical_not(is_dec))
    def _():
        grad = cot_ref[...].astype(F32) + dmem_ref[...].astype(F32)
        normed, inverse = normed_of(sum2_ref[...])
        grad_last = norm_back(grad, normed, inverse, vec_ref[4:5, :])
        dres_ref[...] = grad_last
        grad_ffn = grad_last.astype(BF16)
        df_ref[...] = grad_ffn
        dfirst_ref[...] = grad_last
        wait()

        def value_grad_of(index):
            return dot_t(df_ref[...], weights_ref[index, width:, :])

        def quarter_back(index, grad_value):
            lanes = quarter_lanes(index, hidden)
            grad_pre = (grad_value * slope_ref[:, lanes].astype(F32)).astype(BF16)
            du_ref[:, lanes] = grad_pre
            bgrad_ref[index:index + 1, :] += column_sum(grad_pre)
            dfirst_ref[...] = dfirst_ref[...] + dot_t(grad_pre, weights_ref[index, :width, :])

        over_quarters(value_grad_of, quarter_back)
        vgrad_ref[1:2, :] += column_sum(grad_ffn)
        vgrad_ref[4:5, :] += column_sum(grad * normed)
        vgrad_ref[5:6, :] += column_sum(grad)

    grad_first = dfirst_ref[...]
    normed, inverse = normed_of(sum1_ref[...])
    grad_in = norm_back(grad_first, normed, inverse, vec_ref[2:3, :])
    low = grad_in.astype(BF16)
    da_ref[...] = low
    dmixed_ref[...] = dot_t(low, out_ref[...]).astype(BF16)
    dres_ref[...] = dres_ref[...] + grad_in
    vgrad_ref[0:1, :] += column_sum(low)
    vgrad_ref[2:3, :] += column_sum(grad_first * normed)
    vgrad_ref[3:4, :] += column_sum(grad_first)


def backward_step(
    flag, cot, dmem, sum1, sum2, slope, dh, dq, dlast, du, df, vgrad, bgrad, out_weight, cross_query, vectors, ff_packs
):
    rows, width = cot.shape
    hidden = du.shape[1]
    return pl.pallas_call(
        backward_kernel,
        grid_spec=pltpu.PrefetchScalarGridSpec(
            num_scalar_prefetch=1,
            grid=(rows // TB,),
            in_specs=[
                tokens(width, 0), tokens(width, 0), tokens(width), tokens(width, 0), tokens(hidden, 0),
                tokens(width, 1), tokens(width, 1), tokens(width, 1), tokens(hidden, 1), tokens(width, 1),
                fixed(vgrad.shape), fixed(bgrad.shape),
                fixed(out_weight.shape), fixed(cross_query.shape), fixed(vectors.shape),
            ]
            + [anywhere()] * len(ff_packs),
            out_specs=[
                tokens(hidden), tokens(width), tokens(width), tokens(width), tokens(width),
                fixed(vgrad.shape), fixed(bgrad.shape),
            ],
            scratch_shapes=[pltpu.VMEM((TB, width), F32)] + ff_scratch(ff_packs),
        ),
        out_shape=[
            jax.ShapeDtypeStruct((rows, hidden), BF16),
            jax.ShapeDtypeStruct((rows, width), BF16),
            jax.ShapeDtypeStruct((rows, width), BF16),
            jax.ShapeDtypeStruct((rows, width), BF16),
            jax.ShapeDtypeStruct((rows, width), F32),
            jax.ShapeDtypeStruct(vgrad.shape, F32),
            jax.ShapeDtypeStruct(bgrad.shape, F32),
        ],
        compiler_params=params(),
        cost_estimate=cost(2 * rows * width * (width + 2 * hidden), 40 * rows * width),
        name="backward_step",
    )(
        flag, cot, dmem, sum1, sum2, slope, dh, dq, dlast, du, df, vgrad, bgrad,
        out_weight, cross_query, vectors, *ff_packs,
    )


def input_kernel(dres_ref, *refs):
    *parts, weight_ref, dx_ref = refs
    total = dres_ref[...]
    at = 0
    for part in parts:
        wide = part.shape[1]
        total = total + dot_t(part[...], weight_ref[:, at:at + wide])
        at += wide
    dx_ref[...] = total.astype(BF16)


def input_step(dres, parts, weight):
    rows, width = dres.shape
    block = 256
    spec = lambda v: pl.BlockSpec((block, v.shape[1]), lambda i: (i, 0))
    return pl.pallas_call(
        input_kernel,
        grid=(rows // block,),
        in_specs=[spec(v) for v in (dres, *parts)] + [fixed(weight.shape)],
        out_specs=spec(dres),
        out_shape=jax.ShapeDtypeStruct((rows, width), BF16),
        compiler_params=params(),
        cost_estimate=cost(6 * rows * width * width, 12 * rows * width),
        name="input_step",
    )(dres, *parts, weight)


def finish_kernel(ff_ref, attn_ref, ffin_ref, ffout_ref, qkv_ref, out_ref, bias_ref, hidden_ref, vectors_ref):
    width = ffin_ref.shape[0]
    lane = attn_ref.shape[1]
    ffin_ref[...] = ff_ref[:width, :].astype(F32)
    ffout_ref[...] = ff_ref[width:, :].astype(F32)
    for index in range(3):
        qkv_ref[index] = attn_ref[index * width:(index + 1) * width, :].astype(F32)
    for index in range(width // lane):
        at = 3 * width + index * lane
        out_ref[:, index * lane:(index + 1) * lane] = attn_ref[at:at + lane, :].astype(F32)
    rows = attn_ref[4 * width:, :].astype(F32)
    bias_ref[...] = rows[0:2]
    for index in range(hidden_ref.shape[1] // lane):
        hidden_ref[:, index * lane:(index + 1) * lane] = rows[2 + index:3 + index]
    count = width // lane
    for index in range(6):
        for part in range(count):
            row = 16 + index * count + part
            vectors_ref[index:index + 1, part * lane:(part + 1) * lane] = rows[row:row + 1]


def finish(ff_total, attn_total):
    width, lane = ff_total.shape[1], attn_total.shape[1]
    hidden = ff_total.shape[0] - width
    shapes = [(width, hidden), (hidden, width), (3, width, lane), (lane, width), (2, lane), (1, hidden), (6, width)]
    return pl.pallas_call(
        finish_kernel,
        grid=(1,),
        in_specs=[fixed(ff_total.shape), fixed(attn_total.shape)],
        out_specs=[fixed(shape) for shape in shapes],
        out_shape=[jax.ShapeDtypeStruct(shape, F32) for shape in shapes],
        compiler_params=params(),
        cost_estimate=cost(0, 20 * width * width),
        name="finish",
    )(ff_total, attn_total)


def flipped(value, bits, section=None):
    count = lax.axis_size("tensor")
    if section is None:
        return lax.ppermute(value, "tensor", [(t, t ^ bits) for t in range(count)])
    base = section * count
    return lax.ppermute(value, ("pipe", "tensor"), [(base + t, base + (t ^ bits)) for t in range(count)])


def across(value, source, active):
    count = lax.axis_size("tensor")
    other = 1 - source
    pairs = [(source * count + t, other * count + t) for t in range(active)]
    return lax.ppermute(value, ("pipe", "tensor"), pairs)


def plus(own, received):
    return (own.astype(F32) + received.astype(F32)).astype(BF16)


def along_dp(part, level, section=None):
    count = lax.axis_size("dp")
    if section is None:
        return lax.ppermute(part, "dp", [(i, i ^ (1 << level)) for i in range(count)])
    base = section * count
    return lax.ppermute(part, ("pipe", "dp"), [(base + i, base + (i ^ (1 << level))) for i in range(count)])


def dp_bit(level):
    return lax.shift_right_logical(lax.axis_index("dp"), level) & 1


def halved(value, level, section=None, behind=()):
    rows = value.shape[0] // 2
    mine = dp_bit(level)
    got = along_dp(lax.dynamic_slice_in_dim(value, (1 - mine) * rows, rows, 0), level, section)
    return plus(lax.dynamic_slice_in_dim(after(value, *behind), mine * rows, rows, 0), got)


def doubled(value, level, section=None, behind=()):
    other = along_dp(value, level, section)
    upper = dp_bit(level) == 1
    value = after(value, *behind)
    return jnp.concatenate([jnp.where(upper, other, value), jnp.where(upper, value, other)], 0)


def after(value, *others):
    return lax.optimization_barrier((value,) + others)[0]


def to_rows(shard):
    count = lax.axis_size("tensor")
    shard = jnp.pad(shard, ((0, count - shard.shape[0]), (0, 0), (0, 0)))
    out = lax.all_to_all(shard, "tensor", 0, 0, tiled=True)
    return out.reshape(count * shard.shape[1], shard.shape[2])


def from_rows(row, row_count):
    count = lax.axis_size("tensor")
    parts = row.reshape(count, row.shape[0] // count, row.shape[1])
    return lax.all_to_all(parts, "tensor", 0, 0, tiled=True)[:row_count]


def shards(
    inputs, cotangent, segments, pads, self_qkv, self_bias, self_out, ff_in, ff_bias, ff_out, vectors,
    cross_q, cross_kv, cross_out, cross_small, cross_gain,
):
    section = lax.axis_index("pipe").astype(jnp.int32)
    place = lax.axis_index("tensor").astype(jnp.int32)
    count = lax.axis_size("tensor")
    row_count = inputs.shape[1]
    decoder = section == 1
    flag, place_flag = section[None], place[None]
    width = inputs.shape[3]
    lane = self_qkv.shape[3]
    hidden = ff_in.shape[2]
    half = width // 2
    row = jnp.minimum(place, row_count - 1)

    attn_own = attention_pack(jnp.transpose(self_qkv[0], (1, 0, 2)), self_out[0], self_bias[0], ff_bias)
    attn_far, attn_near = flipped(attn_own, 2), flipped(attn_own, 1)
    stream = to_rows(after(inputs[0], attn_own))
    slots = jnp.concatenate(
        [
            lax.dynamic_index_in_dim(segments, row, 1, False),
            lax.dynamic_slice_in_dim(pads[0], row, 1, 0),
        ],
        0,
    )
    cross_half = cross_pack(
        after(cross_q, attn_own), jnp.transpose(cross_kv, (1, 0, 2)), cross_out, cross_small.reshape(-1, lane),
        cross_gain.reshape(-1, lane),
    )
    other_half = across(cross_half, 0, count)
    attn_packs = [attn_own, attn_near, attn_far, flipped(after(attn_far, cross_half), 1)]
    ff_own = after(jnp.concatenate([ff_in[0], ff_out[0]], 0), stream, attn_far)
    ff_far, ff_near = flipped(ff_own, 2), flipped(ff_own, 1)
    vector_rows = vectors[0]

    qkv, qkv_weight, out_weight, hidden_bias, own_code, key_code, target_code, source_code, self_bounds, cross_bounds = (
        query_key_value(flag, stream, slots, attn_packs)
    )
    parts = ((qkv, 0), (qkv, 1), (qkv, 2))
    self_codes, cross_codes = (own_code, key_code), (target_code, source_code)
    mixed, totals = attend_forward(self_bounds, self_codes, width, *parts)
    cross_own = jnp.concatenate([after(other_half, mixed), cross_half], 0)
    ff_packs = [ff_own, ff_near, ff_far, flipped(after(ff_far, cross_own), 1)]
    cross_far, cross_near = flipped(cross_own, 2, 1), flipped(cross_own, 1, 1)
    blocks, memory_parts = (), []
    for part in range(stream.shape[0] // TB):
        *blocks, memory_part = encoder_forward(
            part, flag, mixed, stream, out_weight, vector_rows, ff_packs, hidden_bias, blocks
        )
        memory_parts.append(across(memory_part, 0, row_count))
    sum1, first_low, g_enc, slope, sum2, memory = blocks
    memory_in = jnp.concatenate(memory_parts, 0)

    cross_packs = [cross_own, cross_near, cross_far, flipped(after(cross_far, memory_parts[0]), 1, 1)]
    cot_row = to_rows(after(cotangent[0], memory_parts[0]))

    cross_query, cross_pair, cross_out_weight, cvec = cross_unpack(place_flag, cross_packs)
    scale = HEAD_DIM ** (-0.5)
    cross_queries = ((dot(first_low, cross_query) + cvec[0]).astype(BF16).astype(F32) * scale).astype(BF16)
    pair_bias = jnp.concatenate([jnp.zeros_like(cvec[1]), cvec[1]])
    cross_rows = jnp.concatenate([(dot(part, cross_pair) + pair_bias).astype(BF16) for part in memory_parts], 0)
    cross_parts = ((cross_queries, 0), (cross_rows, 0), (cross_rows, 1))
    cross_mixed, cross_totals = attend_forward(cross_bounds, cross_codes, width, *cross_parts)
    result, g_all, z_all, du_dec, df_dec, dcross, dcross_mixed, dh_dec, dlast_dec, vgrad_dec, bgrad_dec = decoder_step(
        flag, cross_mixed, sum1, stream, cot_row, g_enc, first_low, memory,
        cross_out_weight, vector_rows, cvec, ff_packs, hidden_bias,
    )
    dq_cross, dk_cross, dv_cross, dmemory = attend_backward(
        cross_bounds, cross_codes, *cross_parts, dcross_mixed, cross_totals, cross_pair
    )
    dmemory_in = across(dmemory, 1, row_count)
    cross_grads = attention_grads(
        True, place_flag, first_low, memory_in, (after(dq_cross, dmemory), dk_cross, dv_cross), cross_mixed, dcross,
        vgrad_dec, bgrad_dec, lane,
    )
    cross_far = plus(after(cross_grads[2], dmemory_in), flipped(cross_grads[3], 1, 1))
    cross_got = flipped(cross_grads[1], 1, 1)

    du_all, df_all, da, dmixed, dres, vgrad, bgrad = backward_step(
        flag, cot_row, dmemory_in, sum1, sum2, slope, dh_dec, after(dq_cross, cross_far, cross_grads[1]), dlast_dec,
        du_dec, df_dec, vgrad_dec, bgrad_dec, out_weight, cross_query, vector_rows, ff_packs,
    )
    cross_near = plus(after(cross_grads[0], da), cross_got)
    cross_part = plus(cross_near, flipped(cross_far, 2, 1))
    levels = range(lax.axis_size("dp").bit_length() - 1)
    ff_third, ff_second = feed_forward_grads(after(z_all, cross_part), du_all, g_all, df_all, 3, hidden)
    ff_first, ff_zeroth = feed_forward_grads(after(z_all, ff_second), du_all, g_all, df_all, 1, hidden)
    cross_total = halved(cross_part, 0, 1, (ff_zeroth,))
    ff_far = plus(after(ff_second, ff_zeroth), flipped(ff_third, 1))
    ff_near = plus(after(ff_zeroth, ff_far, cross_total), flipped(ff_first, 1))
    dqkv = attend_backward(self_bounds, self_codes, *parts, after(dmixed, ff_near), totals)
    for level in levels[1:]:
        cross_total = halved(cross_total, level, 1, (dqkv[0],))
    ff_part = plus(after(ff_near, dqkv[0], cross_total), flipped(ff_far, 2))
    attn_grads = attention_grads(
        False, place_flag, stream, stream, (after(dqkv[0], ff_part), *dqkv[1:]), mixed, da, vgrad, bgrad, lane
    )
    last = reversed(levels)
    cross_total = doubled(cross_total, next(last), 1, (attn_grads[3],))
    ff_total = halved(ff_part, 0, behind=(attn_grads[3],))
    attn_far = plus(after(attn_grads[2], ff_total), flipped(attn_grads[3], 1))
    attn_near = plus(after(attn_grads[0], attn_far), flipped(attn_grads[1], 1))
    dx = input_step(after(dres, attn_near), dqkv, qkv_weight)
    for level in last:
        cross_total = doubled(cross_total, level, 1, (dx,))
    for level in levels[1:]:
        ff_total = halved(ff_total, level, behind=(dx,))
    cross_other = across(cross_total, 1, count)
    attn_part = plus(after(attn_near, ff_total, cross_total), flipped(attn_far, 2))
    attn_total = attn_part
    for level in levels:
        attn_total = halved(attn_total, level)
    for level in reversed(levels):
        ff_total = doubled(ff_total, level, behind=(attn_part,))
    for level in reversed(levels):
        attn_total = doubled(attn_total, level)
    input_grad = from_rows(after(dx, attn_part), row_count).astype(F32)[None]
    section_out = from_rows(after(result, attn_part), row_count)[None]

    own, other = cross_total.astype(F32), cross_other.astype(F32)

    def halves(at):
        return jnp.where(decoder, own[at + half:at + 2 * half], other[at:at + half])

    cross_pair_grad = jnp.stack([halves(width), halves(2 * width)], 1)
    cross_out_grad = jnp.transpose(halves(3 * width).reshape(half // lane, lane, lane), (1, 0, 2)).reshape(lane, half)
    own_rows, other_rows = (v[4 * width:4 * width + 5 * count].reshape(5, width) for v in (own, other))
    small_grad = jnp.where(decoder, jnp.stack([own_rows[2], own_rows[4]]), other_rows[:2])
    gain_grad = jnp.where(decoder, own_rows[3, half:], other_rows[3, :half])
    cross_first, cross_last = halves(0), (cross_pair_grad, cross_out_grad, small_grad, gain_grad)
    ffin_grad, ffout_grad, qkv_grad, out_grad, bias_grad, hidden_grad, vectors_grad = finish(
        ff_total, after(attn_total, cross_first, *cross_last, input_grad, section_out)
    )
    return (
        section_out,
        input_grad,
        jnp.transpose(qkv_grad, (1, 0, 2))[None],
        bias_grad[None],
        out_grad[None],
        ffin_grad[None],
        hidden_grad,
        ffout_grad[None],
        vectors_grad[None],
        cross_first,
        *cross_last,
    )


def solution(mesh):
    token_spec = P("pipe", "dp", "tensor", None)
    weights = (
        P("pipe", None, None, "tensor"),
        P("pipe", None, "tensor"),
        P("pipe", "tensor", None),
        P("pipe", None, "tensor"),
        P("pipe", "tensor"),
        P("pipe", "tensor", None),
        P("pipe", None, None),
        P("pipe", "tensor"),
        P("pipe", None, "tensor"),
        P("tensor", "pipe"),
        P("pipe", None),
        P("pipe"),
    )
    return jax.shard_map(
        shards,
        mesh=mesh,
        in_specs=(token_spec, token_spec, P(None, "dp", None), P("pipe", "dp", None)) + weights,
        out_specs=(token_spec, token_spec) + weights,
        check_vma=False,
    )
```

```python
import functools

import jax
import jax.numpy as jnp
from jax import lax
from jax.experimental import pallas as pl
from jax.experimental.pallas import tpu as pltpu
from jax.sharding import PartitionSpec as P

HEAD_DIM = 64
EPSILON = 1e-05
MASKED = -1e30
SEGS = 8
QF = 256
QB = 256
TB = 512
PIECES = 1
PAIR = 2 * HEAD_DIM
GELU_C = 0.7978845608028654
GELU_A = 0.044715
VMEM_LIMIT = 56 * 1024 * 1024
F32 = jnp.float32
BF16 = jnp.bfloat16


def dot(left, right):
    return jnp.dot(left, right, preferred_element_type=F32)


def dot_t(left, right):
    return lax.dot_general(left, right, (((1,), (1,)), ((), ())), preferred_element_type=F32)


def dot_tl(left, right):
    return lax.dot_general(left, right, (((0,), (0,)), ((), ())), preferred_element_type=F32)


def normed_of(values):
    center = values - jnp.mean(values, -1, keepdims=True)
    inverse = lax.rsqrt(jnp.mean(center * center, -1, keepdims=True) + EPSILON)
    return center * inverse, inverse


def norm_back(grad, normed, inverse, gain):
    scaled = grad * gain
    mean_scaled = jnp.mean(scaled, -1, keepdims=True)
    mean_both = jnp.mean(scaled * normed, -1, keepdims=True)
    return (scaled - mean_scaled - normed * mean_both) * inverse


def column_sum(values):
    return jnp.sum(values.astype(F32), 0, keepdims=True)


def gelu_parts(pre):
    squared = pre * pre
    half = 0.5 * jnp.tanh(pre * (GELU_C + (GELU_C * GELU_A) * squared)) + 0.5
    slope = half + (pre * (half - half * half)) * (2.0 * GELU_C + (6.0 * GELU_C * GELU_A) * squared)
    return pre * half, slope


def cost(flops, moved):
    return pl.CostEstimate(flops=int(flops) // 64, bytes_accessed=int(moved) // 64, transcendentals=0)


def params(axes=1):
    return pltpu.CompilerParams(
        dimension_semantics=("arbitrary",) * axes, vmem_limit_bytes=VMEM_LIMIT
    )


def find_segments(section, slots_ref, own_ref, key_ref, target_ref, source_ref, self_ref, cross_ref):
    length = slots_ref.shape[1]
    source = slots_ref[0:1, :].astype(F32)
    target = slots_ref[1:2, :].astype(F32)
    own = jnp.where(section == 1, target, source)
    own_ref[...] = own
    key_ref[...] = jnp.where(slots_ref[2:3, :] == 0, own, -1.0)
    target_ref[...] = target
    source_ref[...] = source

    def starts(segments):
        found = [jnp.int32(0)]
        for index in range(1, SEGS):
            found.append(jnp.sum(jnp.where(segments < float(index), 1.0, 0.0)).astype(jnp.int32))
        return found + [jnp.int32(length)]

    source_starts, target_starts = starts(source), starts(target)
    for index in range(SEGS):
        own_start = jnp.where(section == 1, target_starts[index], source_starts[index])
        own_end = jnp.where(section == 1, target_starts[index + 1], source_starts[index + 1])
        self_ref[index] = own_start
        self_ref[16 + index] = own_start
        self_ref[32 + index] = own_end
        cross_ref[index] = target_starts[index]
        cross_ref[16 + index] = source_starts[index]
        cross_ref[32 + index] = source_starts[index + 1]
    self_ref[48] = jnp.int32(1)
    self_ref[49] = section
    self_ref[50] = jnp.int32(1)
    cross_ref[48] = jnp.int32(0)
    cross_ref[49] = jnp.int32(0)
    cross_ref[50] = section


def half_masked(values, side):
    lane = lax.broadcasted_iota(jnp.int32, values.shape, 1)
    return jnp.where((lane >= HEAD_DIM) == bool(side), values, jnp.zeros_like(values))


def key_window(bounds, block, block_rows):
    first = block * block_rows
    last = first + (block_rows - 1)
    low, high = jnp.int32(0), jnp.int32(0)
    for index in range(SEGS):
        low = jnp.where(bounds[index] <= first, bounds[16 + index], low)
        high = jnp.where(bounds[index] <= last, bounds[32 + index], high)
    high = jnp.where(bounds[49] == 1, jnp.minimum(high, last + 1), high)
    low_block = lax.shift_right_logical(low, 7)
    high_block = lax.shift_right_logical(high + 127, 7)
    return low_block, jnp.where(bounds[50] == 1, high_block - low_block, 0)


def by_size(bounds, block, block_rows, key_blocks, sizes, body):
    low_block, needed = key_window(bounds, block, block_rows)
    below = 0
    for size in sizes:
        size = min(size, key_blocks)
        if size == below:
            continue

        @pl.when((needed > below) & (needed <= size))
        def _(size=size):
            start = jnp.minimum(low_block, key_blocks - size) * 128
            body(size, pl.multiple_of(start, 128))

        below = size


def as_columns(row):
    parts = []
    for at in range(0, row.shape[1], 128):
        parts.append(jnp.broadcast_to(row[:, at:at + 128], (128, 128)).T)
    return jnp.concatenate(parts, 0)


def window_bias(bounds, block, block_rows, start, key_code, qcode_ref):
    key_at = start + lax.broadcasted_iota(jnp.int32, key_code.shape, 0)
    tiles = []
    for at in range(0, block_rows, 128):
        query_at = block * block_rows + at + lax.broadcasted_iota(jnp.int32, (1, 128), 1)
        limit = jnp.where(bounds[49] == 1, query_at, jnp.int32(1 << 30))
        same_at = jnp.where(bounds[48] == 1, query_at, -1)
        opened = (key_code == qcode_ref[:, at:at + 128]) & (key_at <= limit)
        tiles.append(jnp.where(opened | (key_at == same_at), 0.0, MASKED))
    return jnp.concatenate(tiles, 1)


def attend_forward_kernel(bounds, q_ref, k_ref, v_ref, qcode_ref, kcode_ref, mixed_ref, total_ref):
    block = pl.program_id(0)
    heads = q_ref.shape[1] // HEAD_DIM
    key_blocks = k_ref.shape[0] // 128
    own_code = as_columns(qcode_ref[...])
    query_at = block * QF + lax.broadcasted_iota(jnp.int32, (QF, 128), 0)
    limit = jnp.where(bounds[49] == 1, query_at, jnp.int32(1 << 30))
    same_at = jnp.where(bounds[48] == 1, query_at, -1)
    lane = lax.broadcasted_iota(jnp.int32, (QF, 128), 1)

    def body(size, start):
        window = pl.ds(start, size * 128)
        tiles = []
        for tile in range(size):
            at = start + tile * 128
            key_at = at + lane
            opened = (own_code == kcode_ref[:, pl.ds(pl.multiple_of(at, 128), 128)]) & (key_at <= limit)
            tiles.append(jnp.where(opened | (key_at == same_at), 0.0, MASKED))
        bias = jnp.concatenate(tiles, 1)

        def two_pairs(index, columns):
            lanes = [pl.ds(pl.multiple_of((2 * index + at) * PAIR, PAIR), PAIR) for at in range(2)]
            scores = []
            for at in range(2):
                queries, keys = q_ref[:, lanes[at]], k_ref[window, lanes[at]]
                scores.append([dot_t(half_masked(queries, side), keys) + bias for side in range(2)])
            for at in range(2):
                values = v_ref[window, lanes[at]]
                out = None
                for side in range(2):
                    top = jnp.max(scores[at][side], -1, keepdims=True)
                    weights = jnp.exp(scores[at][side] - top)
                    total = jnp.sum(weights, -1, keepdims=True)
                    part = dot(weights.astype(BF16), half_masked(values, side)) * (1.0 / total)
                    out = part if out is None else out + part
                    columns = jnp.where(lane == (2 * index + at) * 2 + side, top + jnp.log(total), columns)
                mixed_ref[:, lanes[at]] = out.astype(BF16)
            return columns

        columns = lax.fori_loop(0, heads // 4, two_pairs, jnp.zeros((QF, 128), F32))
        total_ref[...] = columns.T[:heads]

    by_size(bounds, block, QF, key_blocks, (2, 3, 4, 5, 6, 8), body)


def attend_forward(bounds, codes, width, queries, keys, values):
    (q_array, q_at), (k_array, k_at), (v_array, v_at) = queries, keys, values
    rows = q_array.shape[0]
    heads = width // HEAD_DIM
    whole = lambda at: (lambda i, *_: (0, at))
    return pl.pallas_call(
        attend_forward_kernel,
        grid_spec=pltpu.PrefetchScalarGridSpec(
            num_scalar_prefetch=1,
            grid=(rows // QF,),
            in_specs=[
                pl.BlockSpec((QF, width), lambda i, *_: (i, q_at)),
                pl.BlockSpec((rows, width), whole(k_at)),
                pl.BlockSpec((rows, width), whole(v_at)),
                pl.BlockSpec((1, QF), lambda i, *_: (0, i)),
                pl.BlockSpec((1, rows), whole(0)),
            ],
            out_specs=[
                pl.BlockSpec((QF, width), lambda i, *_: (i, 0)),
                pl.BlockSpec((heads, QF), lambda i, *_: (0, i)),
            ],
        ),
        out_shape=[
            jax.ShapeDtypeStruct((rows, width), BF16),
            jax.ShapeDtypeStruct((heads, rows), F32),
        ],
        compiler_params=params(),
        cost_estimate=cost(4 * rows * 512 * width * 2, 8 * rows * width),
        name="attend_forward",
    )(bounds, q_array, k_array, v_array, *codes)


def attend_backward_kernel(has_weight, first_head, bounds, q_ref, k_ref, v_ref, grad_ref, total_ref, qcode_ref, kcode_ref, *refs):
    if has_weight:
        weight_ref, dq_ref, dk_ref, dv_ref, dmem_ref, kcol_ref, dkacc_ref, dvacc_ref = refs
    else:
        dq_ref, dk_ref, dv_ref, kcol_ref, dkacc_ref, dvacc_ref = refs
    block = pl.program_id(0)
    width = q_ref.shape[1]
    heads = width // HEAD_DIM
    key_blocks = k_ref.shape[0] // 128

    @pl.when(block == 0)
    def _():
        dkacc_ref[...] = jnp.zeros(dkacc_ref.shape, F32)
        dvacc_ref[...] = jnp.zeros(dvacc_ref.shape, F32)
        kcol_ref[...] = as_columns(kcode_ref[...])

    def body(size, start):
        window = pl.ds(start, size * 128)
        bias = window_bias(bounds, block, QB, start, kcol_ref[window, :], qcode_ref)

        def two_pairs(index, carry):
            prepared = []
            for at in range(2):
                pair = 2 * index + at
                lanes = pl.ds(pl.multiple_of(pair * PAIR, PAIR), PAIR)
                queries, grads = q_ref[:, lanes], grad_ref[:, lanes]
                keys, values = k_ref[window, lanes], v_ref[window, lanes]
                query_halves = [half_masked(queries, side) for side in range(2)]
                grad_halves = [half_masked(grads, side) for side in range(2)]
                products = [
                    (dot_t(keys, query_halves[side]) + bias, dot_t(values, grad_halves[side])) for side in range(2)
                ]
                prepared.append((pair, lanes, keys, query_halves, grad_halves, products))
            for pair, lanes, keys, query_halves, grad_halves, products in prepared:
                dq = dk = dv = None
                for side in range(2):
                    scores, grad_weights = products[side]
                    weights = jnp.exp(scores - total_ref[pl.ds(first_head + pair * 2 + side, 1), :])
                    delta = jnp.sum(weights * grad_weights, 0, keepdims=True)
                    grad_scores = (weights * (grad_weights - delta)).astype(BF16)
                    made = (
                        dot_tl(grad_scores, half_masked(keys, side)),
                        dot(grad_scores, query_halves[side]),
                        dot(weights.astype(BF16), grad_halves[side]),
                    )
                    dq, dk, dv = made if dq is None else (dq + made[0], dk + made[1], dv + made[2])
                dkacc_ref[window, lanes] = dkacc_ref[window, lanes] + dk
                dvacc_ref[window, lanes] = dvacc_ref[window, lanes] + dv
                dq_ref[:, lanes] = (dq * HEAD_DIM ** (-0.5)).astype(BF16)
            return carry

        lax.fori_loop(0, heads // 4, two_pairs, 0)

    by_size(bounds, block, QB, key_blocks, (2, 3, 4, 5, 6, 8), body)

    @pl.when(block == pl.num_programs(0) - 1)
    def _():
        dk_ref[...] = dkacc_ref[...].astype(BF16)
        dv_ref[...] = dvacc_ref[...].astype(BF16)
        if has_weight:
            summed = dot_t(dk_ref[...], weight_ref[:, :width]) + dot_t(dv_ref[...], weight_ref[:, width:])
            dmem_ref[...] = summed.astype(BF16)


def attend_backward(bounds, codes, queries, keys, values, grad, totals, weight=None, part=(0, 1)):
    (q_array, q_at), (k_array, k_at), (v_array, v_at) = queries, keys, values
    index, count = part
    rows = grad.shape[0]
    heads = totals.shape[0]
    width = grad.shape[1] // count
    whole = lambda at: pl.BlockSpec((rows, width), lambda i, *_: (0, at * count + index))
    block = lambda at: pl.BlockSpec((QB, width), lambda i, *_: (i, at * count + index))
    extra = [] if weight is None else [weight]
    first = pl.BlockSpec((rows, width), lambda i, *_: (0, 0))
    return pl.pallas_call(
        functools.partial(attend_backward_kernel, weight is not None, index * heads // count),
        grid_spec=pltpu.PrefetchScalarGridSpec(
            num_scalar_prefetch=1,
            grid=(rows // QB,),
            in_specs=[
                block(q_at),
                whole(k_at),
                whole(v_at),
                block(0),
                pl.BlockSpec((heads, QB), lambda i, *_: (0, i)),
                pl.BlockSpec((1, QB), lambda i, *_: (0, i)),
                pl.BlockSpec((1, rows), lambda i, *_: (0, 0)),
            ]
            + [fixed(v.shape) for v in extra],
            out_specs=[pl.BlockSpec((QB, width), lambda i, *_: (i, 0))] + [first] * (2 + len(extra)),
            scratch_shapes=[
                pltpu.VMEM((rows, 128), F32),
                pltpu.VMEM((rows, width), F32),
                pltpu.VMEM((rows, width), F32),
            ],
        ),
        out_shape=[jax.ShapeDtypeStruct((rows, width), BF16)] * (3 + len(extra)),
        compiler_params=params(),
        cost_estimate=cost(10 * rows * 512 * width * 2, 16 * rows * width),
        name="attend_backward",
    )(bounds, q_array, k_array, v_array, grad, totals, *codes, *extra)


def first_packs_kernel(
    qkv_ref, out_ref, bias_ref, ffb_ref, query_ref, pair_ref, cout_ref, small_ref, gain_ref, pack_ref, half_ref
):
    width = qkv_ref.shape[1]
    lane = qkv_ref.shape[2]
    half = query_ref.shape[0]

    def columns(values):
        return [values[:, at:at + lane] for at in range(0, values.shape[1], lane)]

    def filled(rows):
        rest = jnp.zeros((16 - sum(part.shape[0] for part in rows), lane), F32)
        return jnp.concatenate([*rows, rest], 0).astype(BF16)

    for index in range(3):
        pack_ref[index * width:(index + 1) * width, :] = qkv_ref[index]
    for index, part in enumerate(columns(out_ref[...])):
        at = 3 * width + index * lane
        pack_ref[at:at + lane, :] = part
    bias = bias_ref[...]
    high = bias.astype(BF16).astype(F32)
    middle = (bias - high).astype(BF16).astype(F32)
    least = bias - high - middle
    pack_ref[4 * width:4 * width + 16, :] = filled([high, middle, least, *columns(ffb_ref[...].astype(F32))])
    half_ref[0:half, :] = query_ref[...]
    half_ref[half:2 * half, :] = pair_ref[0]
    half_ref[2 * half:3 * half, :] = pair_ref[1]
    for index, part in enumerate(columns(cout_ref[...])):
        at = 3 * half + index * lane
        half_ref[at:at + lane, :] = part
    small = small_ref[...].astype(F32)
    half_ref[4 * half:4 * half + 16, :] = filled(
        [*columns(small[0:1]), *columns(small[1:2]), *columns(gain_ref[...].astype(F32))]
    )


def first_packs(qkv, out_weight, bias, ff_bias, query, pair, cross_out, small, gain):
    width, lane = qkv.shape[1:]
    half = query.shape[0]
    operands = (qkv, out_weight, bias, ff_bias, query, pair, cross_out, small, gain)
    shapes = [(4 * width + 16, lane), (4 * half + 16, lane)]
    return pl.pallas_call(
        first_packs_kernel,
        grid=(1,),
        in_specs=[fixed(v.shape) for v in operands],
        out_specs=[fixed(shape) for shape in shapes],
        out_shape=[jax.ShapeDtypeStruct(shape, BF16) for shape in shapes],
        compiler_params=params(),
        cost_estimate=cost(0, 24 * width * lane),
        name="first_packs",
    )(*operands)


def query_key_value_kernel(
    flag_ref, x_ref, slots_ref, p0, p1, p2, p3, qkv_ref, weight_ref, out_ref, hidden_ref, *refs
):
    *found_refs, bias_ref = refs
    width = x_ref.shape[1]
    lane = p0.shape[1]

    @pl.when(pl.program_id(0) == 0)
    def _():
        find_segments(flag_ref[0], slots_ref, *found_refs)
        for index, pack in enumerate((p0, p1, p2, p3)):
            columns = slice(index * lane, (index + 1) * lane)
            for part in range(3):
                at = slice(part * width + index * lane, part * width + (index + 1) * lane)
                weight_ref[:, at] = pack[part * width:(part + 1) * width, :]
            for part in range(width // lane):
                at = 3 * width + part * lane
                out_ref[columns, part * lane:(part + 1) * lane] = pack[at:at + lane, :]
            rows = pack[4 * width:4 * width + 16, :].astype(F32)
            bias_ref[0:1, columns] = rows[0:1] + rows[2:3] + rows[4:5]
            bias_ref[1:2, columns] = rows[1:2] + rows[3:4] + rows[5:6]
            for part in range(width // lane):
                hidden_ref[index:index + 1, part * lane:(part + 1) * lane] = rows[6 + part:7 + part]

    made = dot(x_ref[...], weight_ref[...])
    scale = HEAD_DIM ** (-0.5)
    queries = (made[:, :width] + bias_ref[0:1, :]).astype(BF16).astype(F32) * scale
    qkv_ref[:, :width] = queries.astype(BF16)
    qkv_ref[:, width:2 * width] = made[:, width:2 * width].astype(BF16)
    qkv_ref[:, 2 * width:] = (made[:, 2 * width:] + bias_ref[1:2, :]).astype(BF16)


def query_key_value(flag, stream, slots, packs):
    rows, width = stream.shape
    line = jax.ShapeDtypeStruct((1, rows), F32)
    bounds = jax.ShapeDtypeStruct((64,), jnp.int32)
    return pl.pallas_call(
        query_key_value_kernel,
        grid_spec=pltpu.PrefetchScalarGridSpec(
            num_scalar_prefetch=1,
            grid=(rows // TB,),
            in_specs=[tokens(width), fixed(slots.shape)] + [fixed(pack.shape) for pack in packs],
            out_specs=[tokens(3 * width), fixed((width, 3 * width)), fixed((width, width)), fixed((len(packs), width))]
            + [fixed(line.shape)] * 4
            + [pl.BlockSpec(memory_space=pltpu.SMEM)] * 2,
            scratch_shapes=[pltpu.VMEM((8, width), F32)],
        ),
        out_shape=[
            jax.ShapeDtypeStruct((rows, 3 * width), BF16),
            jax.ShapeDtypeStruct((width, 3 * width), BF16),
            jax.ShapeDtypeStruct((width, width), BF16),
            jax.ShapeDtypeStruct((len(packs), width), F32),
        ]
        + [line] * 4
        + [bounds] * 2,
        compiler_params=params(),
        cost_estimate=cost(6 * rows * width * width, 10 * rows * width),
        name="query_key_value",
    )(flag, stream, slots, *packs)


def cross_project_kernel(h_ref, memory_ref, query_ref, pair_ref, cvec_ref, made_ref):
    width = h_ref.shape[1]
    queries = (dot(h_ref[...], query_ref[...]) + cvec_ref[0:1, :]).astype(BF16).astype(F32)
    made_ref[:, :width] = (queries * HEAD_DIM ** (-0.5)).astype(BF16)
    made = dot(memory_ref[...], pair_ref[...])
    made_ref[:, width:2 * width] = made[:, :width].astype(BF16)
    made_ref[:, 2 * width:] = (made[:, width:] + cvec_ref[1:2, :]).astype(BF16)


def cross_project(h, memory, query, pair, cvec):
    rows, width = h.shape
    operands = (h, memory, query, pair, cvec)
    return pl.pallas_call(
        cross_project_kernel,
        grid=(rows // TB,),
        in_specs=[tokens(width)] * 2 + [fixed(v.shape) for v in operands[2:]],
        out_specs=tokens(3 * width),
        out_shape=jax.ShapeDtypeStruct((rows, 3 * width), BF16),
        compiler_params=params(),
        cost_estimate=cost(6 * rows * width * width, 12 * rows * width),
        name="cross_project",
    )(*operands)


def cross_unpack_kernel(place_ref, p0, p1, p2, p3, query_ref, pair_ref, out_ref, cvec_ref):
    lane = p0.shape[1]
    length = p0.shape[0] // 2
    half = (length - 16) // 4
    width = 2 * half
    count = width // lane
    for index, pack in enumerate((p0, p1, p2, p3)):
        columns = slice(index * lane, (index + 1) * lane)
        for side in range(2):
            rows = slice(side * half, (side + 1) * half)
            base = side * length
            query_ref[rows, columns] = pack[base:base + half, :]
            pair_ref[rows, columns] = pack[base + half:base + 2 * half, :]
            pair_ref[rows, width + index * lane:width + (index + 1) * lane] = pack[base + 2 * half:base + 3 * half, :]
            for part in range(half // lane):
                at = base + 3 * half + part * lane
                to = side * half + part * lane
                out_ref[columns, to:to + lane] = pack[at:at + lane, :]
    first = p0[4 * half:4 * half + 16, :].astype(F32)
    second = p0[length + 4 * half:length + 4 * half + 16, :].astype(F32)
    at_row = lax.broadcasted_iota(jnp.int32, (16, lane), 0)
    for index in range(count):
        columns = slice(index * lane, (index + 1) * lane)
        for which in range(2):
            wanted = which * count + (place_ref[0] ^ index)
            cvec_ref[which:which + 1, columns] = jnp.sum(jnp.where(at_row == wanted, first, 0.0), 0, keepdims=True)
        cvec_ref[2:3, columns] = second[index:index + 1]
        cvec_ref[4:5, columns] = second[count + index:count + index + 1]
        side, part = (first, index) if index < count // 2 else (second, index - count // 2)
        cvec_ref[3:4, columns] = side[2 * count + part:2 * count + part + 1]
    cvec_ref[5:8, :] = jnp.zeros((3, width), F32)


def cross_unpack(place, packs):
    length, lane = packs[0].shape
    width = (length // 2 - 16) // 2
    return pl.pallas_call(
        cross_unpack_kernel,
        grid_spec=pltpu.PrefetchScalarGridSpec(
            num_scalar_prefetch=1,
            grid=(1,),
            in_specs=[fixed(pack.shape) for pack in packs],
            out_specs=[fixed((width, width)), fixed((width, 2 * width)), fixed((width, width)), fixed((8, width))],
        ),
        out_shape=[
            jax.ShapeDtypeStruct((width, width), BF16),
            jax.ShapeDtypeStruct((width, 2 * width), BF16),
            jax.ShapeDtypeStruct((width, width), BF16),
            jax.ShapeDtypeStruct((8, width), F32),
        ],
        compiler_params=params(),
        cost_estimate=cost(0, 16 * width * width),
        name="cross_unpack",
    )(place, *packs)


def rows_of(vector, rows, at_row, base, order=None):
    lane = rows.shape[1]
    for index in range(vector.shape[1] // lane):
        to = base + (index if order is None else (order ^ index))
        rows = rows + jnp.where(at_row == to, vector[:, index * lane:(index + 1) * lane], 0.0)
    return rows


def attention_grads_kernel(
    is_cross, parts, place_ref, aq_ref, akv_ref, *refs
):
    width = aq_ref.shape[1]
    dq_refs, dk_refs, dv_refs = (refs[part * parts:(part + 1) * parts] for part in range(3))
    mixed_ref, da_ref, vgrad_ref, bgrad_ref, *packs, made_ref = refs[3 * parts:]
    lane = packs[0].shape[1]
    count = width // lane
    tail = packs[0].shape[0] - 4 * width
    akv = akv_ref if is_cross else aq_ref
    for part, (left, rights) in enumerate(((aq_ref, dq_refs), (akv, dk_refs), (akv, dv_refs))):
        for index, right in enumerate(rights):
            wide = width // parts
            made_ref[:, index * wide:(index + 1) * wide] = dot_tl(left[...], right[...]).astype(BF16)
        for index, pack in enumerate(packs):
            pack[part * width:(part + 1) * width, :] = made_ref[:, index * lane:(index + 1) * lane]
    made_ref[...] = dot_tl(mixed_ref[...], da_ref[...]).astype(BF16)
    for index, pack in enumerate(packs):
        for part in range(count):
            at = 3 * width + part * lane
            pack[at:at + lane, :] = made_ref[index * lane:(index + 1) * lane, part * lane:(part + 1) * lane]
    query_bias, value_bias = (
        jnp.concatenate([column_sum(ref[...]) for ref in some], 1) for some in (dq_refs, dv_refs)
    )
    at_row = lax.broadcasted_iota(jnp.int32, (tail, lane), 0)
    rows = jnp.zeros((tail, lane), F32)
    if is_cross:
        rows = rows_of(query_bias, rows, at_row, 0, place_ref[0])
        rows = rows_of(value_bias, rows, at_row, count, place_ref[0])
        for index in range(3):
            rows = rows_of(vgrad_ref[6 + index:7 + index, :], rows, at_row, (2 + index) * count)
    else:
        for index in range(6):
            rows = rows_of(vgrad_ref[index:index + 1, :], rows, at_row, 16 + index * count)
    for index, pack in enumerate(packs):
        own = rows
        if not is_cross:
            columns = slice(index * lane, (index + 1) * lane)
            own = own + jnp.where(at_row == 0, query_bias[:, columns], 0.0)
            own = own + jnp.where(at_row == 1, value_bias[:, columns], 0.0)
            own = rows_of(bgrad_ref[index:index + 1, :], own, at_row, 2)
        pack[4 * width:, :] = own.astype(BF16)


def attention_grads(is_cross, place, aq, akv, dqkv, mixed, da, vgrad, bgrad, lane):
    rows, width = aq.shape
    length = 4 * width + 64
    operands = (aq, akv, *dqkv, mixed, da, vgrad, bgrad)
    count = width // lane
    return pl.pallas_call(
        functools.partial(attention_grads_kernel, is_cross, len(dqkv) // 3),
        grid_spec=pltpu.PrefetchScalarGridSpec(
            num_scalar_prefetch=1,
            grid=(1,),
            in_specs=[fixed(v.shape) for v in operands],
            out_specs=[fixed((length, lane))] * count,
            scratch_shapes=[pltpu.VMEM((width, width), BF16)],
        ),
        out_shape=[jax.ShapeDtypeStruct((length, lane), BF16)] * count,
        compiler_params=params(),
        cost_estimate=cost(8 * rows * width * width, 14 * rows * width),
        name="cross_grads" if is_cross else "self_grads",
    )(place, *operands)


def feed_forward_grads_kernel(z_ref, du_ref, g_ref, df_ref, *packs):
    width = z_ref.shape[1]
    for index, pack in enumerate(packs):

        @pl.when(pl.program_id(0) == index)
        def _(pack=pack):
            pack[:width, :] = dot_tl(z_ref[...], du_ref[...]).astype(BF16)
            pack[width:, :] = dot_tl(g_ref[...], df_ref[...]).astype(BF16)


def feed_forward_grads(z, du, g, df, first, hidden):
    rows, width = z.shape
    quarter = pl.BlockSpec((rows, hidden), lambda i: (0, first - i))
    pack = (width + hidden, width)
    return pl.pallas_call(
        feed_forward_grads_kernel,
        grid=(2,),
        in_specs=[fixed(z.shape), quarter, quarter, fixed(df.shape)],
        out_specs=[fixed(pack)] * 2,
        out_shape=[jax.ShapeDtypeStruct(pack, BF16)] * 2,
        compiler_params=params(),
        cost_estimate=cost(8 * rows * width * hidden, 12 * rows * hidden),
        name="feed_forward_grads",
    )(z, du, g, df)


def tokens(width, section=None):
    if section is None:
        return pl.BlockSpec((TB, width), lambda i, *_: (i, 0))
    if section == 0:
        return pl.BlockSpec((TB, width), lambda i, flag: (i * (1 - flag[0]), 0))
    return pl.BlockSpec((TB, width), lambda i, flag: (i * flag[0], 0))


def anywhere():
    return pl.BlockSpec(memory_space=pl.ANY)


def ff_scratch(ff_packs):
    return [
        pltpu.VMEM((len(ff_packs),) + ff_packs[0].shape, BF16),
        pltpu.SemaphoreType.DMA((len(ff_packs),)),
    ]


def fetch_packs(packs, weights_ref, sems, wanted):
    started = (pl.program_id(0) == 0) & wanted

    @pl.when(started)
    def _():
        for index, pack in enumerate(packs):
            pltpu.make_async_copy(pack, weights_ref.at[index], sems.at[index]).start()

    def wait():
        @pl.when(started)
        def _():
            for index, pack in enumerate(packs):
                pltpu.make_async_copy(pack, weights_ref.at[index], sems.at[index]).wait()

    return wait


def over_pieces(hidden, first, then):
    piece = hidden // PIECES
    order = [(index, slice(at, at + piece)) for index in range(4) for at in range(0, hidden, piece)]
    made = first(*order[0])
    for here, ahead in zip(order, order[1:] + [None]):
        coming = None if ahead is None else first(*ahead)
        then(*here, made)
        made = coming


def piece_lanes(index, columns, hidden):
    return slice(index * hidden + columns.start, index * hidden + columns.stop)


def fixed(shape):
    return pl.BlockSpec(shape, lambda i, *_: (0,) * len(shape))


def encoder_forward_kernel(
    flag_ref, mixed_ref, x_ref, out_ref, vec_ref, ff0, ff1, ff2, ff3, bias_ref,
    *refs,
):
    sum1_ref, h_ref, g_ref, slope_ref, sum2_ref, memory_ref, weights_ref, sems = refs
    width = x_ref.shape[1]
    hidden = ff0.shape[1]
    is_enc = flag_ref[0] == 0
    wait = fetch_packs((ff0, ff1, ff2, ff3), weights_ref, sems, is_enc)
    stream = x_ref[...].astype(F32)
    summed = stream + (dot(mixed_ref[...], out_ref[...]) + vec_ref[0])
    sum1_ref[...] = summed
    first = normed_of(summed)[0] * vec_ref[2] + vec_ref[3]
    h_ref[...] = first.astype(BF16)
    wait()

    @pl.when(is_enc)
    def _():
        sum2_ref[...] = first + stream + vec_ref[1]

        def hidden_of(index, columns):
            return dot(h_ref[...], weights_ref[index, :width, columns]) + bias_ref[index:index + 1, columns]

        def quarter(index, columns, pre):
            value, slope = gelu_parts(pre)
            value = value.astype(BF16)
            lanes = piece_lanes(index, columns, hidden)
            g_ref[:, lanes] = value
            slope_ref[:, lanes] = slope.astype(BF16)
            below = slice(width + columns.start, width + columns.stop)
            sum2_ref[...] = sum2_ref[...] + dot(value, weights_ref[index, below, :])

        over_pieces(hidden, hidden_of, quarter)
        last = (normed_of(sum2_ref[...])[0] * vec_ref[4] + vec_ref[5]).astype(BF16)
        memory_ref[...] = last


def encoder_forward(flag, mixed, stream, out_weight, vectors, ff_packs, bias):
    rows, width = stream.shape
    hidden = 4 * ff_packs[0].shape[1]
    operands = (flag, mixed, stream, out_weight, vectors, *ff_packs, bias)
    return pl.pallas_call(
        encoder_forward_kernel,
        grid_spec=pltpu.PrefetchScalarGridSpec(
            num_scalar_prefetch=1,
            grid=(rows // TB,),
            in_specs=[tokens(width), tokens(width), fixed(out_weight.shape), fixed(vectors.shape)]
            + [anywhere()] * len(ff_packs)
            + [fixed(bias.shape)],
            out_specs=[
                tokens(width), tokens(width), tokens(hidden, 0), tokens(hidden, 0), tokens(width, 0), tokens(width, 0)
            ],
            scratch_shapes=ff_scratch(ff_packs),
        ),
        out_shape=[
            jax.ShapeDtypeStruct((rows, width), F32),
            jax.ShapeDtypeStruct((rows, width), BF16),
            jax.ShapeDtypeStruct((rows, hidden), BF16),
            jax.ShapeDtypeStruct((rows, hidden), BF16),
            jax.ShapeDtypeStruct((rows, width), F32),
            jax.ShapeDtypeStruct((rows, width), BF16),
        ],
        compiler_params=params(),
        cost_estimate=cost(2 * rows * width * (width + 2 * hidden), 20 * rows * width),
        name="encoder_forward",
    )(*operands)


def decoder_kernel(
    flag_ref, mixed_ref, sum1_ref, x_ref, cot_ref, g_in, h_in, memory_in,
    out_ref, vec_ref, cvec_ref, ff0, ff1, ff2, ff3, bias_ref,
    result_ref, g_ref, z_ref, du_ref, df_ref, dcross_ref, dmixed_ref, dh_ref, dlast_ref, vgrad_ref, bgrad_ref,
    weights_ref, sems, slope_ref, total_ref,
):
    width = x_ref.shape[1]
    hidden = ff0.shape[1]
    wait = fetch_packs((ff0, ff1, ff2, ff3), weights_ref, sems, flag_ref[0] == 1)

    @pl.when(pl.program_id(0) == 0)
    def _():
        vgrad_ref[...] = jnp.zeros(vgrad_ref.shape, F32)
        bgrad_ref[...] = jnp.zeros(bgrad_ref.shape, F32)

    @pl.when(flag_ref[0] == 0)
    def _():
        result_ref[...] = memory_in[...]
        g_ref[...] = g_in[...]
        z_ref[...] = h_in[...]

    @pl.when(flag_ref[0] == 1)
    def _():
        stream = x_ref[...].astype(F32)
        first = normed_of(sum1_ref[...])[0] * vec_ref[2] + vec_ref[3]
        mixed = mixed_ref[...]
        crossed = dot(mixed, out_ref[...]) + cvec_ref[2:3, :]
        normed_c, inverse_c = normed_of(first + crossed)
        second = normed_c * cvec_ref[3:4, :] + cvec_ref[4:5, :]
        second_low = second.astype(BF16)
        z_ref[...] = second_low
        total_ref[...] = second + stream + vec_ref[1]
        wait()

        def hidden_of(index, columns):
            return dot(z_ref[...], weights_ref[index, :width, columns]) + bias_ref[index:index + 1, columns]

        def quarter(index, columns, pre):
            value, slope = gelu_parts(pre)
            value = value.astype(BF16)
            lanes = piece_lanes(index, columns, hidden)
            g_ref[:, lanes] = value
            slope_ref[:, lanes] = slope.astype(BF16)
            below = slice(width + columns.start, width + columns.stop)
            total_ref[...] = total_ref[...] + dot(value, weights_ref[index, below, :])

        over_pieces(hidden, hidden_of, quarter)
        normed, inverse = normed_of(total_ref[...])
        result_ref[...] = (normed * vec_ref[4] + vec_ref[5]).astype(BF16)
        grad = cot_ref[...].astype(F32)
        grad_last = norm_back(grad, normed, inverse, vec_ref[4])
        dlast_ref[...] = grad_last
        grad_ffn = grad_last.astype(BF16)
        df_ref[...] = grad_ffn
        total_ref[...] = grad_last

        def value_grad_of(index, columns):
            return dot_t(df_ref[...], weights_ref[index, width + columns.start:width + columns.stop, :])

        def quarter_back(index, columns, grad_value):
            lanes = piece_lanes(index, columns, hidden)
            grad_pre = (grad_value * slope_ref[:, lanes].astype(F32)).astype(BF16)
            du_ref[:, lanes] = grad_pre
            bgrad_ref[index:index + 1, columns] += column_sum(grad_pre)
            total_ref[...] = total_ref[...] + dot_t(grad_pre, weights_ref[index, :width, columns])

        over_pieces(hidden, value_grad_of, quarter_back)
        grad_second = total_ref[...]
        grad_cross = norm_back(grad_second, normed_c, inverse_c, cvec_ref[3:4, :])
        dh_ref[...] = grad_cross
        cross_low = grad_cross.astype(BF16)
        dcross_ref[...] = cross_low
        dmixed_ref[...] = dot_t(cross_low, out_ref[...]).astype(BF16)
        vgrad_ref[1:2, :] += column_sum(grad_ffn)
        vgrad_ref[4:5, :] += column_sum(grad * normed)
        vgrad_ref[5:6, :] += column_sum(grad)
        vgrad_ref[6:7, :] += column_sum(cross_low)
        vgrad_ref[7:8, :] += column_sum(grad_second * normed_c)
        vgrad_ref[8:9, :] += column_sum(grad_second)


def decoder_step(flag, mixed, sum1, stream, cot, g_in, h_in, memory_in, out_weight, vectors, cvec, ff_packs, bias):
    rows, width = stream.shape
    hidden = g_in.shape[1]
    return pl.pallas_call(
        decoder_kernel,
        grid_spec=pltpu.PrefetchScalarGridSpec(
            num_scalar_prefetch=1,
            grid=(rows // TB,),
            in_specs=[
                tokens(width, 1), tokens(width, 1), tokens(width, 1), tokens(width, 1), tokens(hidden, 0),
                tokens(width, 0), tokens(width, 0), fixed(out_weight.shape), fixed(vectors.shape), fixed(cvec.shape),
            ]
            + [anywhere()] * len(ff_packs)
            + [fixed(bias.shape)],
            out_specs=[
                tokens(width), tokens(hidden), tokens(width), tokens(hidden, 1), tokens(width, 1), tokens(width, 1),
                tokens(width, 1), tokens(width, 1), tokens(width, 1), fixed((16, width)), fixed(bias.shape),
            ],
            scratch_shapes=ff_scratch(ff_packs) + [pltpu.VMEM((TB, hidden), BF16), pltpu.VMEM((TB, width), F32)],
        ),
        out_shape=[
            jax.ShapeDtypeStruct((rows, width), BF16),
            jax.ShapeDtypeStruct((rows, hidden), BF16),
            jax.ShapeDtypeStruct((rows, width), BF16),
            jax.ShapeDtypeStruct((rows, hidden), BF16),
            jax.ShapeDtypeStruct((rows, width), BF16),
            jax.ShapeDtypeStruct((rows, width), BF16),
            jax.ShapeDtypeStruct((rows, width), BF16),
            jax.ShapeDtypeStruct((rows, width), F32),
            jax.ShapeDtypeStruct((rows, width), F32),
            jax.ShapeDtypeStruct((16, width), F32),
            jax.ShapeDtypeStruct(bias.shape, F32),
        ],
        compiler_params=params(),
        cost_estimate=cost(2 * rows * width * (2 * width + 4 * hidden), 40 * rows * width),
        name="decoder_step",
    )(flag, mixed, sum1, stream, cot, g_in, h_in, memory_in, out_weight, vectors, cvec, *ff_packs, bias)


def backward_kernel(
    flag_ref, cot_ref, dmem_ref, sum1_ref, sum2_ref, slope_ref,
    dh_in, dq_in, dlast_in, du_in, df_in, vgrad_in, bgrad_in,
    out_ref, cross_ref, vec_ref, ff0, ff1, ff2, ff3,
    du_ref, df_ref, da_ref, dmixed_ref, dres_ref, vgrad_ref, bgrad_ref, dfirst_ref, weights_ref, sems,
):
    width = cot_ref.shape[1]
    hidden = ff0.shape[1]
    wait = fetch_packs((ff0, ff1, ff2, ff3), weights_ref, sems, flag_ref[0] == 0)
    at_start = pl.program_id(0) == 0
    is_dec = flag_ref[0] == 1

    @pl.when(at_start & is_dec)
    def _():
        vgrad_ref[...] = vgrad_in[...]
        bgrad_ref[...] = bgrad_in[...]

    @pl.when(at_start & jnp.logical_not(is_dec))
    def _():
        vgrad_ref[...] = jnp.zeros(vgrad_ref.shape, F32)
        bgrad_ref[...] = jnp.zeros(bgrad_ref.shape, F32)

    @pl.when(is_dec)
    def _():
        du_ref[...] = du_in[...]
        df_ref[...] = df_in[...]
        dres_ref[...] = dlast_in[...]
        dfirst_ref[...] = dh_in[...] + dot_t(dq_in[...], cross_ref[...])

    @pl.when(jnp.logical_not(is_dec))
    def _():
        grad = cot_ref[...].astype(F32) + dmem_ref[...].astype(F32)
        normed, inverse = normed_of(sum2_ref[...])
        grad_last = norm_back(grad, normed, inverse, vec_ref[4])
        dres_ref[...] = grad_last
        grad_ffn = grad_last.astype(BF16)
        df_ref[...] = grad_ffn
        dfirst_ref[...] = grad_last
        wait()

        def value_grad_of(index, columns):
            return dot_t(df_ref[...], weights_ref[index, width + columns.start:width + columns.stop, :])

        def quarter_back(index, columns, grad_value):
            lanes = piece_lanes(index, columns, hidden)
            grad_pre = (grad_value * slope_ref[:, lanes].astype(F32)).astype(BF16)
            du_ref[:, lanes] = grad_pre
            bgrad_ref[index:index + 1, columns] += column_sum(grad_pre)
            dfirst_ref[...] = dfirst_ref[...] + dot_t(grad_pre, weights_ref[index, :width, columns])

        over_pieces(hidden, value_grad_of, quarter_back)
        vgrad_ref[1:2, :] += column_sum(grad_ffn)
        vgrad_ref[4:5, :] += column_sum(grad * normed)
        vgrad_ref[5:6, :] += column_sum(grad)

    grad_first = dfirst_ref[...]
    normed, inverse = normed_of(sum1_ref[...])
    grad_in = norm_back(grad_first, normed, inverse, vec_ref[2])
    low = grad_in.astype(BF16)
    da_ref[...] = low
    dmixed_ref[...] = dot_t(low, out_ref[...]).astype(BF16)
    dres_ref[...] = dres_ref[...] + grad_in
    vgrad_ref[0:1, :] += column_sum(low)
    vgrad_ref[2:3, :] += column_sum(grad_first * normed)
    vgrad_ref[3:4, :] += column_sum(grad_first)


def backward_step(
    flag, cot, dmem, sum1, sum2, slope, dh, dq, dlast, du, df, vgrad, bgrad, out_weight, cross_query, vectors, ff_packs
):
    rows, width = cot.shape
    hidden = du.shape[1]
    return pl.pallas_call(
        backward_kernel,
        grid_spec=pltpu.PrefetchScalarGridSpec(
            num_scalar_prefetch=1,
            grid=(rows // TB,),
            in_specs=[
                tokens(width, 0), tokens(width, 0), tokens(width), tokens(width, 0), tokens(hidden, 0),
                tokens(width, 1), tokens(width, 1), tokens(width, 1), tokens(hidden, 1), tokens(width, 1),
                fixed(vgrad.shape), fixed(bgrad.shape),
                fixed(out_weight.shape), fixed(cross_query.shape), fixed(vectors.shape),
            ]
            + [anywhere()] * len(ff_packs),
            out_specs=[
                tokens(hidden), tokens(width), tokens(width), tokens(width), tokens(width),
                fixed(vgrad.shape), fixed(bgrad.shape),
            ],
            scratch_shapes=[pltpu.VMEM((TB, width), F32)] + ff_scratch(ff_packs),
        ),
        out_shape=[
            jax.ShapeDtypeStruct((rows, hidden), BF16),
            jax.ShapeDtypeStruct((rows, width), BF16),
            jax.ShapeDtypeStruct((rows, width), BF16),
            jax.ShapeDtypeStruct((rows, width), BF16),
            jax.ShapeDtypeStruct((rows, width), F32),
            jax.ShapeDtypeStruct(vgrad.shape, F32),
            jax.ShapeDtypeStruct(bgrad.shape, F32),
        ],
        compiler_params=params(),
        cost_estimate=cost(2 * rows * width * (width + 2 * hidden), 40 * rows * width),
        name="backward_step",
    )(
        flag, cot, dmem, sum1, sum2, slope, dh, dq, dlast, du, df, vgrad, bgrad,
        out_weight, cross_query, vectors, *ff_packs,
    )


def input_kernel(dres_ref, *refs):
    *parts, weight_ref, dx_ref = refs
    total = dres_ref[...]
    at = 0
    for part in parts:
        wide = part.shape[1]
        total = total + dot_t(part[...], weight_ref[:, at:at + wide])
        at += wide
    dx_ref[...] = total.astype(BF16)


def input_step(dres, parts, weight):
    rows, width = dres.shape
    block = 256
    spec = lambda v: pl.BlockSpec((block, v.shape[1]), lambda i: (i, 0))
    return pl.pallas_call(
        input_kernel,
        grid=(rows // block,),
        in_specs=[spec(v) for v in (dres, *parts)] + [fixed(weight.shape)],
        out_specs=spec(dres),
        out_shape=jax.ShapeDtypeStruct((rows, width), BF16),
        compiler_params=params(),
        cost_estimate=cost(6 * rows * width * width, 12 * rows * width),
        name="input_step",
    )(dres, *parts, weight)


def finish_kernel(ff_ref, attn_ref, ffin_ref, ffout_ref, qkv_ref, out_ref, bias_ref, hidden_ref, vectors_ref):
    width = ffin_ref.shape[0]
    lane = attn_ref.shape[1]
    ffin_ref[...] = ff_ref[:width, :].astype(F32)
    ffout_ref[...] = ff_ref[width:, :].astype(F32)
    for index in range(3):
        qkv_ref[index] = attn_ref[index * width:(index + 1) * width, :].astype(F32)
    for index in range(width // lane):
        at = 3 * width + index * lane
        out_ref[:, index * lane:(index + 1) * lane] = attn_ref[at:at + lane, :].astype(F32)
    rows = attn_ref[4 * width:, :].astype(F32)
    bias_ref[...] = rows[0:2]
    for index in range(hidden_ref.shape[1] // lane):
        hidden_ref[:, index * lane:(index + 1) * lane] = rows[2 + index:3 + index]
    count = width // lane
    for index in range(6):
        for part in range(count):
            row = 16 + index * count + part
            vectors_ref[index, :, part * lane:(part + 1) * lane] = rows[row:row + 1]


def finish(ff_total, attn_total):
    width, lane = ff_total.shape[1], attn_total.shape[1]
    hidden = ff_total.shape[0] - width
    shapes = [(width, hidden), (hidden, width), (3, width, lane), (lane, width), (2, lane), (1, hidden), (6, 1, width)]
    return pl.pallas_call(
        finish_kernel,
        grid=(1,),
        in_specs=[fixed(ff_total.shape), fixed(attn_total.shape)],
        out_specs=[fixed(shape) for shape in shapes],
        out_shape=[jax.ShapeDtypeStruct(shape, F32) for shape in shapes],
        compiler_params=params(),
        cost_estimate=cost(0, 20 * width * width),
        name="finish",
    )(ff_total, attn_total)


def flipped(value, bits, section=None):
    count = lax.axis_size("tensor")
    if section is None:
        return lax.ppermute(value, "tensor", [(t, t ^ bits) for t in range(count)])
    base = section * count
    return lax.ppermute(value, ("pipe", "tensor"), [(base + t, base + (t ^ bits)) for t in range(count)])


def across(value, source, active):
    count = lax.axis_size("tensor")
    other = 1 - source
    pairs = [(source * count + t, other * count + t) for t in range(active)]
    return lax.ppermute(value, ("pipe", "tensor"), pairs)


def plus(own, received):
    return (own.astype(F32) + received.astype(F32)).astype(BF16)


def along_dp(part, level, section=None):
    count = lax.axis_size("dp")
    if section is None:
        return lax.ppermute(part, "dp", [(i, i ^ (1 << level)) for i in range(count)])
    base = section * count
    return lax.ppermute(part, ("pipe", "dp"), [(base + i, base + (i ^ (1 << level))) for i in range(count)])


def summed_whole(value, level, section=None, behind=()):
    return plus(after(value, *behind), along_dp(value, level, section))


def dp_bit(level):
    return lax.shift_right_logical(lax.axis_index("dp"), level) & 1


def halved(value, level, section=None, behind=()):
    rows = value.shape[0] // 2
    mine = dp_bit(level)
    got = along_dp(lax.dynamic_slice_in_dim(value, (1 - mine) * rows, rows, 0), level, section)
    return plus(lax.dynamic_slice_in_dim(after(value, *behind), mine * rows, rows, 0), got)


def doubled(value, level, section=None, behind=()):
    other = along_dp(value, level, section)
    upper = dp_bit(level) == 1
    value = after(value, *behind)
    return jnp.concatenate([jnp.where(upper, other, value), jnp.where(upper, value, other)], 0)


def after(value, *others):
    return lax.optimization_barrier((value, *others))[0]


def to_rows(shard):
    count = lax.axis_size("tensor")
    shard = jnp.pad(shard, ((0, count - shard.shape[0]), (0, 0), (0, 0)))
    out = lax.all_to_all(shard, "tensor", 0, 0, tiled=True)
    return out.reshape(count * shard.shape[1], shard.shape[2])


def from_rows(row, row_count):
    count = lax.axis_size("tensor")
    parts = row.reshape(count, row.shape[0] // count, row.shape[1])
    return lax.all_to_all(parts, "tensor", 0, 0, tiled=True)[:row_count]


def shards(
    inputs, cotangent, segments, pads, self_qkv, self_bias, self_out, ff_in, ff_bias, ff_out, vectors,
    cross_q, cross_kv, cross_out, cross_small, cross_gain,
):
    section = lax.axis_index("pipe").astype(jnp.int32)
    place = lax.axis_index("tensor").astype(jnp.int32)
    count = lax.axis_size("tensor")
    row_count = inputs.shape[1]
    decoder = section == 1
    flag, place_flag = section[None], place[None]
    width = inputs.shape[3]
    lane = self_qkv.shape[3]
    hidden = ff_in.shape[2]
    half = width // 2
    row = jnp.minimum(place, row_count - 1)

    attn_own, cross_half = first_packs(
        jnp.transpose(self_qkv[0], (1, 0, 2)), self_out[0], self_bias[0], ff_bias, cross_q,
        jnp.transpose(cross_kv, (1, 0, 2)), cross_out, cross_small, cross_gain[None],
    )
    attn_far, attn_near = flipped(attn_own, 2), flipped(attn_own, 1)
    stream = to_rows(after(inputs[0], attn_own))
    slots = jnp.concatenate(
        [
            lax.dynamic_index_in_dim(segments, row, 1, False),
            lax.dynamic_slice_in_dim(pads[0], row, 1, 0),
        ],
        0,
    )
    attn_packs = [attn_own, attn_near, attn_far, flipped(attn_far, 1)]
    other_half = across(cross_half, 0, count)
    ff_own = after(jnp.concatenate([ff_in[0], ff_out[0]], 0), stream, attn_far)
    ff_far, ff_near = flipped(ff_own, 2), flipped(ff_own, 1)
    vector_rows = jnp.transpose(vectors, (1, 0, 2))

    qkv, qkv_weight, out_weight, hidden_bias, own_code, key_code, target_code, source_code, self_bounds, cross_bounds = (
        query_key_value(flag, stream, slots, attn_packs)
    )
    parts = ((qkv, 0), (qkv, 1), (qkv, 2))
    self_codes, cross_codes = (own_code, key_code), (target_code, source_code)
    mixed, totals = attend_forward(self_bounds, self_codes, width, *parts)
    cross_own = jnp.concatenate([after(other_half, mixed), cross_half], 0)
    cross_far, cross_near = flipped(cross_own, 2, 1), flipped(cross_own, 1, 1)
    ff_packs = [ff_own, ff_near, ff_far, flipped(after(ff_far, cross_own), 1)]
    sum1, first_low, g_enc, slope, sum2, memory = encoder_forward(
        flag, mixed, stream, out_weight, vector_rows, ff_packs, hidden_bias
    )
    memory_in = across(memory, 0, row_count)
    cross_packs = [cross_own, cross_near, cross_far, flipped(after(cross_far, memory), 1, 1)]
    cot_row = to_rows(after(cotangent[0], memory))

    cross_query, cross_pair, cross_out_weight, cvec = cross_unpack(place_flag, cross_packs)
    cross_made = cross_project(first_low, memory_in, cross_query, cross_pair, cvec)
    cross_parts = ((cross_made, 0), (cross_made, 1), (cross_made, 2))
    cross_mixed, cross_totals = attend_forward(cross_bounds, cross_codes, width, *cross_parts)
    result, g_all, z_all, du_dec, df_dec, dcross, dcross_mixed, dh_dec, dlast_dec, vgrad_dec, bgrad_dec = decoder_step(
        flag, cross_mixed, sum1, stream, cot_row, g_enc, first_low, memory,
        cross_out_weight, vector_rows, cvec, ff_packs, hidden_bias,
    )
    dq_cross, dk_cross, dv_cross, dmemory = attend_backward(
        cross_bounds, cross_codes, *cross_parts, dcross_mixed, cross_totals, cross_pair
    )
    dmemory_in = across(dmemory, 1, row_count)
    cross_grads = attention_grads(
        True, place_flag, first_low, memory_in, (after(dq_cross, dmemory), dk_cross, dv_cross), cross_mixed, dcross,
        vgrad_dec, bgrad_dec, lane,
    )
    cross_far = plus(after(cross_grads[2], dmemory_in), flipped(cross_grads[3], 1, 1))
    cross_got = flipped(cross_grads[1], 1, 1)

    du_all, df_all, da, dmixed, dres, vgrad, bgrad = backward_step(
        flag, cot_row, dmemory_in, sum1, sum2, slope, dh_dec, after(dq_cross, cross_far, cross_grads[1]), dlast_dec,
        du_dec, df_dec, vgrad_dec, bgrad_dec, out_weight, cross_query, vector_rows, ff_packs,
    )
    cross_near = plus(after(cross_grads[0], da), cross_got)
    cross_part = plus(cross_near, flipped(cross_far, 2, 1))
    levels = range(lax.axis_size("dp").bit_length() - 1)
    ff_third, ff_second = feed_forward_grads(after(z_all, cross_part), du_all, g_all, df_all, 3, hidden)
    ff_first, ff_zeroth = feed_forward_grads(after(z_all, ff_second), du_all, g_all, df_all, 1, hidden)
    ff_far = plus(after(ff_second, ff_zeroth), flipped(ff_third, 1))
    ff_near = plus(after(ff_zeroth, ff_far), flipped(ff_first, 1))
    dqkv = attend_backward(self_bounds, self_codes, *parts, after(dmixed, ff_near), totals)
    cross_total = halved(cross_part, 0, 1, (dqkv[0],))
    ff_part = plus(after(ff_near, dqkv[0], cross_total), flipped(ff_far, 2))
    attn_grads = attention_grads(
        False, place_flag, stream, stream, (after(dqkv[0], ff_part), *dqkv[1:]), mixed, da, vgrad, bgrad, lane
    )
    ff_total = halved(ff_part, 0, behind=(attn_grads[3],))
    for level in levels[1:]:
        cross_total = halved(cross_total, level, 1, (ff_total,))
    attn_far = plus(after(attn_grads[2], ff_total, cross_total), flipped(attn_grads[3], 1))
    attn_near = plus(after(attn_grads[0], attn_far), flipped(attn_grads[1], 1))
    for level in levels[1:]:
        ff_total = halved(ff_total, level, behind=(attn_near,))
    cross_total = doubled(cross_total, levels[-1], 1, (ff_total,))
    attn_part = plus(after(attn_near, ff_total, cross_total), flipped(attn_far, 2))
    dx = input_step(after(dres, attn_part), dqkv, qkv_weight)
    ff_total = doubled(ff_total, levels[-1], behind=(dx,))
    attn_total = halved(attn_part, 0, behind=(ff_total,))
    for level in reversed(levels[:-1]):
        cross_total = doubled(cross_total, level, 1, (attn_total,))
    cross_other = across(cross_total, 1, count)
    input_grad = from_rows(after(dx, attn_total), row_count).astype(F32)[None]
    section_out = from_rows(after(result, attn_total), row_count)[None]
    for level in levels[1:]:
        attn_total = halved(attn_total, level, behind=(cross_total,))
    for level in reversed(levels[:-1]):
        ff_total = doubled(ff_total, level, behind=(attn_total, section_out, input_grad))
    attn_total = doubled(attn_total, levels[-1], behind=(ff_total,))
    cross_total, cross_other = after((cross_total, cross_other), attn_total)

    own, other = cross_total.astype(F32), cross_other.astype(F32)

    def halves(at):
        return jnp.where(decoder, own[at + half:at + 2 * half], other[at:at + half])

    cross_pair_grad = jnp.stack([halves(width), halves(2 * width)], 1)
    cross_out_grad = jnp.transpose(halves(3 * width).reshape(half // lane, lane, lane), (1, 0, 2)).reshape(lane, half)
    own_rows, other_rows = (v[4 * width:4 * width + 5 * count].reshape(5, width) for v in (own, other))
    small_grad = jnp.where(decoder, jnp.stack([own_rows[2], own_rows[4]]), other_rows[:2])
    gain_grad = jnp.where(decoder, own_rows[3, half:], other_rows[3, :half])
    cross_first, cross_last = halves(0), (cross_pair_grad, cross_out_grad, small_grad, gain_grad)
    for level in reversed(levels[:-1]):
        attn_total = doubled(attn_total, level, behind=(cross_first, *cross_last))
    ffin_grad, ffout_grad, qkv_grad, out_grad, bias_grad, hidden_grad, vectors_grad = finish(
        ff_total, attn_total
    )
    return (
        section_out,
        input_grad,
        jnp.transpose(qkv_grad, (1, 0, 2))[None],
        bias_grad[None],
        out_grad[None],
        ffin_grad[None],
        hidden_grad,
        ffout_grad[None],
        jnp.transpose(vectors_grad, (1, 0, 2)),
        cross_first,
        *cross_last,
    )


def solution(mesh):
    token_spec = P("pipe", "dp", "tensor", None)
    weights = (
        P("pipe", None, None, "tensor"),
        P("pipe", None, "tensor"),
        P("pipe", "tensor", None),
        P("pipe", None, "tensor"),
        P("pipe", "tensor"),
        P("pipe", "tensor", None),
        P("pipe", None, None),
        P("pipe", "tensor"),
        P("pipe", None, "tensor"),
        P("tensor", "pipe"),
        P("pipe", None),
        P("pipe"),
    )
    return jax.shard_map(
        shards,
        mesh=mesh,
        in_specs=(token_spec, token_spec, P(None, "dp", None), P("pipe", "dp", None)) + weights,
        out_specs=(token_spec, token_spec) + weights,
        check_vma=False,
    )
```

```python
import functools

import jax
import jax.numpy as jnp
from jax import lax
from jax.experimental import pallas as pl
from jax.experimental.pallas import tpu as pltpu
from jax.sharding import PartitionSpec as P

HEAD_DIM = 64
EPSILON = 1e-05
MASKED = -1e30
SEGS = 8
QF = 256
QB = 256
TB = 512
PIECES = 1
PAIR = 2 * HEAD_DIM
GELU_C = 0.7978845608028654
GELU_A = 0.044715
VMEM_LIMIT = 56 * 1024 * 1024
F32 = jnp.float32
BF16 = jnp.bfloat16


def dot(left, right):
    return jnp.dot(left, right, preferred_element_type=F32)


def dot_t(left, right):
    return lax.dot_general(left, right, (((1,), (1,)), ((), ())), preferred_element_type=F32)


def dot_tl(left, right):
    return lax.dot_general(left, right, (((0,), (0,)), ((), ())), preferred_element_type=F32)


def normed_of(values):
    center = values - jnp.mean(values, -1, keepdims=True)
    inverse = lax.rsqrt(jnp.mean(center * center, -1, keepdims=True) + EPSILON)
    return center * inverse, inverse


def norm_back(grad, normed, inverse, gain):
    scaled = grad * gain
    mean_scaled = jnp.mean(scaled, -1, keepdims=True)
    mean_both = jnp.mean(scaled * normed, -1, keepdims=True)
    return (scaled - mean_scaled - normed * mean_both) * inverse


def column_sum(values):
    return jnp.sum(values.astype(F32), 0, keepdims=True)


def gelu_parts(pre):
    squared = pre * pre
    half = 0.5 * jnp.tanh(pre * (GELU_C + (GELU_C * GELU_A) * squared)) + 0.5
    slope = half + (pre * (half - half * half)) * (2.0 * GELU_C + (6.0 * GELU_C * GELU_A) * squared)
    return pre * half, slope


def cost(flops, moved):
    return pl.CostEstimate(flops=int(flops) // 64, bytes_accessed=int(moved) // 64, transcendentals=0)


def params(axes=1):
    return pltpu.CompilerParams(
        dimension_semantics=("arbitrary",) * axes, vmem_limit_bytes=VMEM_LIMIT
    )


def find_segments(section, slots_ref, own_ref, key_ref, target_ref, source_ref, self_ref, cross_ref):
    length = slots_ref.shape[1]
    source = slots_ref[0:1, :].astype(F32)
    target = slots_ref[1:2, :].astype(F32)
    own = jnp.where(section == 1, target, source)
    own_ref[...] = own
    key_ref[...] = jnp.where(slots_ref[2:3, :] == 0, own, -1.0)
    target_ref[...] = target
    source_ref[...] = source

    def starts(segments):
        found = [jnp.int32(0)]
        for index in range(1, SEGS):
            found.append(jnp.sum(jnp.where(segments < float(index), 1.0, 0.0)).astype(jnp.int32))
        return found + [jnp.int32(length)]

    source_starts, target_starts = starts(source), starts(target)
    for index in range(SEGS):
        own_start = jnp.where(section == 1, target_starts[index], source_starts[index])
        own_end = jnp.where(section == 1, target_starts[index + 1], source_starts[index + 1])
        self_ref[index] = own_start
        self_ref[16 + index] = own_start
        self_ref[32 + index] = own_end
        cross_ref[index] = target_starts[index]
        cross_ref[16 + index] = source_starts[index]
        cross_ref[32 + index] = source_starts[index + 1]
    self_ref[48] = jnp.int32(1)
    self_ref[49] = section
    self_ref[50] = jnp.int32(1)
    cross_ref[48] = jnp.int32(0)
    cross_ref[49] = jnp.int32(0)
    cross_ref[50] = section


def half_masked(values, side):
    lane = lax.broadcasted_iota(jnp.int32, values.shape, 1)
    return jnp.where((lane >= HEAD_DIM) == bool(side), values, jnp.zeros_like(values))


def key_window(bounds, block, block_rows):
    first = block * block_rows
    last = first + (block_rows - 1)
    low, high = jnp.int32(0), jnp.int32(0)
    for index in range(SEGS):
        low = jnp.where(bounds[index] <= first, bounds[16 + index], low)
        high = jnp.where(bounds[index] <= last, bounds[32 + index], high)
    high = jnp.where(bounds[49] == 1, jnp.minimum(high, last + 1), high)
    low_block = lax.shift_right_logical(low, 7)
    high_block = lax.shift_right_logical(high + 127, 7)
    return low_block, jnp.where(bounds[50] == 1, high_block - low_block, 0)


def by_size(bounds, block, block_rows, key_blocks, sizes, body):
    low_block, needed = key_window(bounds, block, block_rows)
    below = 0
    for size in sizes:
        size = min(size, key_blocks)
        if size == below:
            continue

        @pl.when((needed > below) & (needed <= size))
        def _(size=size):
            start = jnp.minimum(low_block, key_blocks - size) * 128
            body(size, pl.multiple_of(start, 128))

        below = size


def as_columns(row):
    parts = []
    for at in range(0, row.shape[1], 128):
        parts.append(jnp.broadcast_to(row[:, at:at + 128], (128, 128)).T)
    return jnp.concatenate(parts, 0)


def window_bias(bounds, block, block_rows, start, key_code, qcode_ref):
    key_at = start + lax.broadcasted_iota(jnp.int32, key_code.shape, 0)
    tiles = []
    for at in range(0, block_rows, 128):
        query_at = block * block_rows + at + lax.broadcasted_iota(jnp.int32, (1, 128), 1)
        limit = jnp.where(bounds[49] == 1, query_at, jnp.int32(1 << 30))
        same_at = jnp.where(bounds[48] == 1, query_at, -1)
        opened = (key_code == qcode_ref[:, at:at + 128]) & (key_at <= limit)
        tiles.append(jnp.where(opened | (key_at == same_at), 0.0, MASKED))
    return jnp.concatenate(tiles, 1)


def attend_forward_kernel(bounds, q_ref, k_ref, v_ref, qcode_ref, kcode_ref, mixed_ref, total_ref):
    block = pl.program_id(0)
    heads = q_ref.shape[1] // HEAD_DIM
    key_blocks = k_ref.shape[0] // 128
    own_code = as_columns(qcode_ref[...])
    query_at = block * QF + lax.broadcasted_iota(jnp.int32, (QF, 128), 0)
    limit = jnp.where(bounds[49] == 1, query_at, jnp.int32(1 << 30))
    same_at = jnp.where(bounds[48] == 1, query_at, -1)
    lane = lax.broadcasted_iota(jnp.int32, (QF, 128), 1)

    def body(size, start):
        window = pl.ds(start, size * 128)
        tiles = []
        for tile in range(size):
            at = start + tile * 128
            key_at = at + lane
            opened = (own_code == kcode_ref[:, pl.ds(pl.multiple_of(at, 128), 128)]) & (key_at <= limit)
            tiles.append(jnp.where(opened | (key_at == same_at), 0.0, MASKED))
        bias = jnp.concatenate(tiles, 1)

        def two_pairs(index, columns):
            lanes = [pl.ds(pl.multiple_of((2 * index + at) * PAIR, PAIR), PAIR) for at in range(2)]
            scores = []
            for at in range(2):
                queries, keys = q_ref[:, lanes[at]], k_ref[window, lanes[at]]
                scores.append([dot_t(half_masked(queries, side), keys) + bias for side in range(2)])
            for at in range(2):
                values = v_ref[window, lanes[at]]
                out = None
                for side in range(2):
                    top = jnp.max(scores[at][side], -1, keepdims=True)
                    weights = jnp.exp(scores[at][side] - top)
                    total = jnp.sum(weights, -1, keepdims=True)
                    part = dot(weights.astype(BF16), half_masked(values, side)) * (1.0 / total)
                    out = part if out is None else out + part
                    columns = jnp.where(lane == (2 * index + at) * 2 + side, top + jnp.log(total), columns)
                mixed_ref[:, lanes[at]] = out.astype(BF16)
            return columns

        columns = lax.fori_loop(0, heads // 4, two_pairs, jnp.zeros((QF, 128), F32))
        total_ref[...] = columns.T[:heads]

    by_size(bounds, block, QF, key_blocks, (2, 3, 4, 5, 6, 8), body)


def attend_forward(bounds, codes, width, queries, keys, values):
    (q_array, q_at), (k_array, k_at), (v_array, v_at) = queries, keys, values
    rows = q_array.shape[0]
    heads = width // HEAD_DIM
    whole = lambda at: (lambda i, *_: (0, at))
    return pl.pallas_call(
        attend_forward_kernel,
        grid_spec=pltpu.PrefetchScalarGridSpec(
            num_scalar_prefetch=1,
            grid=(rows // QF,),
            in_specs=[
                pl.BlockSpec((QF, width), lambda i, *_: (i, q_at)),
                pl.BlockSpec((rows, width), whole(k_at)),
                pl.BlockSpec((rows, width), whole(v_at)),
                pl.BlockSpec((1, QF), lambda i, *_: (0, i)),
                pl.BlockSpec((1, rows), whole(0)),
            ],
            out_specs=[
                pl.BlockSpec((QF, width), lambda i, *_: (i, 0)),
                pl.BlockSpec((heads, QF), lambda i, *_: (0, i)),
            ],
        ),
        out_shape=[
            jax.ShapeDtypeStruct((rows, width), BF16),
            jax.ShapeDtypeStruct((heads, rows), F32),
        ],
        compiler_params=params(),
        cost_estimate=cost(4 * rows * 512 * width * 2, 8 * rows * width),
        name="attend_forward",
    )(bounds, q_array, k_array, v_array, *codes)


def attend_backward_kernel(has_weight, first_head, bounds, q_ref, k_ref, v_ref, grad_ref, total_ref, qcode_ref, kcode_ref, *refs):
    if has_weight:
        weight_ref, dq_ref, dk_ref, dv_ref, dmem_ref, kcol_ref, dkacc_ref, dvacc_ref = refs
    else:
        dq_ref, dk_ref, dv_ref, kcol_ref, dkacc_ref, dvacc_ref = refs
    block = pl.program_id(0)
    width = q_ref.shape[1]
    heads = width // HEAD_DIM
    key_blocks = k_ref.shape[0] // 128

    @pl.when(block == 0)
    def _():
        dkacc_ref[...] = jnp.zeros(dkacc_ref.shape, F32)
        dvacc_ref[...] = jnp.zeros(dvacc_ref.shape, F32)
        kcol_ref[...] = as_columns(kcode_ref[...])

    def body(size, start):
        window = pl.ds(start, size * 128)
        bias = window_bias(bounds, block, QB, start, kcol_ref[window, :], qcode_ref)

        def two_pairs(index, carry):
            prepared = []
            for at in range(2):
                pair = 2 * index + at
                lanes = pl.ds(pl.multiple_of(pair * PAIR, PAIR), PAIR)
                queries, grads = q_ref[:, lanes], grad_ref[:, lanes]
                keys, values = k_ref[window, lanes], v_ref[window, lanes]
                query_halves = [half_masked(queries, side) for side in range(2)]
                grad_halves = [half_masked(grads, side) for side in range(2)]
                products = [
                    (dot_t(keys, query_halves[side]) + bias, dot_t(values, grad_halves[side])) for side in range(2)
                ]
                prepared.append((pair, lanes, keys, query_halves, grad_halves, products))
            for pair, lanes, keys, query_halves, grad_halves, products in prepared:
                dq = dk = dv = None
                for side in range(2):
                    scores, grad_weights = products[side]
                    weights = jnp.exp(scores - total_ref[pl.ds(first_head + pair * 2 + side, 1), :])
                    delta = jnp.sum(weights * grad_weights, 0, keepdims=True)
                    grad_scores = (weights * (grad_weights - delta)).astype(BF16)
                    made = (
                        dot_tl(grad_scores, half_masked(keys, side)),
                        dot(grad_scores, query_halves[side]),
                        dot(weights.astype(BF16), grad_halves[side]),
                    )
                    dq, dk, dv = made if dq is None else (dq + made[0], dk + made[1], dv + made[2])
                dkacc_ref[window, lanes] = dkacc_ref[window, lanes] + dk
                dvacc_ref[window, lanes] = dvacc_ref[window, lanes] + dv
                dq_ref[:, lanes] = (dq * HEAD_DIM ** (-0.5)).astype(BF16)
            return carry

        lax.fori_loop(0, heads // 4, two_pairs, 0)

    by_size(bounds, block, QB, key_blocks, (2, 3, 4, 5, 6, 8), body)

    @pl.when(block == pl.num_programs(0) - 1)
    def _():
        dk_ref[...] = dkacc_ref[...].astype(BF16)
        dv_ref[...] = dvacc_ref[...].astype(BF16)
        if has_weight:
            summed = dot_t(dk_ref[...], weight_ref[:, :width]) + dot_t(dv_ref[...], weight_ref[:, width:])
            dmem_ref[...] = summed.astype(BF16)


def attend_backward(bounds, codes, queries, keys, values, grad, totals, weight=None, part=(0, 1)):
    (q_array, q_at), (k_array, k_at), (v_array, v_at) = queries, keys, values
    index, count = part
    rows = grad.shape[0]
    heads = totals.shape[0]
    width = grad.shape[1] // count
    whole = lambda at: pl.BlockSpec((rows, width), lambda i, *_: (0, at * count + index))
    block = lambda at: pl.BlockSpec((QB, width), lambda i, *_: (i, at * count + index))
    extra = [] if weight is None else [weight]
    first = pl.BlockSpec((rows, width), lambda i, *_: (0, 0))
    return pl.pallas_call(
        functools.partial(attend_backward_kernel, weight is not None, index * heads // count),
        grid_spec=pltpu.PrefetchScalarGridSpec(
            num_scalar_prefetch=1,
            grid=(rows // QB,),
            in_specs=[
                block(q_at),
                whole(k_at),
                whole(v_at),
                block(0),
                pl.BlockSpec((heads, QB), lambda i, *_: (0, i)),
                pl.BlockSpec((1, QB), lambda i, *_: (0, i)),
                pl.BlockSpec((1, rows), lambda i, *_: (0, 0)),
            ]
            + [fixed(v.shape) for v in extra],
            out_specs=[pl.BlockSpec((QB, width), lambda i, *_: (i, 0))] + [first] * (2 + len(extra)),
            scratch_shapes=[
                pltpu.VMEM((rows, 128), F32),
                pltpu.VMEM((rows, width), F32),
                pltpu.VMEM((rows, width), F32),
            ],
        ),
        out_shape=[jax.ShapeDtypeStruct((rows, width), BF16)] * (3 + len(extra)),
        compiler_params=params(),
        cost_estimate=cost(10 * rows * 512 * width * 2, 16 * rows * width),
        name="attend_backward",
    )(bounds, q_array, k_array, v_array, grad, totals, *codes, *extra)


def first_packs_kernel(
    qkv_ref, out_ref, bias_ref, ffb_ref, query_ref, pair_ref, cout_ref, small_ref, gain_ref, pack_ref, half_ref
):
    width = qkv_ref.shape[1]
    lane = qkv_ref.shape[2]
    half = query_ref.shape[0]

    def columns(values):
        return [values[:, at:at + lane] for at in range(0, values.shape[1], lane)]

    def filled(rows):
        rest = jnp.zeros((16 - sum(part.shape[0] for part in rows), lane), F32)
        return jnp.concatenate([*rows, rest], 0).astype(BF16)

    for index in range(3):
        pack_ref[index * width:(index + 1) * width, :] = qkv_ref[index]
    for index, part in enumerate(columns(out_ref[...])):
        at = 3 * width + index * lane
        pack_ref[at:at + lane, :] = part
    bias = bias_ref[...]
    high = bias.astype(BF16).astype(F32)
    middle = (bias - high).astype(BF16).astype(F32)
    least = bias - high - middle
    pack_ref[4 * width:4 * width + 16, :] = filled([high, middle, least, *columns(ffb_ref[...].astype(F32))])
    half_ref[0:half, :] = query_ref[...]
    half_ref[half:2 * half, :] = pair_ref[0]
    half_ref[2 * half:3 * half, :] = pair_ref[1]
    for index, part in enumerate(columns(cout_ref[...])):
        at = 3 * half + index * lane
        half_ref[at:at + lane, :] = part
    small = small_ref[...].astype(F32)
    half_ref[4 * half:4 * half + 16, :] = filled(
        [*columns(small[0:1]), *columns(small[1:2]), *columns(gain_ref[...].astype(F32))]
    )


def first_packs(qkv, out_weight, bias, ff_bias, query, pair, cross_out, small, gain):
    width, lane = qkv.shape[1:]
    half = query.shape[0]
    operands = (qkv, out_weight, bias, ff_bias, query, pair, cross_out, small, gain)
    shapes = [(4 * width + 16, lane), (4 * half + 16, lane)]
    return pl.pallas_call(
        first_packs_kernel,
        grid=(1,),
        in_specs=[fixed(v.shape) for v in operands],
        out_specs=[fixed(shape) for shape in shapes],
        out_shape=[jax.ShapeDtypeStruct(shape, BF16) for shape in shapes],
        compiler_params=params(),
        cost_estimate=cost(0, 24 * width * lane),
        name="first_packs",
    )(*operands)


def query_key_value_kernel(
    flag_ref, x_ref, slots_ref, p0, p1, p2, p3, qkv_ref, weight_ref, out_ref, hidden_ref, *refs
):
    *found_refs, bias_ref = refs
    width = x_ref.shape[1]
    lane = p0.shape[1]

    @pl.when(pl.program_id(0) == 0)
    def _():
        find_segments(flag_ref[0], slots_ref, *found_refs)
        for index, pack in enumerate((p0, p1, p2, p3)):
            columns = slice(index * lane, (index + 1) * lane)
            for part in range(3):
                at = slice(part * width + index * lane, part * width + (index + 1) * lane)
                weight_ref[:, at] = pack[part * width:(part + 1) * width, :]
            for part in range(width // lane):
                at = 3 * width + part * lane
                out_ref[columns, part * lane:(part + 1) * lane] = pack[at:at + lane, :]
            rows = pack[4 * width:4 * width + 16, :].astype(F32)
            bias_ref[0:1, columns] = rows[0:1] + rows[2:3] + rows[4:5]
            bias_ref[1:2, columns] = rows[1:2] + rows[3:4] + rows[5:6]
            for part in range(width // lane):
                hidden_ref[index:index + 1, part * lane:(part + 1) * lane] = rows[6 + part:7 + part]

    made = dot(x_ref[...], weight_ref[...])
    scale = HEAD_DIM ** (-0.5)
    queries = (made[:, :width] + bias_ref[0:1, :]).astype(BF16).astype(F32) * scale
    qkv_ref[:, :width] = queries.astype(BF16)
    qkv_ref[:, width:2 * width] = made[:, width:2 * width].astype(BF16)
    qkv_ref[:, 2 * width:] = (made[:, 2 * width:] + bias_ref[1:2, :]).astype(BF16)


def query_key_value(flag, stream, slots, packs):
    rows, width = stream.shape
    line = jax.ShapeDtypeStruct((1, rows), F32)
    bounds = jax.ShapeDtypeStruct((64,), jnp.int32)
    return pl.pallas_call(
        query_key_value_kernel,
        grid_spec=pltpu.PrefetchScalarGridSpec(
            num_scalar_prefetch=1,
            grid=(rows // TB,),
            in_specs=[tokens(width), fixed(slots.shape)] + [fixed(pack.shape) for pack in packs],
            out_specs=[tokens(3 * width), fixed((width, 3 * width)), fixed((width, width)), fixed((len(packs), width))]
            + [fixed(line.shape)] * 4
            + [pl.BlockSpec(memory_space=pltpu.SMEM)] * 2,
            scratch_shapes=[pltpu.VMEM((8, width), F32)],
        ),
        out_shape=[
            jax.ShapeDtypeStruct((rows, 3 * width), BF16),
            jax.ShapeDtypeStruct((width, 3 * width), BF16),
            jax.ShapeDtypeStruct((width, width), BF16),
            jax.ShapeDtypeStruct((len(packs), width), F32),
        ]
        + [line] * 4
        + [bounds] * 2,
        compiler_params=params(),
        cost_estimate=cost(6 * rows * width * width, 10 * rows * width),
        name="query_key_value",
    )(flag, stream, slots, *packs)


def cross_project_kernel(h_ref, memory_ref, query_ref, pair_ref, cvec_ref, made_ref):
    width = h_ref.shape[1]
    queries = (dot(h_ref[...], query_ref[...]) + cvec_ref[0:1, :]).astype(BF16).astype(F32)
    made_ref[:, :width] = (queries * HEAD_DIM ** (-0.5)).astype(BF16)
    made = dot(memory_ref[...], pair_ref[...])
    made_ref[:, width:2 * width] = made[:, :width].astype(BF16)
    made_ref[:, 2 * width:] = (made[:, width:] + cvec_ref[1:2, :]).astype(BF16)


def cross_project(h, memory, query, pair, cvec):
    rows, width = h.shape
    operands = (h, memory, query, pair, cvec)
    return pl.pallas_call(
        cross_project_kernel,
        grid=(rows // TB,),
        in_specs=[tokens(width)] * 2 + [fixed(v.shape) for v in operands[2:]],
        out_specs=tokens(3 * width),
        out_shape=jax.ShapeDtypeStruct((rows, 3 * width), BF16),
        compiler_params=params(),
        cost_estimate=cost(6 * rows * width * width, 12 * rows * width),
        name="cross_project",
    )(*operands)


def cross_unpack_kernel(place_ref, p0, p1, p2, p3, query_ref, pair_ref, out_ref, cvec_ref):
    lane = p0.shape[1]
    length = p0.shape[0] // 2
    half = (length - 16) // 4
    width = 2 * half
    count = width // lane
    for index, pack in enumerate((p0, p1, p2, p3)):
        columns = slice(index * lane, (index + 1) * lane)
        for side in range(2):
            rows = slice(side * half, (side + 1) * half)
            base = side * length
            query_ref[rows, columns] = pack[base:base + half, :]
            pair_ref[rows, columns] = pack[base + half:base + 2 * half, :]
            pair_ref[rows, width + index * lane:width + (index + 1) * lane] = pack[base + 2 * half:base + 3 * half, :]
            for part in range(half // lane):
                at = base + 3 * half + part * lane
                to = side * half + part * lane
                out_ref[columns, to:to + lane] = pack[at:at + lane, :]
    first = p0[4 * half:4 * half + 16, :].astype(F32)
    second = p0[length + 4 * half:length + 4 * half + 16, :].astype(F32)
    at_row = lax.broadcasted_iota(jnp.int32, (16, lane), 0)
    for index in range(count):
        columns = slice(index * lane, (index + 1) * lane)
        for which in range(2):
            wanted = which * count + (place_ref[0] ^ index)
            cvec_ref[which:which + 1, columns] = jnp.sum(jnp.where(at_row == wanted, first, 0.0), 0, keepdims=True)
        cvec_ref[2:3, columns] = second[index:index + 1]
        cvec_ref[4:5, columns] = second[count + index:count + index + 1]
        side, part = (first, index) if index < count // 2 else (second, index - count // 2)
        cvec_ref[3:4, columns] = side[2 * count + part:2 * count + part + 1]
    cvec_ref[5:8, :] = jnp.zeros((3, width), F32)


def cross_unpack(place, packs):
    length, lane = packs[0].shape
    width = (length // 2 - 16) // 2
    return pl.pallas_call(
        cross_unpack_kernel,
        grid_spec=pltpu.PrefetchScalarGridSpec(
            num_scalar_prefetch=1,
            grid=(1,),
            in_specs=[fixed(pack.shape) for pack in packs],
            out_specs=[fixed((width, width)), fixed((width, 2 * width)), fixed((width, width)), fixed((8, width))],
        ),
        out_shape=[
            jax.ShapeDtypeStruct((width, width), BF16),
            jax.ShapeDtypeStruct((width, 2 * width), BF16),
            jax.ShapeDtypeStruct((width, width), BF16),
            jax.ShapeDtypeStruct((8, width), F32),
        ],
        compiler_params=params(),
        cost_estimate=cost(0, 16 * width * width),
        name="cross_unpack",
    )(place, *packs)


def rows_of(vector, rows, at_row, base, order=None):
    lane = rows.shape[1]
    for index in range(vector.shape[1] // lane):
        to = base + (index if order is None else (order ^ index))
        rows = rows + jnp.where(at_row == to, vector[:, index * lane:(index + 1) * lane], 0.0)
    return rows


def attention_grads_kernel(
    is_cross, parts, place_ref, aq_ref, akv_ref, *refs
):
    width = aq_ref.shape[1]
    dq_refs, dk_refs, dv_refs = (refs[part * parts:(part + 1) * parts] for part in range(3))
    mixed_ref, da_ref, vgrad_ref, bgrad_ref, *packs, made_ref = refs[3 * parts:]
    lane = packs[0].shape[1]
    count = width // lane
    tail = packs[0].shape[0] - 4 * width
    akv = akv_ref if is_cross else aq_ref
    for part, (left, rights) in enumerate(((aq_ref, dq_refs), (akv, dk_refs), (akv, dv_refs))):
        for index, right in enumerate(rights):
            wide = width // parts
            made_ref[:, index * wide:(index + 1) * wide] = dot_tl(left[...], right[...]).astype(BF16)
        for index, pack in enumerate(packs):
            pack[part * width:(part + 1) * width, :] = made_ref[:, index * lane:(index + 1) * lane]
    made_ref[...] = dot_tl(mixed_ref[...], da_ref[...]).astype(BF16)
    for index, pack in enumerate(packs):
        for part in range(count):
            at = 3 * width + part * lane
            pack[at:at + lane, :] = made_ref[index * lane:(index + 1) * lane, part * lane:(part + 1) * lane]
    query_bias, value_bias = (
        jnp.concatenate([column_sum(ref[...]) for ref in some], 1) for some in (dq_refs, dv_refs)
    )
    at_row = lax.broadcasted_iota(jnp.int32, (tail, lane), 0)
    rows = jnp.zeros((tail, lane), F32)
    if is_cross:
        rows = rows_of(query_bias, rows, at_row, 0, place_ref[0])
        rows = rows_of(value_bias, rows, at_row, count, place_ref[0])
        for index in range(3):
            rows = rows_of(vgrad_ref[6 + index:7 + index, :], rows, at_row, (2 + index) * count)
    else:
        for index in range(6):
            rows = rows_of(vgrad_ref[index:index + 1, :], rows, at_row, 16 + index * count)
    for index, pack in enumerate(packs):
        own = rows
        if not is_cross:
            columns = slice(index * lane, (index + 1) * lane)
            own = own + jnp.where(at_row == 0, query_bias[:, columns], 0.0)
            own = own + jnp.where(at_row == 1, value_bias[:, columns], 0.0)
            own = rows_of(bgrad_ref[index:index + 1, :], own, at_row, 2)
        pack[4 * width:, :] = own.astype(BF16)


def attention_grads(is_cross, place, aq, akv, dqkv, mixed, da, vgrad, bgrad, lane):
    rows, width = aq.shape
    length = 4 * width + 64
    operands = (aq, akv, *dqkv, mixed, da, vgrad, bgrad)
    count = width // lane
    return pl.pallas_call(
        functools.partial(attention_grads_kernel, is_cross, len(dqkv) // 3),
        grid_spec=pltpu.PrefetchScalarGridSpec(
            num_scalar_prefetch=1,
            grid=(1,),
            in_specs=[fixed(v.shape) for v in operands],
            out_specs=[fixed((length, lane))] * count,
            scratch_shapes=[pltpu.VMEM((width, width), BF16)],
        ),
        out_shape=[jax.ShapeDtypeStruct((length, lane), BF16)] * count,
        compiler_params=params(),
        cost_estimate=cost(8 * rows * width * width, 14 * rows * width),
        name="cross_grads" if is_cross else "self_grads",
    )(place, *operands)


def feed_forward_grads_kernel(z_ref, du_ref, g_ref, df_ref, *packs):
    width = z_ref.shape[1]
    for index, pack in enumerate(packs):

        @pl.when(pl.program_id(0) == index)
        def _(pack=pack):
            pack[:width, :] = dot_tl(z_ref[...], du_ref[...]).astype(BF16)
            pack[width:, :] = dot_tl(g_ref[...], df_ref[...]).astype(BF16)


def feed_forward_grads(z, du, g, df, first, hidden):
    rows, width = z.shape
    quarter = pl.BlockSpec((rows, hidden), lambda i: (0, first - i))
    pack = (width + hidden, width)
    return pl.pallas_call(
        feed_forward_grads_kernel,
        grid=(2,),
        in_specs=[fixed(z.shape), quarter, quarter, fixed(df.shape)],
        out_specs=[fixed(pack)] * 2,
        out_shape=[jax.ShapeDtypeStruct(pack, BF16)] * 2,
        compiler_params=params(),
        cost_estimate=cost(8 * rows * width * hidden, 12 * rows * hidden),
        name="feed_forward_grads",
    )(z, du, g, df)


def tokens(width, section=None):
    if section is None:
        return pl.BlockSpec((TB, width), lambda i, *_: (i, 0))
    if section == 0:
        return pl.BlockSpec((TB, width), lambda i, flag: (i * (1 - flag[0]), 0))
    return pl.BlockSpec((TB, width), lambda i, flag: (i * flag[0], 0))


def anywhere():
    return pl.BlockSpec(memory_space=pl.ANY)


def ff_scratch(ff_packs):
    return [
        pltpu.VMEM((len(ff_packs),) + ff_packs[0].shape, BF16),
        pltpu.SemaphoreType.DMA((len(ff_packs),)),
    ]


def fetch_packs(packs, weights_ref, sems, wanted):
    started = (pl.program_id(0) == 0) & wanted

    @pl.when(started)
    def _():
        for index, pack in enumerate(packs):
            pltpu.make_async_copy(pack, weights_ref.at[index], sems.at[index]).start()

    def wait():
        @pl.when(started)
        def _():
            for index, pack in enumerate(packs):
                pltpu.make_async_copy(pack, weights_ref.at[index], sems.at[index]).wait()

    return wait


def over_pieces(hidden, first, then):
    piece = hidden // PIECES
    order = [(index, slice(at, at + piece)) for index in range(4) for at in range(0, hidden, piece)]
    made = first(*order[0])
    for here, ahead in zip(order, order[1:] + [None]):
        coming = None if ahead is None else first(*ahead)
        then(*here, made)
        made = coming


def piece_lanes(index, columns, hidden):
    return slice(index * hidden + columns.start, index * hidden + columns.stop)


def fixed(shape):
    return pl.BlockSpec(shape, lambda i, *_: (0,) * len(shape))


def encoder_forward_kernel(
    flag_ref, mixed_ref, x_ref, out_ref, vec_ref, ff0, ff1, ff2, ff3, bias_ref,
    *refs,
):
    sum1_ref, h_ref, g_ref, slope_ref, sum2_ref, memory_ref, weights_ref, sems = refs
    width = x_ref.shape[1]
    hidden = ff0.shape[1]
    is_enc = flag_ref[0] == 0
    wait = fetch_packs((ff0, ff1, ff2, ff3), weights_ref, sems, is_enc)
    stream = x_ref[...].astype(F32)
    summed = stream + (dot(mixed_ref[...], out_ref[...]) + vec_ref[0])
    sum1_ref[...] = summed
    first = normed_of(summed)[0] * vec_ref[2] + vec_ref[3]
    h_ref[...] = first.astype(BF16)
    wait()

    @pl.when(is_enc)
    def _():
        sum2_ref[...] = first + stream + vec_ref[1]

        def hidden_of(index, columns):
            return dot(h_ref[...], weights_ref[index, :width, columns]) + bias_ref[index:index + 1, columns]

        def quarter(index, columns, pre):
            value, slope = gelu_parts(pre)
            value = value.astype(BF16)
            lanes = piece_lanes(index, columns, hidden)
            g_ref[:, lanes] = value
            slope_ref[:, lanes] = slope.astype(BF16)
            below = slice(width + columns.start, width + columns.stop)
            sum2_ref[...] = sum2_ref[...] + dot(value, weights_ref[index, below, :])

        over_pieces(hidden, hidden_of, quarter)
        last = (normed_of(sum2_ref[...])[0] * vec_ref[4] + vec_ref[5]).astype(BF16)
        memory_ref[...] = last


def encoder_forward(flag, mixed, stream, out_weight, vectors, ff_packs, bias):
    rows, width = stream.shape
    hidden = 4 * ff_packs[0].shape[1]
    operands = (flag, mixed, stream, out_weight, vectors, *ff_packs, bias)
    return pl.pallas_call(
        encoder_forward_kernel,
        grid_spec=pltpu.PrefetchScalarGridSpec(
            num_scalar_prefetch=1,
            grid=(rows // TB,),
            in_specs=[tokens(width), tokens(width), fixed(out_weight.shape), fixed(vectors.shape)]
            + [anywhere()] * len(ff_packs)
            + [fixed(bias.shape)],
            out_specs=[
                tokens(width), tokens(width), tokens(hidden, 0), tokens(hidden, 0), tokens(width, 0), tokens(width, 0)
            ],
            scratch_shapes=ff_scratch(ff_packs),
        ),
        out_shape=[
            jax.ShapeDtypeStruct((rows, width), F32),
            jax.ShapeDtypeStruct((rows, width), BF16),
            jax.ShapeDtypeStruct((rows, hidden), BF16),
            jax.ShapeDtypeStruct((rows, hidden), BF16),
            jax.ShapeDtypeStruct((rows, width), F32),
            jax.ShapeDtypeStruct((rows, width), BF16),
        ],
        compiler_params=params(),
        cost_estimate=cost(2 * rows * width * (width + 2 * hidden), 20 * rows * width),
        name="encoder_forward",
    )(*operands)


def decoder_kernel(
    flag_ref, mixed_ref, sum1_ref, x_ref, cot_ref, g_in, h_in, memory_in,
    out_ref, vec_ref, cvec_ref, ff0, ff1, ff2, ff3, bias_ref,
    result_ref, g_ref, z_ref, du_ref, df_ref, dcross_ref, dmixed_ref, dh_ref, dlast_ref, vgrad_ref, bgrad_ref,
    weights_ref, sems, slope_ref, total_ref,
):
    width = x_ref.shape[1]
    hidden = ff0.shape[1]
    wait = fetch_packs((ff0, ff1, ff2, ff3), weights_ref, sems, flag_ref[0] == 1)

    @pl.when(pl.program_id(0) == 0)
    def _():
        vgrad_ref[...] = jnp.zeros(vgrad_ref.shape, F32)
        bgrad_ref[...] = jnp.zeros(bgrad_ref.shape, F32)

    @pl.when(flag_ref[0] == 0)
    def _():
        result_ref[...] = memory_in[...]
        g_ref[...] = g_in[...]
        z_ref[...] = h_in[...]

    @pl.when(flag_ref[0] == 1)
    def _():
        stream = x_ref[...].astype(F32)
        first = normed_of(sum1_ref[...])[0] * vec_ref[2] + vec_ref[3]
        mixed = mixed_ref[...]
        crossed = dot(mixed, out_ref[...]) + cvec_ref[2:3, :]
        normed_c, inverse_c = normed_of(first + crossed)
        second = normed_c * cvec_ref[3:4, :] + cvec_ref[4:5, :]
        second_low = second.astype(BF16)
        z_ref[...] = second_low
        total_ref[...] = second + stream + vec_ref[1]
        wait()

        def hidden_of(index, columns):
            return dot(z_ref[...], weights_ref[index, :width, columns]) + bias_ref[index:index + 1, columns]

        def quarter(index, columns, pre):
            value, slope = gelu_parts(pre)
            value = value.astype(BF16)
            lanes = piece_lanes(index, columns, hidden)
            g_ref[:, lanes] = value
            slope_ref[:, lanes] = slope.astype(BF16)
            below = slice(width + columns.start, width + columns.stop)
            total_ref[...] = total_ref[...] + dot(value, weights_ref[index, below, :])

        over_pieces(hidden, hidden_of, quarter)
        normed, inverse = normed_of(total_ref[...])
        result_ref[...] = (normed * vec_ref[4] + vec_ref[5]).astype(BF16)
        grad = cot_ref[...].astype(F32)
        grad_last = norm_back(grad, normed, inverse, vec_ref[4])
        dlast_ref[...] = grad_last
        grad_ffn = grad_last.astype(BF16)
        df_ref[...] = grad_ffn
        total_ref[...] = grad_last

        def value_grad_of(index, columns):
            return dot_t(df_ref[...], weights_ref[index, width + columns.start:width + columns.stop, :])

        def quarter_back(index, columns, grad_value):
            lanes = piece_lanes(index, columns, hidden)
            grad_pre = (grad_value * slope_ref[:, lanes].astype(F32)).astype(BF16)
            du_ref[:, lanes] = grad_pre
            bgrad_ref[index:index + 1, columns] += column_sum(grad_pre)
            total_ref[...] = total_ref[...] + dot_t(grad_pre, weights_ref[index, :width, columns])

        over_pieces(hidden, value_grad_of, quarter_back)
        grad_second = total_ref[...]
        grad_cross = norm_back(grad_second, normed_c, inverse_c, cvec_ref[3:4, :])
        dh_ref[...] = grad_cross
        cross_low = grad_cross.astype(BF16)
        dcross_ref[...] = cross_low
        dmixed_ref[...] = dot_t(cross_low, out_ref[...]).astype(BF16)
        vgrad_ref[1:2, :] += column_sum(grad_ffn)
        vgrad_ref[4:5, :] += column_sum(grad * normed)
        vgrad_ref[5:6, :] += column_sum(grad)
        vgrad_ref[6:7, :] += column_sum(cross_low)
        vgrad_ref[7:8, :] += column_sum(grad_second * normed_c)
        vgrad_ref[8:9, :] += column_sum(grad_second)


def decoder_step(flag, mixed, sum1, stream, cot, g_in, h_in, memory_in, out_weight, vectors, cvec, ff_packs, bias):
    rows, width = stream.shape
    hidden = g_in.shape[1]
    return pl.pallas_call(
        decoder_kernel,
        grid_spec=pltpu.PrefetchScalarGridSpec(
            num_scalar_prefetch=1,
            grid=(rows // TB,),
            in_specs=[
                tokens(width, 1), tokens(width, 1), tokens(width, 1), tokens(width, 1), tokens(hidden, 0),
                tokens(width, 0), tokens(width, 0), fixed(out_weight.shape), fixed(vectors.shape), fixed(cvec.shape),
            ]
            + [anywhere()] * len(ff_packs)
            + [fixed(bias.shape)],
            out_specs=[
                tokens(width), tokens(hidden), tokens(width), tokens(hidden, 1), tokens(width, 1), tokens(width, 1),
                tokens(width, 1), tokens(width, 1), tokens(width, 1), fixed((16, width)), fixed(bias.shape),
            ],
            scratch_shapes=ff_scratch(ff_packs) + [pltpu.VMEM((TB, hidden), BF16), pltpu.VMEM((TB, width), F32)],
        ),
        out_shape=[
            jax.ShapeDtypeStruct((rows, width), BF16),
            jax.ShapeDtypeStruct((rows, hidden), BF16),
            jax.ShapeDtypeStruct((rows, width), BF16),
            jax.ShapeDtypeStruct((rows, hidden), BF16),
            jax.ShapeDtypeStruct((rows, width), BF16),
            jax.ShapeDtypeStruct((rows, width), BF16),
            jax.ShapeDtypeStruct((rows, width), BF16),
            jax.ShapeDtypeStruct((rows, width), F32),
            jax.ShapeDtypeStruct((rows, width), F32),
            jax.ShapeDtypeStruct((16, width), F32),
            jax.ShapeDtypeStruct(bias.shape, F32),
        ],
        compiler_params=params(),
        cost_estimate=cost(2 * rows * width * (2 * width + 4 * hidden), 40 * rows * width),
        name="decoder_step",
    )(flag, mixed, sum1, stream, cot, g_in, h_in, memory_in, out_weight, vectors, cvec, *ff_packs, bias)


def backward_kernel(
    flag_ref, cot_ref, dmem_ref, sum1_ref, sum2_ref, slope_ref,
    dh_in, dq_in, dlast_in, du_in, df_in, vgrad_in, bgrad_in,
    out_ref, cross_ref, vec_ref, ff0, ff1, ff2, ff3,
    du_ref, df_ref, da_ref, dmixed_ref, dres_ref, vgrad_ref, bgrad_ref, dfirst_ref, weights_ref, sems,
):
    width = cot_ref.shape[1]
    hidden = ff0.shape[1]
    wait = fetch_packs((ff0, ff1, ff2, ff3), weights_ref, sems, flag_ref[0] == 0)
    at_start = pl.program_id(0) == 0
    is_dec = flag_ref[0] == 1

    @pl.when(at_start & is_dec)
    def _():
        vgrad_ref[...] = vgrad_in[...]
        bgrad_ref[...] = bgrad_in[...]

    @pl.when(at_start & jnp.logical_not(is_dec))
    def _():
        vgrad_ref[...] = jnp.zeros(vgrad_ref.shape, F32)
        bgrad_ref[...] = jnp.zeros(bgrad_ref.shape, F32)

    @pl.when(is_dec)
    def _():
        du_ref[...] = du_in[...]
        df_ref[...] = df_in[...]
        dres_ref[...] = dlast_in[...]
        dfirst_ref[...] = dh_in[...] + dot_t(dq_in[...], cross_ref[...])

    @pl.when(jnp.logical_not(is_dec))
    def _():
        grad = cot_ref[...].astype(F32) + dmem_ref[...].astype(F32)
        normed, inverse = normed_of(sum2_ref[...])
        grad_last = norm_back(grad, normed, inverse, vec_ref[4])
        dres_ref[...] = grad_last
        grad_ffn = grad_last.astype(BF16)
        df_ref[...] = grad_ffn
        dfirst_ref[...] = grad_last
        wait()

        def value_grad_of(index, columns):
            return dot_t(df_ref[...], weights_ref[index, width + columns.start:width + columns.stop, :])

        def quarter_back(index, columns, grad_value):
            lanes = piece_lanes(index, columns, hidden)
            grad_pre = (grad_value * slope_ref[:, lanes].astype(F32)).astype(BF16)
            du_ref[:, lanes] = grad_pre
            bgrad_ref[index:index + 1, columns] += column_sum(grad_pre)
            dfirst_ref[...] = dfirst_ref[...] + dot_t(grad_pre, weights_ref[index, :width, columns])

        over_pieces(hidden, value_grad_of, quarter_back)
        vgrad_ref[1:2, :] += column_sum(grad_ffn)
        vgrad_ref[4:5, :] += column_sum(grad * normed)
        vgrad_ref[5:6, :] += column_sum(grad)

    grad_first = dfirst_ref[...]
    normed, inverse = normed_of(sum1_ref[...])
    grad_in = norm_back(grad_first, normed, inverse, vec_ref[2])
    low = grad_in.astype(BF16)
    da_ref[...] = low
    dmixed_ref[...] = dot_t(low, out_ref[...]).astype(BF16)
    dres_ref[...] = dres_ref[...] + grad_in
    vgrad_ref[0:1, :] += column_sum(low)
    vgrad_ref[2:3, :] += column_sum(grad_first * normed)
    vgrad_ref[3:4, :] += column_sum(grad_first)


def backward_step(
    flag, cot, dmem, sum1, sum2, slope, dh, dq, dlast, du, df, vgrad, bgrad, out_weight, cross_query, vectors, ff_packs
):
    rows, width = cot.shape
    hidden = du.shape[1]
    return pl.pallas_call(
        backward_kernel,
        grid_spec=pltpu.PrefetchScalarGridSpec(
            num_scalar_prefetch=1,
            grid=(rows // TB,),
            in_specs=[
                tokens(width, 0), tokens(width, 0), tokens(width), tokens(width, 0), tokens(hidden, 0),
                tokens(width, 1), tokens(width, 1), tokens(width, 1), tokens(hidden, 1), tokens(width, 1),
                fixed(vgrad.shape), fixed(bgrad.shape),
                fixed(out_weight.shape), fixed(cross_query.shape), fixed(vectors.shape),
            ]
            + [anywhere()] * len(ff_packs),
            out_specs=[
                tokens(hidden), tokens(width), tokens(width), tokens(width), tokens(width),
                fixed(vgrad.shape), fixed(bgrad.shape),
            ],
            scratch_shapes=[pltpu.VMEM((TB, width), F32)] + ff_scratch(ff_packs),
        ),
        out_shape=[
            jax.ShapeDtypeStruct((rows, hidden), BF16),
            jax.ShapeDtypeStruct((rows, width), BF16),
            jax.ShapeDtypeStruct((rows, width), BF16),
            jax.ShapeDtypeStruct((rows, width), BF16),
            jax.ShapeDtypeStruct((rows, width), F32),
            jax.ShapeDtypeStruct(vgrad.shape, F32),
            jax.ShapeDtypeStruct(bgrad.shape, F32),
        ],
        compiler_params=params(),
        cost_estimate=cost(2 * rows * width * (width + 2 * hidden), 40 * rows * width),
        name="backward_step",
    )(
        flag, cot, dmem, sum1, sum2, slope, dh, dq, dlast, du, df, vgrad, bgrad,
        out_weight, cross_query, vectors, *ff_packs,
    )


def input_kernel(dres_ref, *refs):
    *parts, weight_ref, dx_ref = refs
    total = dres_ref[...]
    at = 0
    for part in parts:
        wide = part.shape[1]
        total = total + dot_t(part[...], weight_ref[:, at:at + wide])
        at += wide
    dx_ref[...] = total.astype(BF16)


def input_step(dres, parts, weight):
    rows, width = dres.shape
    block = 256
    spec = lambda v: pl.BlockSpec((block, v.shape[1]), lambda i: (i, 0))
    return pl.pallas_call(
        input_kernel,
        grid=(rows // block,),
        in_specs=[spec(v) for v in (dres, *parts)] + [fixed(weight.shape)],
        out_specs=spec(dres),
        out_shape=jax.ShapeDtypeStruct((rows, width), BF16),
        compiler_params=params(),
        cost_estimate=cost(6 * rows * width * width, 12 * rows * width),
        name="input_step",
    )(dres, *parts, weight)


def finish_kernel(ff_ref, attn_ref, ffin_ref, ffout_ref, qkv_ref, out_ref, bias_ref, hidden_ref, vectors_ref):
    width = ffin_ref.shape[0]
    lane = attn_ref.shape[1]
    ffin_ref[...] = ff_ref[:width, :].astype(F32)
    ffout_ref[...] = ff_ref[width:, :].astype(F32)
    for index in range(3):
        qkv_ref[index] = attn_ref[index * width:(index + 1) * width, :].astype(F32)
    for index in range(width // lane):
        at = 3 * width + index * lane
        out_ref[:, index * lane:(index + 1) * lane] = attn_ref[at:at + lane, :].astype(F32)
    rows = attn_ref[4 * width:, :].astype(F32)
    bias_ref[...] = rows[0:2]
    for index in range(hidden_ref.shape[1] // lane):
        hidden_ref[:, index * lane:(index + 1) * lane] = rows[2 + index:3 + index]
    count = width // lane
    for index in range(6):
        for part in range(count):
            row = 16 + index * count + part
            vectors_ref[index, :, part * lane:(part + 1) * lane] = rows[row:row + 1]


def finish(ff_total, attn_total):
    width, lane = ff_total.shape[1], attn_total.shape[1]
    hidden = ff_total.shape[0] - width
    shapes = [(width, hidden), (hidden, width), (3, width, lane), (lane, width), (2, lane), (1, hidden), (6, 1, width)]
    return pl.pallas_call(
        finish_kernel,
        grid=(1,),
        in_specs=[fixed(ff_total.shape), fixed(attn_total.shape)],
        out_specs=[fixed(shape) for shape in shapes],
        out_shape=[jax.ShapeDtypeStruct(shape, F32) for shape in shapes],
        compiler_params=params(),
        cost_estimate=cost(0, 20 * width * width),
        name="finish",
    )(ff_total, attn_total)


def flipped(value, bits, section=None):
    count = lax.axis_size("tensor")
    if section is None:
        return lax.ppermute(value, "tensor", [(t, t ^ bits) for t in range(count)])
    base = section * count
    return lax.ppermute(value, ("pipe", "tensor"), [(base + t, base + (t ^ bits)) for t in range(count)])


def across(value, source, active):
    count = lax.axis_size("tensor")
    other = 1 - source
    pairs = [(source * count + t, other * count + t) for t in range(active)]
    return lax.ppermute(value, ("pipe", "tensor"), pairs)


def plus(own, received):
    return (own.astype(F32) + received.astype(F32)).astype(BF16)


def along_dp(part, level, section=None):
    count = lax.axis_size("dp")
    if section is None:
        return lax.ppermute(part, "dp", [(i, i ^ (1 << level)) for i in range(count)])
    base = section * count
    return lax.ppermute(part, ("pipe", "dp"), [(base + i, base + (i ^ (1 << level))) for i in range(count)])


def summed_whole(value, level, section=None, behind=()):
    return plus(after(value, *behind), along_dp(value, level, section))


def dp_bit(level):
    return lax.shift_right_logical(lax.axis_index("dp"), level) & 1


def halved(value, level, section=None, behind=()):
    rows = value.shape[0] // 2
    mine = dp_bit(level)
    got = along_dp(lax.dynamic_slice_in_dim(value, (1 - mine) * rows, rows, 0), level, section)
    return plus(lax.dynamic_slice_in_dim(after(value, *behind), mine * rows, rows, 0), got)


def doubled(value, level, section=None, behind=()):
    other = along_dp(value, level, section)
    upper = dp_bit(level) == 1
    value = after(value, *behind)
    return jnp.concatenate([jnp.where(upper, other, value), jnp.where(upper, value, other)], 0)


def after(value, *others):
    return lax.optimization_barrier((value, *others))[0]


def to_rows(shard):
    count = lax.axis_size("tensor")
    shard = jnp.pad(shard, ((0, count - shard.shape[0]), (0, 0), (0, 0)))
    out = lax.all_to_all(shard, "tensor", 0, 0, tiled=True)
    return out.reshape(count * shard.shape[1], shard.shape[2])


def from_rows(row, row_count):
    count = lax.axis_size("tensor")
    parts = row.reshape(count, row.shape[0] // count, row.shape[1])
    return lax.all_to_all(parts, "tensor", 0, 0, tiled=True)[:row_count]


def shards(
    inputs, cotangent, segments, pads, self_qkv, self_bias, self_out, ff_in, ff_bias, ff_out, vectors,
    cross_q, cross_kv, cross_out, cross_small, cross_gain,
):
    section = lax.axis_index("pipe").astype(jnp.int32)
    place = lax.axis_index("tensor").astype(jnp.int32)
    count = lax.axis_size("tensor")
    row_count = inputs.shape[1]
    decoder = section == 1
    flag, place_flag = section[None], place[None]
    width = inputs.shape[3]
    lane = self_qkv.shape[3]
    hidden = ff_in.shape[2]
    half = width // 2
    row = jnp.minimum(place, row_count - 1)

    attn_own, cross_half = first_packs(
        jnp.transpose(self_qkv[0], (1, 0, 2)), self_out[0], self_bias[0], ff_bias, cross_q,
        jnp.transpose(cross_kv, (1, 0, 2)), cross_out, cross_small, cross_gain[None],
    )
    attn_far, attn_near = flipped(attn_own, 2), flipped(attn_own, 1)
    stream = to_rows(after(inputs[0], attn_own))
    slots = jnp.concatenate(
        [
            lax.dynamic_index_in_dim(segments, row, 1, False),
            lax.dynamic_slice_in_dim(pads[0], row, 1, 0),
        ],
        0,
    )
    attn_packs = [attn_own, attn_near, attn_far, flipped(attn_far, 1)]
    other_half = across(cross_half, 0, count)
    ff_own = after(jnp.concatenate([ff_in[0], ff_out[0]], 0), stream, attn_far)
    ff_far, ff_near = flipped(ff_own, 2), flipped(ff_own, 1)
    vector_rows = jnp.transpose(vectors, (1, 0, 2))

    qkv, qkv_weight, out_weight, hidden_bias, own_code, key_code, target_code, source_code, self_bounds, cross_bounds = (
        query_key_value(flag, stream, slots, attn_packs)
    )
    parts = ((qkv, 0), (qkv, 1), (qkv, 2))
    self_codes, cross_codes = (own_code, key_code), (target_code, source_code)
    mixed, totals = attend_forward(self_bounds, self_codes, width, *parts)
    cross_own = jnp.concatenate([after(other_half, mixed), cross_half], 0)
    cross_far, cross_near = flipped(cross_own, 2, 1), flipped(cross_own, 1, 1)
    ff_packs = [ff_own, ff_near, ff_far, flipped(after(ff_far, cross_own), 1)]
    sum1, first_low, g_enc, slope, sum2, memory = encoder_forward(
        flag, mixed, stream, out_weight, vector_rows, ff_packs, hidden_bias
    )
    memory_in = across(memory, 0, row_count)
    cross_packs = [cross_own, cross_near, cross_far, flipped(after(cross_far, memory), 1, 1)]
    cot_row = to_rows(after(cotangent[0], memory))

    cross_query, cross_pair, cross_out_weight, cvec = cross_unpack(place_flag, cross_packs)
    cross_made = cross_project(first_low, memory_in, cross_query, cross_pair, cvec)
    cross_parts = ((cross_made, 0), (cross_made, 1), (cross_made, 2))
    cross_mixed, cross_totals = attend_forward(cross_bounds, cross_codes, width, *cross_parts)
    result, g_all, z_all, du_dec, df_dec, dcross, dcross_mixed, dh_dec, dlast_dec, vgrad_dec, bgrad_dec = decoder_step(
        flag, cross_mixed, sum1, stream, cot_row, g_enc, first_low, memory,
        cross_out_weight, vector_rows, cvec, ff_packs, hidden_bias,
    )
    dq_cross, dk_cross, dv_cross, dmemory = attend_backward(
        cross_bounds, cross_codes, *cross_parts, dcross_mixed, cross_totals, cross_pair
    )
    dmemory_in = across(dmemory, 1, row_count)
    cross_grads = attention_grads(
        True, place_flag, first_low, memory_in, (after(dq_cross, dmemory), dk_cross, dv_cross), cross_mixed, dcross,
        vgrad_dec, bgrad_dec, lane,
    )
    cross_far = plus(after(cross_grads[2], dmemory_in), flipped(cross_grads[3], 1, 1))
    cross_got = flipped(cross_grads[1], 1, 1)

    du_all, df_all, da, dmixed, dres, vgrad, bgrad = backward_step(
        flag, cot_row, dmemory_in, sum1, sum2, slope, dh_dec, after(dq_cross, cross_far, cross_grads[1]), dlast_dec,
        du_dec, df_dec, vgrad_dec, bgrad_dec, out_weight, cross_query, vector_rows, ff_packs,
    )
    cross_near = plus(after(cross_grads[0], da), cross_got)
    cross_part = plus(cross_near, flipped(cross_far, 2, 1))
    levels = range(lax.axis_size("dp").bit_length() - 1)
    ff_third, ff_second = feed_forward_grads(after(z_all, cross_part), du_all, g_all, df_all, 3, hidden)
    ff_first, ff_zeroth = feed_forward_grads(after(z_all, ff_second), du_all, g_all, df_all, 1, hidden)
    ff_far = plus(after(ff_second, ff_zeroth), flipped(ff_third, 1))
    ff_near = plus(after(ff_zeroth, ff_far), flipped(ff_first, 1))
    dqkv = attend_backward(self_bounds, self_codes, *parts, after(dmixed, ff_near), totals)
    cross_total = halved(cross_part, 0, 1, (dqkv[0],))
    ff_part = plus(after(ff_near, dqkv[0], cross_total), flipped(ff_far, 2))
    attn_grads = attention_grads(
        False, place_flag, stream, stream, (after(dqkv[0], ff_part), *dqkv[1:]), mixed, da, vgrad, bgrad, lane
    )
    ff_total = halved(ff_part, 0, behind=(attn_grads[3],))
    for level in levels[1:]:
        cross_total = halved(cross_total, level, 1, (ff_total,))
    attn_far = plus(after(attn_grads[2], ff_total, cross_total), flipped(attn_grads[3], 1))
    attn_near = plus(after(attn_grads[0], attn_far), flipped(attn_grads[1], 1))
    dx = input_step(after(dres, attn_near), dqkv, qkv_weight)
    section_out = from_rows(after(result, dx), row_count)[None]
    for level in levels[1:]:
        ff_total = halved(ff_total, level, behind=(dx,))
    cross_total = doubled(cross_total, levels[-1], 1, (ff_total,))
    attn_part = plus(after(attn_near, ff_total, cross_total), flipped(attn_far, 2))
    ff_total = doubled(ff_total, levels[-1], behind=(attn_part, section_out))
    attn_total = halved(attn_part, 0, behind=(ff_total,))
    for level in reversed(levels[:-1]):
        cross_total = doubled(cross_total, level, 1, (attn_total,))
    cross_other = across(cross_total, 1, count)
    input_grad = from_rows(after(dx, attn_total), row_count).astype(F32)[None]
    for level in levels[1:]:
        attn_total = halved(attn_total, level, behind=(cross_total,))
    for level in reversed(levels[:-1]):
        ff_total = doubled(ff_total, level, behind=(attn_total,))
    attn_total = doubled(attn_total, levels[-1], behind=(ff_total, input_grad))
    cross_total, cross_other = after((cross_total, cross_other), attn_total)

    own, other = cross_total.astype(F32), cross_other.astype(F32)

    def halves(at):
        return jnp.where(decoder, own[at + half:at + 2 * half], other[at:at + half])

    cross_pair_grad = jnp.stack([halves(width), halves(2 * width)], 1)
    cross_out_grad = jnp.transpose(halves(3 * width).reshape(half // lane, lane, lane), (1, 0, 2)).reshape(lane, half)
    own_rows, other_rows = (v[4 * width:4 * width + 5 * count].reshape(5, width) for v in (own, other))
    small_grad = jnp.where(decoder, jnp.stack([own_rows[2], own_rows[4]]), other_rows[:2])
    gain_grad = jnp.where(decoder, own_rows[3, half:], other_rows[3, :half])
    cross_first, cross_last = halves(0), (cross_pair_grad, cross_out_grad, small_grad, gain_grad)
    for level in reversed(levels[:-1]):
        attn_total = doubled(attn_total, level, behind=(cross_first, *cross_last))
    ffin_grad, ffout_grad, qkv_grad, out_grad, bias_grad, hidden_grad, vectors_grad = finish(
        ff_total, attn_total
    )
    return (
        section_out,
        input_grad,
        jnp.transpose(qkv_grad, (1, 0, 2))[None],
        bias_grad[None],
        out_grad[None],
        ffin_grad[None],
        hidden_grad,
        ffout_grad[None],
        jnp.transpose(vectors_grad, (1, 0, 2)),
        cross_first,
        *cross_last,
    )


def solution(mesh):
    token_spec = P("pipe", "dp", "tensor", None)
    weights = (
        P("pipe", None, None, "tensor"),
        P("pipe", None, "tensor"),
        P("pipe", "tensor", None),
        P("pipe", None, "tensor"),
        P("pipe", "tensor"),
        P("pipe", "tensor", None),
        P("pipe", None, None),
        P("pipe", "tensor"),
        P("pipe", None, "tensor"),
        P("tensor", "pipe"),
        P("pipe", None),
        P("pipe"),
    )
    return jax.shard_map(
        shards,
        mesh=mesh,
        in_specs=(token_spec, token_spec, P(None, "dp", None), P("pipe", "dp", None)) + weights,
        out_specs=(token_spec, token_spec) + weights,
        check_vma=False,
    )
```

```python
import functools

import jax
import jax.numpy as jnp
from jax import lax
from jax.experimental import pallas as pl
from jax.experimental.pallas import tpu as pltpu
from jax.sharding import PartitionSpec as P

HEAD_DIM = 64
EPSILON = 1e-05
MASKED = -1e30
SEGS = 8
QF = 256
QB = 256
TB = 512
PIECES = 1
PAIR = 2 * HEAD_DIM
GELU_C = 0.7978845608028654
GELU_A = 0.044715
VMEM_LIMIT = 56 * 1024 * 1024
F32 = jnp.float32
BF16 = jnp.bfloat16


def dot(left, right):
    return jnp.dot(left, right, preferred_element_type=F32)


def dot_t(left, right):
    return lax.dot_general(left, right, (((1,), (1,)), ((), ())), preferred_element_type=F32)


def dot_tl(left, right):
    return lax.dot_general(left, right, (((0,), (0,)), ((), ())), preferred_element_type=F32)


def normed_of(values):
    center = values - jnp.mean(values, -1, keepdims=True)
    inverse = lax.rsqrt(jnp.mean(center * center, -1, keepdims=True) + EPSILON)
    return center * inverse, inverse


def norm_back(grad, normed, inverse, gain):
    scaled = grad * gain
    mean_scaled = jnp.mean(scaled, -1, keepdims=True)
    mean_both = jnp.mean(scaled * normed, -1, keepdims=True)
    return (scaled - mean_scaled - normed * mean_both) * inverse


def column_sum(values):
    return jnp.sum(values.astype(F32), 0, keepdims=True)


def gelu_parts(pre):
    squared = pre * pre
    half = 0.5 * jnp.tanh(pre * (GELU_C + (GELU_C * GELU_A) * squared)) + 0.5
    slope = half + (pre * (half - half * half)) * (2.0 * GELU_C + (6.0 * GELU_C * GELU_A) * squared)
    return pre * half, slope


def cost(flops, moved):
    return pl.CostEstimate(flops=int(flops) // 64, bytes_accessed=int(moved) // 64, transcendentals=0)


def params(axes=1):
    return pltpu.CompilerParams(
        dimension_semantics=("arbitrary",) * axes, vmem_limit_bytes=VMEM_LIMIT
    )


def find_segments(section, slots_ref, own_ref, key_ref, target_ref, source_ref, self_ref, cross_ref):
    length = slots_ref.shape[1]
    source = slots_ref[0:1, :].astype(F32)
    target = slots_ref[1:2, :].astype(F32)
    own = jnp.where(section == 1, target, source)
    own_ref[...] = own
    key_ref[...] = jnp.where(slots_ref[2:3, :] == 0, own, -1.0)
    target_ref[...] = target
    source_ref[...] = source

    def starts(segments):
        found = [jnp.int32(0)]
        for index in range(1, SEGS):
            found.append(jnp.sum(jnp.where(segments < float(index), 1.0, 0.0)).astype(jnp.int32))
        return found + [jnp.int32(length)]

    source_starts, target_starts = starts(source), starts(target)
    for index in range(SEGS):
        own_start = jnp.where(section == 1, target_starts[index], source_starts[index])
        own_end = jnp.where(section == 1, target_starts[index + 1], source_starts[index + 1])
        self_ref[index] = own_start
        self_ref[16 + index] = own_start
        self_ref[32 + index] = own_end
        cross_ref[index] = target_starts[index]
        cross_ref[16 + index] = source_starts[index]
        cross_ref[32 + index] = source_starts[index + 1]
    self_ref[48] = jnp.int32(1)
    self_ref[49] = section
    self_ref[50] = jnp.int32(1)
    cross_ref[48] = jnp.int32(0)
    cross_ref[49] = jnp.int32(0)
    cross_ref[50] = section


def half_masked(values, side):
    lane = lax.broadcasted_iota(jnp.int32, values.shape, 1)
    return jnp.where((lane >= HEAD_DIM) == bool(side), values, jnp.zeros_like(values))


def key_window(bounds, block, block_rows):
    first = block * block_rows
    last = first + (block_rows - 1)
    low, high = jnp.int32(0), jnp.int32(0)
    for index in range(SEGS):
        low = jnp.where(bounds[index] <= first, bounds[16 + index], low)
        high = jnp.where(bounds[index] <= last, bounds[32 + index], high)
    high = jnp.where(bounds[49] == 1, jnp.minimum(high, last + 1), high)
    low_block = lax.shift_right_logical(low, 7)
    high_block = lax.shift_right_logical(high + 127, 7)
    return low_block, jnp.where(bounds[50] == 1, high_block - low_block, 0)


def by_size(bounds, block, block_rows, key_blocks, sizes, body):
    low_block, needed = key_window(bounds, block, block_rows)
    below = 0
    for size in sizes:
        size = min(size, key_blocks)
        if size == below:
            continue

        @pl.when((needed > below) & (needed <= size))
        def _(size=size):
            start = jnp.minimum(low_block, key_blocks - size) * 128
            body(size, pl.multiple_of(start, 128))

        below = size


def as_columns(row):
    parts = []
    for at in range(0, row.shape[1], 128):
        parts.append(jnp.broadcast_to(row[:, at:at + 128], (128, 128)).T)
    return jnp.concatenate(parts, 0)


def window_bias(bounds, block, block_rows, start, key_code, qcode_ref):
    key_at = start + lax.broadcasted_iota(jnp.int32, key_code.shape, 0)
    tiles = []
    for at in range(0, block_rows, 128):
        query_at = block * block_rows + at + lax.broadcasted_iota(jnp.int32, (1, 128), 1)
        limit = jnp.where(bounds[49] == 1, query_at, jnp.int32(1 << 30))
        same_at = jnp.where(bounds[48] == 1, query_at, -1)
        opened = (key_code == qcode_ref[:, at:at + 128]) & (key_at <= limit)
        tiles.append(jnp.where(opened | (key_at == same_at), 0.0, MASKED))
    return jnp.concatenate(tiles, 1)


def attend_forward_kernel(bounds, q_ref, k_ref, v_ref, qcode_ref, kcode_ref, mixed_ref, total_ref):
    block = pl.program_id(0)
    heads = q_ref.shape[1] // HEAD_DIM
    key_blocks = k_ref.shape[0] // 128
    own_code = as_columns(qcode_ref[...])
    query_at = block * QF + lax.broadcasted_iota(jnp.int32, (QF, 128), 0)
    limit = jnp.where(bounds[49] == 1, query_at, jnp.int32(1 << 30))
    same_at = jnp.where(bounds[48] == 1, query_at, -1)
    lane = lax.broadcasted_iota(jnp.int32, (QF, 128), 1)

    def body(size, start):
        window = pl.ds(start, size * 128)
        tiles = []
        for tile in range(size):
            at = start + tile * 128
            key_at = at + lane
            opened = (own_code == kcode_ref[:, pl.ds(pl.multiple_of(at, 128), 128)]) & (key_at <= limit)
            tiles.append(jnp.where(opened | (key_at == same_at), 0.0, MASKED))
        bias = jnp.concatenate(tiles, 1)

        def two_pairs(index, columns):
            lanes = [pl.ds(pl.multiple_of((2 * index + at) * PAIR, PAIR), PAIR) for at in range(2)]
            scores = []
            for at in range(2):
                queries, keys = q_ref[:, lanes[at]], k_ref[window, lanes[at]]
                scores.append([dot_t(half_masked(queries, side), keys) + bias for side in range(2)])
            for at in range(2):
                values = v_ref[window, lanes[at]]
                out = None
                for side in range(2):
                    top = jnp.max(scores[at][side], -1, keepdims=True)
                    weights = jnp.exp(scores[at][side] - top)
                    total = jnp.sum(weights, -1, keepdims=True)
                    part = dot(weights.astype(BF16), half_masked(values, side)) * (1.0 / total)
                    out = part if out is None else out + part
                    columns = jnp.where(lane == (2 * index + at) * 2 + side, top + jnp.log(total), columns)
                mixed_ref[:, lanes[at]] = out.astype(BF16)
            return columns

        columns = lax.fori_loop(0, heads // 4, two_pairs, jnp.zeros((QF, 128), F32))
        total_ref[...] = columns.T[:heads]

    by_size(bounds, block, QF, key_blocks, (2, 3, 4, 5, 6, 8), body)


def attend_forward(bounds, codes, width, queries, keys, values):
    (q_array, q_at), (k_array, k_at), (v_array, v_at) = queries, keys, values
    rows = q_array.shape[0]
    heads = width // HEAD_DIM
    whole = lambda at: (lambda i, *_: (0, at))
    return pl.pallas_call(
        attend_forward_kernel,
        grid_spec=pltpu.PrefetchScalarGridSpec(
            num_scalar_prefetch=1,
            grid=(rows // QF,),
            in_specs=[
                pl.BlockSpec((QF, width), lambda i, *_: (i, q_at)),
                pl.BlockSpec((rows, width), whole(k_at)),
                pl.BlockSpec((rows, width), whole(v_at)),
                pl.BlockSpec((1, QF), lambda i, *_: (0, i)),
                pl.BlockSpec((1, rows), whole(0)),
            ],
            out_specs=[
                pl.BlockSpec((QF, width), lambda i, *_: (i, 0)),
                pl.BlockSpec((heads, QF), lambda i, *_: (0, i)),
            ],
        ),
        out_shape=[
            jax.ShapeDtypeStruct((rows, width), BF16),
            jax.ShapeDtypeStruct((heads, rows), F32),
        ],
        compiler_params=params(),
        cost_estimate=cost(4 * rows * 512 * width * 2, 8 * rows * width),
        name="attend_forward",
    )(bounds, q_array, k_array, v_array, *codes)


def attend_backward_kernel(has_weight, first_head, bounds, q_ref, k_ref, v_ref, grad_ref, total_ref, qcode_ref, kcode_ref, *refs):
    if has_weight:
        weight_ref, dq_ref, dk_ref, dv_ref, dmem_ref, kcol_ref, dkacc_ref, dvacc_ref = refs
    else:
        dq_ref, dk_ref, dv_ref, kcol_ref, dkacc_ref, dvacc_ref = refs
    block = pl.program_id(0)
    width = q_ref.shape[1]
    heads = width // HEAD_DIM
    key_blocks = k_ref.shape[0] // 128

    @pl.when(block == 0)
    def _():
        dkacc_ref[...] = jnp.zeros(dkacc_ref.shape, F32)
        dvacc_ref[...] = jnp.zeros(dvacc_ref.shape, F32)
        kcol_ref[...] = as_columns(kcode_ref[...])

    def body(size, start):
        window = pl.ds(start, size * 128)
        bias = window_bias(bounds, block, QB, start, kcol_ref[window, :], qcode_ref)

        def two_pairs(index, carry):
            prepared = []
            for at in range(2):
                pair = 2 * index + at
                lanes = pl.ds(pl.multiple_of(pair * PAIR, PAIR), PAIR)
                queries, grads = q_ref[:, lanes], grad_ref[:, lanes]
                keys, values = k_ref[window, lanes], v_ref[window, lanes]
                query_halves = [half_masked(queries, side) for side in range(2)]
                grad_halves = [half_masked(grads, side) for side in range(2)]
                products = [
                    (dot_t(keys, query_halves[side]) + bias, dot_t(values, grad_halves[side])) for side in range(2)
                ]
                prepared.append((pair, lanes, keys, query_halves, grad_halves, products))
            for pair, lanes, keys, query_halves, grad_halves, products in prepared:
                dq = dk = dv = None
                for side in range(2):
                    scores, grad_weights = products[side]
                    weights = jnp.exp(scores - total_ref[pl.ds(first_head + pair * 2 + side, 1), :])
                    delta = jnp.sum(weights * grad_weights, 0, keepdims=True)
                    grad_scores = (weights * (grad_weights - delta)).astype(BF16)
                    made = (
                        dot_tl(grad_scores, half_masked(keys, side)),
                        dot(grad_scores, query_halves[side]),
                        dot(weights.astype(BF16), grad_halves[side]),
                    )
                    dq, dk, dv = made if dq is None else (dq + made[0], dk + made[1], dv + made[2])
                dkacc_ref[window, lanes] = dkacc_ref[window, lanes] + dk
                dvacc_ref[window, lanes] = dvacc_ref[window, lanes] + dv
                dq_ref[:, lanes] = (dq * HEAD_DIM ** (-0.5)).astype(BF16)
            return carry

        lax.fori_loop(0, heads // 4, two_pairs, 0)

    by_size(bounds, block, QB, key_blocks, (2, 3, 4, 5, 6, 8), body)

    @pl.when(block == pl.num_programs(0) - 1)
    def _():
        dk_ref[...] = dkacc_ref[...].astype(BF16)
        dv_ref[...] = dvacc_ref[...].astype(BF16)
        if has_weight:
            summed = dot_t(dk_ref[...], weight_ref[:, :width]) + dot_t(dv_ref[...], weight_ref[:, width:])
            dmem_ref[...] = summed.astype(BF16)


def attend_backward(bounds, codes, queries, keys, values, grad, totals, weight=None, part=(0, 1)):
    (q_array, q_at), (k_array, k_at), (v_array, v_at) = queries, keys, values
    index, count = part
    rows = grad.shape[0]
    heads = totals.shape[0]
    width = grad.shape[1] // count
    whole = lambda at: pl.BlockSpec((rows, width), lambda i, *_: (0, at * count + index))
    block = lambda at: pl.BlockSpec((QB, width), lambda i, *_: (i, at * count + index))
    extra = [] if weight is None else [weight]
    first = pl.BlockSpec((rows, width), lambda i, *_: (0, 0))
    return pl.pallas_call(
        functools.partial(attend_backward_kernel, weight is not None, index * heads // count),
        grid_spec=pltpu.PrefetchScalarGridSpec(
            num_scalar_prefetch=1,
            grid=(rows // QB,),
            in_specs=[
                block(q_at),
                whole(k_at),
                whole(v_at),
                block(0),
                pl.BlockSpec((heads, QB), lambda i, *_: (0, i)),
                pl.BlockSpec((1, QB), lambda i, *_: (0, i)),
                pl.BlockSpec((1, rows), lambda i, *_: (0, 0)),
            ]
            + [fixed(v.shape) for v in extra],
            out_specs=[pl.BlockSpec((QB, width), lambda i, *_: (i, 0))] + [first] * (2 + len(extra)),
            scratch_shapes=[
                pltpu.VMEM((rows, 128), F32),
                pltpu.VMEM((rows, width), F32),
                pltpu.VMEM((rows, width), F32),
            ],
        ),
        out_shape=[jax.ShapeDtypeStruct((rows, width), BF16)] * (3 + len(extra)),
        compiler_params=params(),
        cost_estimate=cost(10 * rows * 512 * width * 2, 16 * rows * width),
        name="attend_backward",
    )(bounds, q_array, k_array, v_array, grad, totals, *codes, *extra)


def first_packs_kernel(
    qkv_ref, out_ref, bias_ref, ffb_ref, query_ref, pair_ref, cout_ref, small_ref, gain_ref, pack_ref, half_ref
):
    width = qkv_ref.shape[1]
    lane = qkv_ref.shape[2]
    half = query_ref.shape[0]

    def columns(values):
        return [values[:, at:at + lane] for at in range(0, values.shape[1], lane)]

    def filled(rows):
        rest = jnp.zeros((16 - sum(part.shape[0] for part in rows), lane), F32)
        return jnp.concatenate([*rows, rest], 0).astype(BF16)

    for index in range(3):
        pack_ref[index * width:(index + 1) * width, :] = qkv_ref[index]
    for index, part in enumerate(columns(out_ref[...])):
        at = 3 * width + index * lane
        pack_ref[at:at + lane, :] = part
    bias = bias_ref[...]
    high = bias.astype(BF16).astype(F32)
    middle = (bias - high).astype(BF16).astype(F32)
    least = bias - high - middle
    pack_ref[4 * width:4 * width + 16, :] = filled([high, middle, least, *columns(ffb_ref[...].astype(F32))])
    half_ref[0:half, :] = query_ref[...]
    half_ref[half:2 * half, :] = pair_ref[0]
    half_ref[2 * half:3 * half, :] = pair_ref[1]
    for index, part in enumerate(columns(cout_ref[...])):
        at = 3 * half + index * lane
        half_ref[at:at + lane, :] = part
    small = small_ref[...].astype(F32)
    half_ref[4 * half:4 * half + 16, :] = filled(
        [*columns(small[0:1]), *columns(small[1:2]), *columns(gain_ref[...].astype(F32))]
    )


def first_packs(qkv, out_weight, bias, ff_bias, query, pair, cross_out, small, gain):
    width, lane = qkv.shape[1:]
    half = query.shape[0]
    operands = (qkv, out_weight, bias, ff_bias, query, pair, cross_out, small, gain)
    shapes = [(4 * width + 16, lane), (4 * half + 16, lane)]
    return pl.pallas_call(
        first_packs_kernel,
        grid=(1,),
        in_specs=[fixed(v.shape) for v in operands],
        out_specs=[fixed(shape) for shape in shapes],
        out_shape=[jax.ShapeDtypeStruct(shape, BF16) for shape in shapes],
        compiler_params=params(),
        cost_estimate=cost(0, 24 * width * lane),
        name="first_packs",
    )(*operands)


def query_key_value_kernel(
    flag_ref, x_ref, slots_ref, p0, p1, p2, p3, qkv_ref, weight_ref, out_ref, hidden_ref, *refs
):
    *found_refs, bias_ref = refs
    width = x_ref.shape[1]
    lane = p0.shape[1]

    @pl.when(pl.program_id(0) == 0)
    def _():
        find_segments(flag_ref[0], slots_ref, *found_refs)
        for index, pack in enumerate((p0, p1, p2, p3)):
            columns = slice(index * lane, (index + 1) * lane)
            for part in range(3):
                at = slice(part * width + index * lane, part * width + (index + 1) * lane)
                weight_ref[:, at] = pack[part * width:(part + 1) * width, :]
            for part in range(width // lane):
                at = 3 * width + part * lane
                out_ref[columns, part * lane:(part + 1) * lane] = pack[at:at + lane, :]
            rows = pack[4 * width:4 * width + 16, :].astype(F32)
            bias_ref[0:1, columns] = rows[0:1] + rows[2:3] + rows[4:5]
            bias_ref[1:2, columns] = rows[1:2] + rows[3:4] + rows[5:6]
            for part in range(width // lane):
                hidden_ref[index:index + 1, part * lane:(part + 1) * lane] = rows[6 + part:7 + part]

    made = dot(x_ref[...], weight_ref[...])
    scale = HEAD_DIM ** (-0.5)
    queries = (made[:, :width] + bias_ref[0:1, :]).astype(BF16).astype(F32) * scale
    qkv_ref[:, :width] = queries.astype(BF16)
    qkv_ref[:, width:2 * width] = made[:, width:2 * width].astype(BF16)
    qkv_ref[:, 2 * width:] = (made[:, 2 * width:] + bias_ref[1:2, :]).astype(BF16)


def query_key_value(flag, stream, slots, packs):
    rows, width = stream.shape
    line = jax.ShapeDtypeStruct((1, rows), F32)
    bounds = jax.ShapeDtypeStruct((64,), jnp.int32)
    return pl.pallas_call(
        query_key_value_kernel,
        grid_spec=pltpu.PrefetchScalarGridSpec(
            num_scalar_prefetch=1,
            grid=(rows // TB,),
            in_specs=[tokens(width), fixed(slots.shape)] + [fixed(pack.shape) for pack in packs],
            out_specs=[tokens(3 * width), fixed((width, 3 * width)), fixed((width, width)), fixed((len(packs), width))]
            + [fixed(line.shape)] * 4
            + [pl.BlockSpec(memory_space=pltpu.SMEM)] * 2,
            scratch_shapes=[pltpu.VMEM((8, width), F32)],
        ),
        out_shape=[
            jax.ShapeDtypeStruct((rows, 3 * width), BF16),
            jax.ShapeDtypeStruct((width, 3 * width), BF16),
            jax.ShapeDtypeStruct((width, width), BF16),
            jax.ShapeDtypeStruct((len(packs), width), F32),
        ]
        + [line] * 4
        + [bounds] * 2,
        compiler_params=params(),
        cost_estimate=cost(6 * rows * width * width, 10 * rows * width),
        name="query_key_value",
    )(flag, stream, slots, *packs)


def cross_project_kernel(h_ref, memory_ref, query_ref, pair_ref, cvec_ref, made_ref):
    width = h_ref.shape[1]
    queries = (dot(h_ref[...], query_ref[...]) + cvec_ref[0:1, :]).astype(BF16).astype(F32)
    made_ref[:, :width] = (queries * HEAD_DIM ** (-0.5)).astype(BF16)
    made = dot(memory_ref[...], pair_ref[...])
    made_ref[:, width:2 * width] = made[:, :width].astype(BF16)
    made_ref[:, 2 * width:] = (made[:, width:] + cvec_ref[1:2, :]).astype(BF16)


def cross_project(h, memory, query, pair, cvec):
    rows, width = h.shape
    operands = (h, memory, query, pair, cvec)
    return pl.pallas_call(
        cross_project_kernel,
        grid=(rows // TB,),
        in_specs=[tokens(width)] * 2 + [fixed(v.shape) for v in operands[2:]],
        out_specs=tokens(3 * width),
        out_shape=jax.ShapeDtypeStruct((rows, 3 * width), BF16),
        compiler_params=params(),
        cost_estimate=cost(6 * rows * width * width, 12 * rows * width),
        name="cross_project",
    )(*operands)


def cross_unpack_kernel(place_ref, p0, p1, p2, p3, query_ref, pair_ref, out_ref, cvec_ref):
    lane = p0.shape[1]
    length = p0.shape[0] // 2
    half = (length - 16) // 4
    width = 2 * half
    count = width // lane
    for index, pack in enumerate((p0, p1, p2, p3)):
        columns = slice(index * lane, (index + 1) * lane)
        for side in range(2):
            rows = slice(side * half, (side + 1) * half)
            base = side * length
            query_ref[rows, columns] = pack[base:base + half, :]
            pair_ref[rows, columns] = pack[base + half:base + 2 * half, :]
            pair_ref[rows, width + index * lane:width + (index + 1) * lane] = pack[base + 2 * half:base + 3 * half, :]
            for part in range(half // lane):
                at = base + 3 * half + part * lane
                to = side * half + part * lane
                out_ref[columns, to:to + lane] = pack[at:at + lane, :]
    first = p0[4 * half:4 * half + 16, :].astype(F32)
    second = p0[length + 4 * half:length + 4 * half + 16, :].astype(F32)
    at_row = lax.broadcasted_iota(jnp.int32, (16, lane), 0)
    for index in range(count):
        columns = slice(index * lane, (index + 1) * lane)
        for which in range(2):
            wanted = which * count + (place_ref[0] ^ index)
            cvec_ref[which:which + 1, columns] = jnp.sum(jnp.where(at_row == wanted, first, 0.0), 0, keepdims=True)
        cvec_ref[2:3, columns] = second[index:index + 1]
        cvec_ref[4:5, columns] = second[count + index:count + index + 1]
        side, part = (first, index) if index < count // 2 else (second, index - count // 2)
        cvec_ref[3:4, columns] = side[2 * count + part:2 * count + part + 1]
    cvec_ref[5:8, :] = jnp.zeros((3, width), F32)


def cross_unpack(place, packs):
    length, lane = packs[0].shape
    width = (length // 2 - 16) // 2
    return pl.pallas_call(
        cross_unpack_kernel,
        grid_spec=pltpu.PrefetchScalarGridSpec(
            num_scalar_prefetch=1,
            grid=(1,),
            in_specs=[fixed(pack.shape) for pack in packs],
            out_specs=[fixed((width, width)), fixed((width, 2 * width)), fixed((width, width)), fixed((8, width))],
        ),
        out_shape=[
            jax.ShapeDtypeStruct((width, width), BF16),
            jax.ShapeDtypeStruct((width, 2 * width), BF16),
            jax.ShapeDtypeStruct((width, width), BF16),
            jax.ShapeDtypeStruct((8, width), F32),
        ],
        compiler_params=params(),
        cost_estimate=cost(0, 16 * width * width),
        name="cross_unpack",
    )(place, *packs)


def rows_of(vector, rows, at_row, base, order=None):
    lane = rows.shape[1]
    for index in range(vector.shape[1] // lane):
        to = base + (index if order is None else (order ^ index))
        rows = rows + jnp.where(at_row == to, vector[:, index * lane:(index + 1) * lane], 0.0)
    return rows


def attention_grads_kernel(
    is_cross, parts, place_ref, aq_ref, akv_ref, *refs
):
    width = aq_ref.shape[1]
    dq_refs, dk_refs, dv_refs = (refs[part * parts:(part + 1) * parts] for part in range(3))
    mixed_ref, da_ref, vgrad_ref, bgrad_ref, *packs, made_ref = refs[3 * parts:]
    lane = packs[0].shape[1]
    count = width // lane
    tail = packs[0].shape[0] - 4 * width
    akv = akv_ref if is_cross else aq_ref
    for part, (left, rights) in enumerate(((aq_ref, dq_refs), (akv, dk_refs), (akv, dv_refs))):
        for index, right in enumerate(rights):
            wide = width // parts
            made_ref[:, index * wide:(index + 1) * wide] = dot_tl(left[...], right[...]).astype(BF16)
        for index, pack in enumerate(packs):
            pack[part * width:(part + 1) * width, :] = made_ref[:, index * lane:(index + 1) * lane]
    made_ref[...] = dot_tl(mixed_ref[...], da_ref[...]).astype(BF16)
    for index, pack in enumerate(packs):
        for part in range(count):
            at = 3 * width + part * lane
            pack[at:at + lane, :] = made_ref[index * lane:(index + 1) * lane, part * lane:(part + 1) * lane]
    query_bias, value_bias = (
        jnp.concatenate([column_sum(ref[...]) for ref in some], 1) for some in (dq_refs, dv_refs)
    )
    at_row = lax.broadcasted_iota(jnp.int32, (tail, lane), 0)
    rows = jnp.zeros((tail, lane), F32)
    if is_cross:
        rows = rows_of(query_bias, rows, at_row, 0, place_ref[0])
        rows = rows_of(value_bias, rows, at_row, count, place_ref[0])
        for index in range(3):
            rows = rows_of(vgrad_ref[6 + index:7 + index, :], rows, at_row, (2 + index) * count)
    else:
        for index in range(6):
            rows = rows_of(vgrad_ref[index:index + 1, :], rows, at_row, 16 + index * count)
    for index, pack in enumerate(packs):
        own = rows
        if not is_cross:
            columns = slice(index * lane, (index + 1) * lane)
            own = own + jnp.where(at_row == 0, query_bias[:, columns], 0.0)
            own = own + jnp.where(at_row == 1, value_bias[:, columns], 0.0)
            own = rows_of(bgrad_ref[index:index + 1, :], own, at_row, 2)
        pack[4 * width:, :] = own.astype(BF16)


def attention_grads(is_cross, place, aq, akv, dqkv, mixed, da, vgrad, bgrad, lane):
    rows, width = aq.shape
    length = 4 * width + 64
    operands = (aq, akv, *dqkv, mixed, da, vgrad, bgrad)
    count = width // lane
    return pl.pallas_call(
        functools.partial(attention_grads_kernel, is_cross, len(dqkv) // 3),
        grid_spec=pltpu.PrefetchScalarGridSpec(
            num_scalar_prefetch=1,
            grid=(1,),
            in_specs=[fixed(v.shape) for v in operands],
            out_specs=[fixed((length, lane))] * count,
            scratch_shapes=[pltpu.VMEM((width, width), BF16)],
        ),
        out_shape=[jax.ShapeDtypeStruct((length, lane), BF16)] * count,
        compiler_params=params(),
        cost_estimate=cost(8 * rows * width * width, 14 * rows * width),
        name="cross_grads" if is_cross else "self_grads",
    )(place, *operands)


def feed_forward_grads_kernel(z_ref, du_ref, g_ref, df_ref, *packs):
    width = z_ref.shape[1]
    for index, pack in enumerate(packs):

        @pl.when(pl.program_id(0) == index)
        def _(pack=pack):
            pack[:width, :] = dot_tl(z_ref[...], du_ref[...]).astype(BF16)
            pack[width:, :] = dot_tl(g_ref[...], df_ref[...]).astype(BF16)


def feed_forward_grads(z, du, g, df, first, hidden):
    rows, width = z.shape
    quarter = pl.BlockSpec((rows, hidden), lambda i: (0, first - i))
    pack = (width + hidden, width)
    return pl.pallas_call(
        feed_forward_grads_kernel,
        grid=(2,),
        in_specs=[fixed(z.shape), quarter, quarter, fixed(df.shape)],
        out_specs=[fixed(pack)] * 2,
        out_shape=[jax.ShapeDtypeStruct(pack, BF16)] * 2,
        compiler_params=params(),
        cost_estimate=cost(8 * rows * width * hidden, 12 * rows * hidden),
        name="feed_forward_grads",
    )(z, du, g, df)


def tokens(width, section=None):
    if section is None:
        return pl.BlockSpec((TB, width), lambda i, *_: (i, 0))
    if section == 0:
        return pl.BlockSpec((TB, width), lambda i, flag: (i * (1 - flag[0]), 0))
    return pl.BlockSpec((TB, width), lambda i, flag: (i * flag[0], 0))


def anywhere():
    return pl.BlockSpec(memory_space=pl.ANY)


def ff_scratch(ff_packs):
    return [
        pltpu.VMEM((len(ff_packs),) + ff_packs[0].shape, BF16),
        pltpu.SemaphoreType.DMA((len(ff_packs),)),
    ]


def fetch_packs(packs, weights_ref, sems, wanted):
    started = (pl.program_id(0) == 0) & wanted

    @pl.when(started)
    def _():
        for index, pack in enumerate(packs):
            pltpu.make_async_copy(pack, weights_ref.at[index], sems.at[index]).start()

    def wait():
        @pl.when(started)
        def _():
            for index, pack in enumerate(packs):
                pltpu.make_async_copy(pack, weights_ref.at[index], sems.at[index]).wait()

    return wait


def over_pieces(hidden, first, then):
    piece = hidden // PIECES
    order = [(index, slice(at, at + piece)) for index in range(4) for at in range(0, hidden, piece)]
    made = first(*order[0])
    for here, ahead in zip(order, order[1:] + [None]):
        coming = None if ahead is None else first(*ahead)
        then(*here, made)
        made = coming


def piece_lanes(index, columns, hidden):
    return slice(index * hidden + columns.start, index * hidden + columns.stop)


def fixed(shape):
    return pl.BlockSpec(shape, lambda i, *_: (0,) * len(shape))


def encoder_forward_kernel(
    flag_ref, mixed_ref, x_ref, out_ref, vec_ref, ff0, ff1, ff2, ff3, bias_ref,
    *refs,
):
    sum1_ref, h_ref, g_ref, slope_ref, sum2_ref, memory_ref, weights_ref, sems = refs
    width = x_ref.shape[1]
    hidden = ff0.shape[1]
    is_enc = flag_ref[0] == 0
    wait = fetch_packs((ff0, ff1, ff2, ff3), weights_ref, sems, is_enc)
    stream = x_ref[...].astype(F32)
    summed = stream + (dot(mixed_ref[...], out_ref[...]) + vec_ref[0])
    sum1_ref[...] = summed
    first = normed_of(summed)[0] * vec_ref[2] + vec_ref[3]
    h_ref[...] = first.astype(BF16)
    wait()

    @pl.when(is_enc)
    def _():
        sum2_ref[...] = first + stream + vec_ref[1]

        def hidden_of(index, columns):
            return dot(h_ref[...], weights_ref[index, :width, columns]) + bias_ref[index:index + 1, columns]

        def quarter(index, columns, pre):
            value, slope = gelu_parts(pre)
            value = value.astype(BF16)
            lanes = piece_lanes(index, columns, hidden)
            g_ref[:, lanes] = value
            slope_ref[:, lanes] = slope.astype(BF16)
            below = slice(width + columns.start, width + columns.stop)
            sum2_ref[...] = sum2_ref[...] + dot(value, weights_ref[index, below, :])

        over_pieces(hidden, hidden_of, quarter)
        last = (normed_of(sum2_ref[...])[0] * vec_ref[4] + vec_ref[5]).astype(BF16)
        memory_ref[...] = last


def encoder_forward(flag, mixed, stream, out_weight, vectors, ff_packs, bias):
    rows, width = stream.shape
    hidden = 4 * ff_packs[0].shape[1]
    operands = (flag, mixed, stream, out_weight, vectors, *ff_packs, bias)
    return pl.pallas_call(
        encoder_forward_kernel,
        grid_spec=pltpu.PrefetchScalarGridSpec(
            num_scalar_prefetch=1,
            grid=(rows // TB,),
            in_specs=[tokens(width), tokens(width), fixed(out_weight.shape), fixed(vectors.shape)]
            + [anywhere()] * len(ff_packs)
            + [fixed(bias.shape)],
            out_specs=[
                tokens(width), tokens(width), tokens(hidden, 0), tokens(hidden, 0), tokens(width, 0), tokens(width, 0)
            ],
            scratch_shapes=ff_scratch(ff_packs),
        ),
        out_shape=[
            jax.ShapeDtypeStruct((rows, width), F32),
            jax.ShapeDtypeStruct((rows, width), BF16),
            jax.ShapeDtypeStruct((rows, hidden), BF16),
            jax.ShapeDtypeStruct((rows, hidden), BF16),
            jax.ShapeDtypeStruct((rows, width), F32),
            jax.ShapeDtypeStruct((rows, width), BF16),
        ],
        compiler_params=params(),
        cost_estimate=cost(2 * rows * width * (width + 2 * hidden), 20 * rows * width),
        name="encoder_forward",
    )(*operands)


def decoder_kernel(
    flag_ref, mixed_ref, sum1_ref, x_ref, cot_ref, g_in, h_in, memory_in,
    out_ref, vec_ref, cvec_ref, ff0, ff1, ff2, ff3, bias_ref,
    result_ref, g_ref, z_ref, du_ref, df_ref, dcross_ref, dmixed_ref, dh_ref, dlast_ref, vgrad_ref, bgrad_ref,
    weights_ref, sems, slope_ref, total_ref,
):
    width = x_ref.shape[1]
    hidden = ff0.shape[1]
    wait = fetch_packs((ff0, ff1, ff2, ff3), weights_ref, sems, flag_ref[0] == 1)

    @pl.when(pl.program_id(0) == 0)
    def _():
        vgrad_ref[...] = jnp.zeros(vgrad_ref.shape, F32)
        bgrad_ref[...] = jnp.zeros(bgrad_ref.shape, F32)

    @pl.when(flag_ref[0] == 0)
    def _():
        result_ref[...] = memory_in[...]
        g_ref[...] = g_in[...]
        z_ref[...] = h_in[...]

    @pl.when(flag_ref[0] == 1)
    def _():
        stream = x_ref[...].astype(F32)
        first = normed_of(sum1_ref[...])[0] * vec_ref[2] + vec_ref[3]
        mixed = mixed_ref[...]
        crossed = dot(mixed, out_ref[...]) + cvec_ref[2:3, :]
        normed_c, inverse_c = normed_of(first + crossed)
        second = normed_c * cvec_ref[3:4, :] + cvec_ref[4:5, :]
        second_low = second.astype(BF16)
        z_ref[...] = second_low
        total_ref[...] = second + stream + vec_ref[1]
        wait()

        def hidden_of(index, columns):
            return dot(z_ref[...], weights_ref[index, :width, columns]) + bias_ref[index:index + 1, columns]

        def quarter(index, columns, pre):
            value, slope = gelu_parts(pre)
            value = value.astype(BF16)
            lanes = piece_lanes(index, columns, hidden)
            g_ref[:, lanes] = value
            slope_ref[:, lanes] = slope.astype(BF16)
            below = slice(width + columns.start, width + columns.stop)
            total_ref[...] = total_ref[...] + dot(value, weights_ref[index, below, :])

        over_pieces(hidden, hidden_of, quarter)
        normed, inverse = normed_of(total_ref[...])
        result_ref[...] = (normed * vec_ref[4] + vec_ref[5]).astype(BF16)
        grad = cot_ref[...].astype(F32)
        grad_last = norm_back(grad, normed, inverse, vec_ref[4])
        dlast_ref[...] = grad_last
        grad_ffn = grad_last.astype(BF16)
        df_ref[...] = grad_ffn
        total_ref[...] = grad_last

        def value_grad_of(index, columns):
            return dot_t(df_ref[...], weights_ref[index, width + columns.start:width + columns.stop, :])

        def quarter_back(index, columns, grad_value):
            lanes = piece_lanes(index, columns, hidden)
            grad_pre = (grad_value * slope_ref[:, lanes].astype(F32)).astype(BF16)
            du_ref[:, lanes] = grad_pre
            bgrad_ref[index:index + 1, columns] += column_sum(grad_pre)
            total_ref[...] = total_ref[...] + dot_t(grad_pre, weights_ref[index, :width, columns])

        over_pieces(hidden, value_grad_of, quarter_back)
        grad_second = total_ref[...]
        grad_cross = norm_back(grad_second, normed_c, inverse_c, cvec_ref[3:4, :])
        dh_ref[...] = grad_cross
        cross_low = grad_cross.astype(BF16)
        dcross_ref[...] = cross_low
        dmixed_ref[...] = dot_t(cross_low, out_ref[...]).astype(BF16)
        vgrad_ref[1:2, :] += column_sum(grad_ffn)
        vgrad_ref[4:5, :] += column_sum(grad * normed)
        vgrad_ref[5:6, :] += column_sum(grad)
        vgrad_ref[6:7, :] += column_sum(cross_low)
        vgrad_ref[7:8, :] += column_sum(grad_second * normed_c)
        vgrad_ref[8:9, :] += column_sum(grad_second)


def decoder_step(flag, mixed, sum1, stream, cot, g_in, h_in, memory_in, out_weight, vectors, cvec, ff_packs, bias):
    rows, width = stream.shape
    hidden = g_in.shape[1]
    return pl.pallas_call(
        decoder_kernel,
        grid_spec=pltpu.PrefetchScalarGridSpec(
            num_scalar_prefetch=1,
            grid=(rows // TB,),
            in_specs=[
                tokens(width, 1), tokens(width, 1), tokens(width, 1), tokens(width, 1), tokens(hidden, 0),
                tokens(width, 0), tokens(width, 0), fixed(out_weight.shape), fixed(vectors.shape), fixed(cvec.shape),
            ]
            + [anywhere()] * len(ff_packs)
            + [fixed(bias.shape)],
            out_specs=[
                tokens(width), tokens(hidden), tokens(width), tokens(hidden, 1), tokens(width, 1), tokens(width, 1),
                tokens(width, 1), tokens(width, 1), tokens(width, 1), fixed((16, width)), fixed(bias.shape),
            ],
            scratch_shapes=ff_scratch(ff_packs) + [pltpu.VMEM((TB, hidden), BF16), pltpu.VMEM((TB, width), F32)],
        ),
        out_shape=[
            jax.ShapeDtypeStruct((rows, width), BF16),
            jax.ShapeDtypeStruct((rows, hidden), BF16),
            jax.ShapeDtypeStruct((rows, width), BF16),
            jax.ShapeDtypeStruct((rows, hidden), BF16),
            jax.ShapeDtypeStruct((rows, width), BF16),
            jax.ShapeDtypeStruct((rows, width), BF16),
            jax.ShapeDtypeStruct((rows, width), BF16),
            jax.ShapeDtypeStruct((rows, width), F32),
            jax.ShapeDtypeStruct((rows, width), F32),
            jax.ShapeDtypeStruct((16, width), F32),
            jax.ShapeDtypeStruct(bias.shape, F32),
        ],
        compiler_params=params(),
        cost_estimate=cost(2 * rows * width * (2 * width + 4 * hidden), 40 * rows * width),
        name="decoder_step",
    )(flag, mixed, sum1, stream, cot, g_in, h_in, memory_in, out_weight, vectors, cvec, *ff_packs, bias)


def backward_kernel(
    flag_ref, cot_ref, dmem_ref, sum1_ref, sum2_ref, slope_ref,
    dh_in, dq_in, dlast_in, du_in, df_in, vgrad_in, bgrad_in,
    out_ref, cross_ref, vec_ref, ff0, ff1, ff2, ff3,
    du_ref, df_ref, da_ref, dmixed_ref, dres_ref, vgrad_ref, bgrad_ref, dfirst_ref, weights_ref, sems,
):
    width = cot_ref.shape[1]
    hidden = ff0.shape[1]
    wait = fetch_packs((ff0, ff1, ff2, ff3), weights_ref, sems, flag_ref[0] == 0)
    at_start = pl.program_id(0) == 0
    is_dec = flag_ref[0] == 1

    @pl.when(at_start & is_dec)
    def _():
        vgrad_ref[...] = vgrad_in[...]
        bgrad_ref[...] = bgrad_in[...]

    @pl.when(at_start & jnp.logical_not(is_dec))
    def _():
        vgrad_ref[...] = jnp.zeros(vgrad_ref.shape, F32)
        bgrad_ref[...] = jnp.zeros(bgrad_ref.shape, F32)

    @pl.when(is_dec)
    def _():
        du_ref[...] = du_in[...]
        df_ref[...] = df_in[...]
        dres_ref[...] = dlast_in[...]
        dfirst_ref[...] = dh_in[...] + dot_t(dq_in[...], cross_ref[...])

    @pl.when(jnp.logical_not(is_dec))
    def _():
        grad = cot_ref[...].astype(F32) + dmem_ref[...].astype(F32)
        normed, inverse = normed_of(sum2_ref[...])
        grad_last = norm_back(grad, normed, inverse, vec_ref[4])
        dres_ref[...] = grad_last
        grad_ffn = grad_last.astype(BF16)
        df_ref[...] = grad_ffn
        dfirst_ref[...] = grad_last
        wait()

        def value_grad_of(index, columns):
            return dot_t(df_ref[...], weights_ref[index, width + columns.start:width + columns.stop, :])

        def quarter_back(index, columns, grad_value):
            lanes = piece_lanes(index, columns, hidden)
            grad_pre = (grad_value * slope_ref[:, lanes].astype(F32)).astype(BF16)
            du_ref[:, lanes] = grad_pre
            bgrad_ref[index:index + 1, columns] += column_sum(grad_pre)
            dfirst_ref[...] = dfirst_ref[...] + dot_t(grad_pre, weights_ref[index, :width, columns])

        over_pieces(hidden, value_grad_of, quarter_back)
        vgrad_ref[1:2, :] += column_sum(grad_ffn)
        vgrad_ref[4:5, :] += column_sum(grad * normed)
        vgrad_ref[5:6, :] += column_sum(grad)

    grad_first = dfirst_ref[...]
    normed, inverse = normed_of(sum1_ref[...])
    grad_in = norm_back(grad_first, normed, inverse, vec_ref[2])
    low = grad_in.astype(BF16)
    da_ref[...] = low
    dmixed_ref[...] = dot_t(low, out_ref[...]).astype(BF16)
    dres_ref[...] = dres_ref[...] + grad_in
    vgrad_ref[0:1, :] += column_sum(low)
    vgrad_ref[2:3, :] += column_sum(grad_first * normed)
    vgrad_ref[3:4, :] += column_sum(grad_first)


def backward_step(
    flag, cot, dmem, sum1, sum2, slope, dh, dq, dlast, du, df, vgrad, bgrad, out_weight, cross_query, vectors, ff_packs
):
    rows, width = cot.shape
    hidden = du.shape[1]
    return pl.pallas_call(
        backward_kernel,
        grid_spec=pltpu.PrefetchScalarGridSpec(
            num_scalar_prefetch=1,
            grid=(rows // TB,),
            in_specs=[
                tokens(width, 0), tokens(width, 0), tokens(width), tokens(width, 0), tokens(hidden, 0),
                tokens(width, 1), tokens(width, 1), tokens(width, 1), tokens(hidden, 1), tokens(width, 1),
                fixed(vgrad.shape), fixed(bgrad.shape),
                fixed(out_weight.shape), fixed(cross_query.shape), fixed(vectors.shape),
            ]
            + [anywhere()] * len(ff_packs),
            out_specs=[
                tokens(hidden), tokens(width), tokens(width), tokens(width), tokens(width),
                fixed(vgrad.shape), fixed(bgrad.shape),
            ],
            scratch_shapes=[pltpu.VMEM((TB, width), F32)] + ff_scratch(ff_packs),
        ),
        out_shape=[
            jax.ShapeDtypeStruct((rows, hidden), BF16),
            jax.ShapeDtypeStruct((rows, width), BF16),
            jax.ShapeDtypeStruct((rows, width), BF16),
            jax.ShapeDtypeStruct((rows, width), BF16),
            jax.ShapeDtypeStruct((rows, width), F32),
            jax.ShapeDtypeStruct(vgrad.shape, F32),
            jax.ShapeDtypeStruct(bgrad.shape, F32),
        ],
        compiler_params=params(),
        cost_estimate=cost(2 * rows * width * (width + 2 * hidden), 40 * rows * width),
        name="backward_step",
    )(
        flag, cot, dmem, sum1, sum2, slope, dh, dq, dlast, du, df, vgrad, bgrad,
        out_weight, cross_query, vectors, *ff_packs,
    )


def input_kernel(dres_ref, *refs):
    *parts, weight_ref, dx_ref = refs
    total = dres_ref[...]
    at = 0
    for part in parts:
        wide = part.shape[1]
        total = total + dot_t(part[...], weight_ref[:, at:at + wide])
        at += wide
    dx_ref[...] = total.astype(BF16)


def input_step(dres, parts, weight):
    rows, width = dres.shape
    block = 256
    spec = lambda v: pl.BlockSpec((block, v.shape[1]), lambda i: (i, 0))
    return pl.pallas_call(
        input_kernel,
        grid=(rows // block,),
        in_specs=[spec(v) for v in (dres, *parts)] + [fixed(weight.shape)],
        out_specs=spec(dres),
        out_shape=jax.ShapeDtypeStruct((rows, width), BF16),
        compiler_params=params(),
        cost_estimate=cost(6 * rows * width * width, 12 * rows * width),
        name="input_step",
    )(dres, *parts, weight)


def finish_kernel(ff_ref, attn_ref, ffin_ref, ffout_ref, qkv_ref, out_ref, bias_ref, hidden_ref, vectors_ref):
    width = ffin_ref.shape[0]
    lane = attn_ref.shape[1]
    ffin_ref[...] = ff_ref[:width, :].astype(F32)
    ffout_ref[...] = ff_ref[width:, :].astype(F32)
    for index in range(3):
        qkv_ref[index] = attn_ref[index * width:(index + 1) * width, :].astype(F32)
    for index in range(width // lane):
        at = 3 * width + index * lane
        out_ref[:, index * lane:(index + 1) * lane] = attn_ref[at:at + lane, :].astype(F32)
    rows = attn_ref[4 * width:, :].astype(F32)
    bias_ref[...] = rows[0:2]
    for index in range(hidden_ref.shape[1] // lane):
        hidden_ref[:, index * lane:(index + 1) * lane] = rows[2 + index:3 + index]
    count = width // lane
    for index in range(6):
        for part in range(count):
            row = 16 + index * count + part
            vectors_ref[index, :, part * lane:(part + 1) * lane] = rows[row:row + 1]


def finish(ff_total, attn_total):
    width, lane = ff_total.shape[1], attn_total.shape[1]
    hidden = ff_total.shape[0] - width
    shapes = [(width, hidden), (hidden, width), (3, width, lane), (lane, width), (2, lane), (1, hidden), (6, 1, width)]
    return pl.pallas_call(
        finish_kernel,
        grid=(1,),
        in_specs=[fixed(ff_total.shape), fixed(attn_total.shape)],
        out_specs=[fixed(shape) for shape in shapes],
        out_shape=[jax.ShapeDtypeStruct(shape, F32) for shape in shapes],
        compiler_params=params(),
        cost_estimate=cost(0, 20 * width * width),
        name="finish",
    )(ff_total, attn_total)


def flipped(value, bits, section=None):
    count = lax.axis_size("tensor")
    if section is None:
        return lax.ppermute(value, "tensor", [(t, t ^ bits) for t in range(count)])
    base = section * count
    return lax.ppermute(value, ("pipe", "tensor"), [(base + t, base + (t ^ bits)) for t in range(count)])


def across(value, source, active):
    count = lax.axis_size("tensor")
    other = 1 - source
    pairs = [(source * count + t, other * count + t) for t in range(active)]
    return lax.ppermute(value, ("pipe", "tensor"), pairs)


def plus(own, received):
    return (own.astype(F32) + received.astype(F32)).astype(BF16)


def along_dp(part, level, section=None):
    count = lax.axis_size("dp")
    if section is None:
        return lax.ppermute(part, "dp", [(i, i ^ (1 << level)) for i in range(count)])
    base = section * count
    return lax.ppermute(part, ("pipe", "dp"), [(base + i, base + (i ^ (1 << level))) for i in range(count)])


def summed_whole(value, level, section=None, behind=()):
    return plus(after(value, *behind), along_dp(value, level, section))


def dp_bit(level):
    return lax.shift_right_logical(lax.axis_index("dp"), level) & 1


def halved(value, level, section=None, behind=()):
    rows = value.shape[0] // 2
    mine = dp_bit(level)
    got = along_dp(lax.dynamic_slice_in_dim(value, (1 - mine) * rows, rows, 0), level, section)
    return plus(lax.dynamic_slice_in_dim(after(value, *behind), mine * rows, rows, 0), got)


def doubled(value, level, section=None, behind=()):
    other = along_dp(value, level, section)
    upper = dp_bit(level) == 1
    value = after(value, *behind)
    return jnp.concatenate([jnp.where(upper, other, value), jnp.where(upper, value, other)], 0)


def after(value, *others):
    return lax.optimization_barrier((value, *others))[0]


def to_rows(shard):
    count = lax.axis_size("tensor")
    shard = jnp.pad(shard, ((0, count - shard.shape[0]), (0, 0), (0, 0)))
    out = lax.all_to_all(shard, "tensor", 0, 0, tiled=True)
    return out.reshape(count * shard.shape[1], shard.shape[2])


def from_rows(row, row_count):
    count = lax.axis_size("tensor")
    parts = row.reshape(count, row.shape[0] // count, row.shape[1])
    return lax.all_to_all(parts, "tensor", 0, 0, tiled=True)[:row_count]


def shards(
    inputs, cotangent, segments, pads, self_qkv, self_bias, self_out, ff_in, ff_bias, ff_out, vectors,
    cross_q, cross_kv, cross_out, cross_small, cross_gain,
):
    section = lax.axis_index("pipe").astype(jnp.int32)
    place = lax.axis_index("tensor").astype(jnp.int32)
    count = lax.axis_size("tensor")
    row_count = inputs.shape[1]
    decoder = section == 1
    flag, place_flag = section[None], place[None]
    width = inputs.shape[3]
    lane = self_qkv.shape[3]
    hidden = ff_in.shape[2]
    half = width // 2
    row = jnp.minimum(place, row_count - 1)

    attn_own, cross_half = first_packs(
        jnp.transpose(self_qkv[0], (1, 0, 2)), self_out[0], self_bias[0], ff_bias, cross_q,
        jnp.transpose(cross_kv, (1, 0, 2)), cross_out, cross_small, cross_gain[None],
    )
    attn_far, attn_near = flipped(attn_own, 2), flipped(attn_own, 1)
    stream = to_rows(after(inputs[0], attn_own))
    slots = jnp.concatenate(
        [
            lax.dynamic_index_in_dim(segments, row, 1, False),
            lax.dynamic_slice_in_dim(pads[0], row, 1, 0),
        ],
        0,
    )
    attn_packs = [attn_own, attn_near, attn_far, flipped(attn_far, 1)]
    other_half = across(cross_half, 0, count)
    ff_own = after(jnp.concatenate([ff_in[0], ff_out[0]], 0), stream, attn_far)
    ff_far, ff_near = flipped(ff_own, 2), flipped(ff_own, 1)
    vector_rows = jnp.transpose(vectors, (1, 0, 2))

    qkv, qkv_weight, out_weight, hidden_bias, own_code, key_code, target_code, source_code, self_bounds, cross_bounds = (
        query_key_value(flag, stream, slots, attn_packs)
    )
    parts = ((qkv, 0), (qkv, 1), (qkv, 2))
    self_codes, cross_codes = (own_code, key_code), (target_code, source_code)
    mixed, totals = attend_forward(self_bounds, self_codes, width, *parts)
    cross_own = jnp.concatenate([after(other_half, mixed), cross_half], 0)
    cross_far, cross_near = flipped(cross_own, 2, 1), flipped(cross_own, 1, 1)
    ff_packs = [ff_own, ff_near, ff_far, flipped(after(ff_far, cross_own), 1)]
    sum1, first_low, g_enc, slope, sum2, memory = encoder_forward(
        flag, mixed, stream, out_weight, vector_rows, ff_packs, hidden_bias
    )
    memory_in = across(memory, 0, row_count)
    cross_packs = [cross_own, cross_near, cross_far, flipped(after(cross_far, memory), 1, 1)]
    cot_row = to_rows(after(cotangent[0], memory))

    cross_query, cross_pair, cross_out_weight, cvec = cross_unpack(place_flag, cross_packs)
    cross_made = cross_project(first_low, memory_in, cross_query, cross_pair, cvec)
    cross_parts = ((cross_made, 0), (cross_made, 1), (cross_made, 2))
    cross_mixed, cross_totals = attend_forward(cross_bounds, cross_codes, width, *cross_parts)
    result, g_all, z_all, du_dec, df_dec, dcross, dcross_mixed, dh_dec, dlast_dec, vgrad_dec, bgrad_dec = decoder_step(
        flag, cross_mixed, sum1, stream, cot_row, g_enc, first_low, memory,
        cross_out_weight, vector_rows, cvec, ff_packs, hidden_bias,
    )
    dq_cross, dk_cross, dv_cross, dmemory = attend_backward(
        cross_bounds, cross_codes, *cross_parts, dcross_mixed, cross_totals, cross_pair
    )
    dmemory_in = across(dmemory, 1, row_count)
    cross_grads = attention_grads(
        True, place_flag, first_low, memory_in, (after(dq_cross, dmemory), dk_cross, dv_cross), cross_mixed, dcross,
        vgrad_dec, bgrad_dec, lane,
    )
    cross_far = plus(after(cross_grads[2], dmemory_in), flipped(cross_grads[3], 1, 1))
    cross_got = flipped(cross_grads[1], 1, 1)

    du_all, df_all, da, dmixed, dres, vgrad, bgrad = backward_step(
        flag, cot_row, dmemory_in, sum1, sum2, slope, dh_dec, after(dq_cross, cross_far, cross_grads[1]), dlast_dec,
        du_dec, df_dec, vgrad_dec, bgrad_dec, out_weight, cross_query, vector_rows, ff_packs,
    )
    cross_near = plus(after(cross_grads[0], da), cross_got)
    cross_part = plus(cross_near, flipped(cross_far, 2, 1))
    levels = range(lax.axis_size("dp").bit_length() - 1)
    ff_third, ff_second = feed_forward_grads(after(z_all, cross_part), du_all, g_all, df_all, 3, hidden)
    ff_first, ff_zeroth = feed_forward_grads(after(z_all, ff_second), du_all, g_all, df_all, 1, hidden)
    ff_far = plus(after(ff_second, ff_zeroth), flipped(ff_third, 1))
    ff_near = plus(after(ff_zeroth, ff_far), flipped(ff_first, 1))
    dqkv = attend_backward(self_bounds, self_codes, *parts, after(dmixed, ff_near), totals)
    cross_total = halved(cross_part, 0, 1, (dqkv[0],))
    ff_part = plus(after(ff_near, dqkv[0], cross_total), flipped(ff_far, 2))
    attn_grads = attention_grads(
        False, place_flag, stream, stream, (after(dqkv[0], ff_part), *dqkv[1:]), mixed, da, vgrad, bgrad, lane
    )
    ff_total = halved(ff_part, 0, behind=(attn_grads[3],))
    for level in levels[1:]:
        cross_total = halved(cross_total, level, 1, (ff_total,))
    attn_far = plus(after(attn_grads[2], ff_total, cross_total), flipped(attn_grads[3], 1))
    attn_near = plus(after(attn_grads[0], attn_far), flipped(attn_grads[1], 1))
    dx = input_step(after(dres, attn_near), dqkv, qkv_weight)
    section_out = from_rows(after(result, dx), row_count)[None]
    for level in levels[1:]:
        ff_total = halved(ff_total, level, behind=(dx,))
    cross_total = doubled(cross_total, levels[-1], 1, (ff_total,))
    attn_part = plus(after(attn_near, ff_total, cross_total), flipped(attn_far, 2))
    ff_total = doubled(ff_total, levels[-1], behind=(attn_part,))
    for level in reversed(levels[:-1]):
        cross_total = doubled(cross_total, level, 1, (ff_total,))
    cross_other = across(cross_total, 1, count)
    attn_total = halved(attn_part, 0, behind=(ff_total, cross_total, section_out))
    input_grad = from_rows(after(dx, attn_total), row_count).astype(F32)[None]
    for level in levels[1:]:
        attn_total = halved(attn_total, level, behind=(cross_total,))
    for level in reversed(levels[:-1]):
        ff_total = doubled(ff_total, level, behind=(attn_total,))
    attn_total = doubled(attn_total, levels[-1], behind=(ff_total, input_grad))
    cross_total, cross_other = after((cross_total, cross_other), attn_total)

    own, other = cross_total.astype(F32), cross_other.astype(F32)

    def halves(at):
        return jnp.where(decoder, own[at + half:at + 2 * half], other[at:at + half])

    cross_pair_grad = jnp.stack([halves(width), halves(2 * width)], 1)
    cross_out_grad = jnp.transpose(halves(3 * width).reshape(half // lane, lane, lane), (1, 0, 2)).reshape(lane, half)
    own_rows, other_rows = (v[4 * width:4 * width + 5 * count].reshape(5, width) for v in (own, other))
    small_grad = jnp.where(decoder, jnp.stack([own_rows[2], own_rows[4]]), other_rows[:2])
    gain_grad = jnp.where(decoder, own_rows[3, half:], other_rows[3, :half])
    cross_first, cross_last = halves(0), (cross_pair_grad, cross_out_grad, small_grad, gain_grad)
    for level in reversed(levels[:-1]):
        attn_total = doubled(attn_total, level, behind=(cross_first, *cross_last))
    ffin_grad, ffout_grad, qkv_grad, out_grad, bias_grad, hidden_grad, vectors_grad = finish(
        ff_total, attn_total
    )
    return (
        section_out,
        input_grad,
        jnp.transpose(qkv_grad, (1, 0, 2))[None],
        bias_grad[None],
        out_grad[None],
        ffin_grad[None],
        hidden_grad,
        ffout_grad[None],
        jnp.transpose(vectors_grad, (1, 0, 2)),
        cross_first,
        *cross_last,
    )


def solution(mesh):
    token_spec = P("pipe", "dp", "tensor", None)
    weights = (
        P("pipe", None, None, "tensor"),
        P("pipe", None, "tensor"),
        P("pipe", "tensor", None),
        P("pipe", None, "tensor"),
        P("pipe", "tensor"),
        P("pipe", "tensor", None),
        P("pipe", None, None),
        P("pipe", "tensor"),
        P("pipe", None, "tensor"),
        P("tensor", "pipe"),
        P("pipe", None),
        P("pipe"),
    )
    return jax.shard_map(
        shards,
        mesh=mesh,
        in_specs=(token_spec, token_spec, P(None, "dp", None), P("pipe", "dp", None)) + weights,
        out_specs=(token_spec, token_spec) + weights,
        check_vma=False,
    )
```

```python
import functools

import jax
import jax.numpy as jnp
from jax import lax
from jax.experimental import pallas as pl
from jax.experimental.pallas import tpu as pltpu
from jax.sharding import PartitionSpec as P

HEAD_DIM = 64
EPSILON = 1e-05
MASKED = -1e30
SEGS = 8
QF = 256
QB = 256
TB = 512
PIECES = 1
PAIR = 2 * HEAD_DIM
GELU_C = 0.7978845608028654
GELU_A = 0.044715
VMEM_LIMIT = 56 * 1024 * 1024
F32 = jnp.float32
BF16 = jnp.bfloat16


def dot(left, right):
    return jnp.dot(left, right, preferred_element_type=F32)


def dot_t(left, right):
    return lax.dot_general(left, right, (((1,), (1,)), ((), ())), preferred_element_type=F32)


def dot_tl(left, right):
    return lax.dot_general(left, right, (((0,), (0,)), ((), ())), preferred_element_type=F32)


def normed_of(values):
    center = values - jnp.mean(values, -1, keepdims=True)
    inverse = lax.rsqrt(jnp.mean(center * center, -1, keepdims=True) + EPSILON)
    return center * inverse, inverse


def norm_back(grad, normed, inverse, gain):
    scaled = grad * gain
    mean_scaled = jnp.mean(scaled, -1, keepdims=True)
    mean_both = jnp.mean(scaled * normed, -1, keepdims=True)
    return (scaled - mean_scaled - normed * mean_both) * inverse


def column_sum(values):
    return jnp.sum(values.astype(F32), 0, keepdims=True)


def gelu_parts(pre):
    squared = pre * pre
    half = 0.5 * jnp.tanh(pre * (GELU_C + (GELU_C * GELU_A) * squared)) + 0.5
    slope = half + (pre * (half - half * half)) * (2.0 * GELU_C + (6.0 * GELU_C * GELU_A) * squared)
    return pre * half, slope


def cost(flops, moved):
    return pl.CostEstimate(flops=int(flops) // 64, bytes_accessed=int(moved) // 64, transcendentals=0)


def params(axes=1):
    return pltpu.CompilerParams(
        dimension_semantics=("arbitrary",) * axes, vmem_limit_bytes=VMEM_LIMIT
    )


def find_segments(section, slots_ref, own_ref, key_ref, target_ref, source_ref, self_ref, cross_ref):
    length = slots_ref.shape[1]
    source = slots_ref[0:1, :].astype(F32)
    target = slots_ref[1:2, :].astype(F32)
    own = jnp.where(section == 1, target, source)
    own_ref[...] = own
    key_ref[...] = jnp.where(slots_ref[2:3, :] == 0, own, -1.0)
    target_ref[...] = target
    source_ref[...] = source

    def starts(segments):
        found = [jnp.int32(0)]
        for index in range(1, SEGS):
            found.append(jnp.sum(jnp.where(segments < float(index), 1.0, 0.0)).astype(jnp.int32))
        return found + [jnp.int32(length)]

    source_starts, target_starts = starts(source), starts(target)
    for index in range(SEGS):
        own_start = jnp.where(section == 1, target_starts[index], source_starts[index])
        own_end = jnp.where(section == 1, target_starts[index + 1], source_starts[index + 1])
        self_ref[index] = own_start
        self_ref[16 + index] = own_start
        self_ref[32 + index] = own_end
        cross_ref[index] = target_starts[index]
        cross_ref[16 + index] = source_starts[index]
        cross_ref[32 + index] = source_starts[index + 1]
    self_ref[48] = jnp.int32(1)
    self_ref[49] = section
    self_ref[50] = jnp.int32(1)
    cross_ref[48] = jnp.int32(0)
    cross_ref[49] = jnp.int32(0)
    cross_ref[50] = section


def half_masked(values, side):
    lane = lax.broadcasted_iota(jnp.int32, values.shape, 1)
    return jnp.where((lane >= HEAD_DIM) == bool(side), values, jnp.zeros_like(values))


def key_window(bounds, block, block_rows):
    first = block * block_rows
    last = first + (block_rows - 1)
    low, high = jnp.int32(0), jnp.int32(0)
    for index in range(SEGS):
        low = jnp.where(bounds[index] <= first, bounds[16 + index], low)
        high = jnp.where(bounds[index] <= last, bounds[32 + index], high)
    high = jnp.where(bounds[49] == 1, jnp.minimum(high, last + 1), high)
    low_block = lax.shift_right_logical(low, 7)
    high_block = lax.shift_right_logical(high + 127, 7)
    return low_block, jnp.where(bounds[50] == 1, high_block - low_block, 0)


def by_size(bounds, block, block_rows, key_blocks, sizes, body):
    low_block, needed = key_window(bounds, block, block_rows)
    below = 0
    for size in sizes:
        size = min(size, key_blocks)
        if size == below:
            continue

        @pl.when((needed > below) & (needed <= size))
        def _(size=size):
            start = jnp.minimum(low_block, key_blocks - size) * 128
            body(size, pl.multiple_of(start, 128))

        below = size


def as_columns(row):
    parts = []
    for at in range(0, row.shape[1], 128):
        parts.append(jnp.broadcast_to(row[:, at:at + 128], (128, 128)).T)
    return jnp.concatenate(parts, 0)


def window_bias(bounds, block, block_rows, start, key_code, qcode_ref):
    key_at = start + lax.broadcasted_iota(jnp.int32, key_code.shape, 0)
    tiles = []
    for at in range(0, block_rows, 128):
        query_at = block * block_rows + at + lax.broadcasted_iota(jnp.int32, (1, 128), 1)
        limit = jnp.where(bounds[49] == 1, query_at, jnp.int32(1 << 30))
        same_at = jnp.where(bounds[48] == 1, query_at, -1)
        opened = (key_code == qcode_ref[:, at:at + 128]) & (key_at <= limit)
        tiles.append(jnp.where(opened | (key_at == same_at), 0.0, MASKED))
    return jnp.concatenate(tiles, 1)


def attend_forward_kernel(bounds, q_ref, k_ref, v_ref, qcode_ref, kcode_ref, mixed_ref, total_ref):
    block = pl.program_id(0)
    heads = q_ref.shape[1] // HEAD_DIM
    key_blocks = k_ref.shape[0] // 128
    own_code = as_columns(qcode_ref[...])
    query_at = block * QF + lax.broadcasted_iota(jnp.int32, (QF, 128), 0)
    limit = jnp.where(bounds[49] == 1, query_at, jnp.int32(1 << 30))
    same_at = jnp.where(bounds[48] == 1, query_at, -1)
    lane = lax.broadcasted_iota(jnp.int32, (QF, 128), 1)

    def body(size, start):
        window = pl.ds(start, size * 128)
        tiles = []
        for tile in range(size):
            at = start + tile * 128
            key_at = at + lane
            opened = (own_code == kcode_ref[:, pl.ds(pl.multiple_of(at, 128), 128)]) & (key_at <= limit)
            tiles.append(jnp.where(opened | (key_at == same_at), 0.0, MASKED))
        bias = jnp.concatenate(tiles, 1)

        def two_pairs(index, columns):
            lanes = [pl.ds(pl.multiple_of((2 * index + at) * PAIR, PAIR), PAIR) for at in range(2)]
            scores = []
            for at in range(2):
                queries, keys = q_ref[:, lanes[at]], k_ref[window, lanes[at]]
                scores.append([dot_t(half_masked(queries, side), keys) + bias for side in range(2)])
            for at in range(2):
                values = v_ref[window, lanes[at]]
                out = None
                for side in range(2):
                    top = jnp.max(scores[at][side], -1, keepdims=True)
                    weights = jnp.exp(scores[at][side] - top)
                    total = jnp.sum(weights, -1, keepdims=True)
                    part = dot(weights.astype(BF16), half_masked(values, side)) * (1.0 / total)
                    out = part if out is None else out + part
                    columns = jnp.where(lane == (2 * index + at) * 2 + side, top + jnp.log(total), columns)
                mixed_ref[:, lanes[at]] = out.astype(BF16)
            return columns

        columns = lax.fori_loop(0, heads // 4, two_pairs, jnp.zeros((QF, 128), F32))
        total_ref[...] = columns.T[:heads]

    by_size(bounds, block, QF, key_blocks, (2, 3, 4, 5, 6, 8), body)


def attend_forward(bounds, codes, width, queries, keys, values):
    (q_array, q_at), (k_array, k_at), (v_array, v_at) = queries, keys, values
    rows = q_array.shape[0]
    heads = width // HEAD_DIM
    whole = lambda at: (lambda i, *_: (0, at))
    return pl.pallas_call(
        attend_forward_kernel,
        grid_spec=pltpu.PrefetchScalarGridSpec(
            num_scalar_prefetch=1,
            grid=(rows // QF,),
            in_specs=[
                pl.BlockSpec((QF, width), lambda i, *_: (i, q_at)),
                pl.BlockSpec((rows, width), whole(k_at)),
                pl.BlockSpec((rows, width), whole(v_at)),
                pl.BlockSpec((1, QF), lambda i, *_: (0, i)),
                pl.BlockSpec((1, rows), whole(0)),
            ],
            out_specs=[
                pl.BlockSpec((QF, width), lambda i, *_: (i, 0)),
                pl.BlockSpec((heads, QF), lambda i, *_: (0, i)),
            ],
        ),
        out_shape=[
            jax.ShapeDtypeStruct((rows, width), BF16),
            jax.ShapeDtypeStruct((heads, rows), F32),
        ],
        compiler_params=params(),
        cost_estimate=cost(4 * rows * 512 * width * 2, 8 * rows * width),
        name="attend_forward",
    )(bounds, q_array, k_array, v_array, *codes)


def attend_backward_kernel(has_weight, first_head, bounds, q_ref, k_ref, v_ref, grad_ref, total_ref, qcode_ref, kcode_ref, *refs):
    if has_weight:
        weight_ref, dq_ref, dk_ref, dv_ref, dmem_ref, kcol_ref, dkacc_ref, dvacc_ref = refs
    else:
        dq_ref, dk_ref, dv_ref, kcol_ref, dkacc_ref, dvacc_ref = refs
    block = pl.program_id(0)
    width = q_ref.shape[1]
    heads = width // HEAD_DIM
    key_blocks = k_ref.shape[0] // 128

    @pl.when(block == 0)
    def _():
        dkacc_ref[...] = jnp.zeros(dkacc_ref.shape, F32)
        dvacc_ref[...] = jnp.zeros(dvacc_ref.shape, F32)
        kcol_ref[...] = as_columns(kcode_ref[...])

    def body(size, start):
        window = pl.ds(start, size * 128)
        bias = window_bias(bounds, block, QB, start, kcol_ref[window, :], qcode_ref)

        def two_pairs(index, carry):
            prepared = []
            for at in range(2):
                pair = 2 * index + at
                lanes = pl.ds(pl.multiple_of(pair * PAIR, PAIR), PAIR)
                queries, grads = q_ref[:, lanes], grad_ref[:, lanes]
                keys, values = k_ref[window, lanes], v_ref[window, lanes]
                query_halves = [half_masked(queries, side) for side in range(2)]
                grad_halves = [half_masked(grads, side) for side in range(2)]
                products = [
                    (dot_t(keys, query_halves[side]) + bias, dot_t(values, grad_halves[side])) for side in range(2)
                ]
                prepared.append((pair, lanes, keys, query_halves, grad_halves, products))
            for pair, lanes, keys, query_halves, grad_halves, products in prepared:
                dq = dk = dv = None
                for side in range(2):
                    scores, grad_weights = products[side]
                    weights = jnp.exp(scores - total_ref[pl.ds(first_head + pair * 2 + side, 1), :])
                    delta = jnp.sum(weights * grad_weights, 0, keepdims=True)
                    grad_scores = (weights * (grad_weights - delta)).astype(BF16)
                    made = (
                        dot_tl(grad_scores, half_masked(keys, side)),
                        dot(grad_scores, query_halves[side]),
                        dot(weights.astype(BF16), grad_halves[side]),
                    )
                    dq, dk, dv = made if dq is None else (dq + made[0], dk + made[1], dv + made[2])
                dkacc_ref[window, lanes] = dkacc_ref[window, lanes] + dk
                dvacc_ref[window, lanes] = dvacc_ref[window, lanes] + dv
                dq_ref[:, lanes] = (dq * HEAD_DIM ** (-0.5)).astype(BF16)
            return carry

        lax.fori_loop(0, heads // 4, two_pairs, 0)

    by_size(bounds, block, QB, key_blocks, (2, 3, 4, 5, 6, 8), body)

    @pl.when(block == pl.num_programs(0) - 1)
    def _():
        dk_ref[...] = dkacc_ref[...].astype(BF16)
        dv_ref[...] = dvacc_ref[...].astype(BF16)
        if has_weight:
            summed = dot_t(dk_ref[...], weight_ref[:, :width]) + dot_t(dv_ref[...], weight_ref[:, width:])
            dmem_ref[...] = summed.astype(BF16)


def attend_backward(bounds, codes, queries, keys, values, grad, totals, weight=None, part=(0, 1)):
    (q_array, q_at), (k_array, k_at), (v_array, v_at) = queries, keys, values
    index, count = part
    rows = grad.shape[0]
    heads = totals.shape[0]
    width = grad.shape[1] // count
    whole = lambda at: pl.BlockSpec((rows, width), lambda i, *_: (0, at * count + index))
    block = lambda at: pl.BlockSpec((QB, width), lambda i, *_: (i, at * count + index))
    extra = [] if weight is None else [weight]
    first = pl.BlockSpec((rows, width), lambda i, *_: (0, 0))
    return pl.pallas_call(
        functools.partial(attend_backward_kernel, weight is not None, index * heads // count),
        grid_spec=pltpu.PrefetchScalarGridSpec(
            num_scalar_prefetch=1,
            grid=(rows // QB,),
            in_specs=[
                block(q_at),
                whole(k_at),
                whole(v_at),
                block(0),
                pl.BlockSpec((heads, QB), lambda i, *_: (0, i)),
                pl.BlockSpec((1, QB), lambda i, *_: (0, i)),
                pl.BlockSpec((1, rows), lambda i, *_: (0, 0)),
            ]
            + [fixed(v.shape) for v in extra],
            out_specs=[pl.BlockSpec((QB, width), lambda i, *_: (i, 0))] + [first] * (2 + len(extra)),
            scratch_shapes=[
                pltpu.VMEM((rows, 128), F32),
                pltpu.VMEM((rows, width), F32),
                pltpu.VMEM((rows, width), F32),
            ],
        ),
        out_shape=[jax.ShapeDtypeStruct((rows, width), BF16)] * (3 + len(extra)),
        compiler_params=params(),
        cost_estimate=cost(10 * rows * 512 * width * 2, 16 * rows * width),
        name="attend_backward",
    )(bounds, q_array, k_array, v_array, grad, totals, *codes, *extra)


def first_packs_kernel(
    qkv_ref, out_ref, bias_ref, ffb_ref, query_ref, pair_ref, cout_ref, small_ref, gain_ref, pack_ref, half_ref
):
    width = qkv_ref.shape[1]
    lane = qkv_ref.shape[2]
    half = query_ref.shape[0]

    def columns(values):
        return [values[:, at:at + lane] for at in range(0, values.shape[1], lane)]

    def filled(rows):
        rest = jnp.zeros((16 - sum(part.shape[0] for part in rows), lane), F32)
        return jnp.concatenate([*rows, rest], 0).astype(BF16)

    for index in range(3):
        pack_ref[index * width:(index + 1) * width, :] = qkv_ref[index]
    for index, part in enumerate(columns(out_ref[...])):
        at = 3 * width + index * lane
        pack_ref[at:at + lane, :] = part
    bias = bias_ref[...]
    high = bias.astype(BF16).astype(F32)
    middle = (bias - high).astype(BF16).astype(F32)
    least = bias - high - middle
    pack_ref[4 * width:4 * width + 16, :] = filled([high, middle, least, *columns(ffb_ref[...].astype(F32))])
    half_ref[0:half, :] = query_ref[...]
    half_ref[half:2 * half, :] = pair_ref[0]
    half_ref[2 * half:3 * half, :] = pair_ref[1]
    for index, part in enumerate(columns(cout_ref[...])):
        at = 3 * half + index * lane
        half_ref[at:at + lane, :] = part
    small = small_ref[...].astype(F32)
    half_ref[4 * half:4 * half + 16, :] = filled(
        [*columns(small[0:1]), *columns(small[1:2]), *columns(gain_ref[...].astype(F32))]
    )


def first_packs(qkv, out_weight, bias, ff_bias, query, pair, cross_out, small, gain):
    width, lane = qkv.shape[1:]
    half = query.shape[0]
    operands = (qkv, out_weight, bias, ff_bias, query, pair, cross_out, small, gain)
    shapes = [(4 * width + 16, lane), (4 * half + 16, lane)]
    return pl.pallas_call(
        first_packs_kernel,
        grid=(1,),
        in_specs=[fixed(v.shape) for v in operands],
        out_specs=[fixed(shape) for shape in shapes],
        out_shape=[jax.ShapeDtypeStruct(shape, BF16) for shape in shapes],
        compiler_params=params(),
        cost_estimate=cost(0, 24 * width * lane),
        name="first_packs",
    )(*operands)


def query_key_value_kernel(
    flag_ref, x_ref, slots_ref, p0, p1, p2, p3, qkv_ref, weight_ref, out_ref, hidden_ref, *refs
):
    *found_refs, bias_ref = refs
    width = x_ref.shape[1]
    lane = p0.shape[1]

    @pl.when(pl.program_id(0) == 0)
    def _():
        find_segments(flag_ref[0], slots_ref, *found_refs)
        for index, pack in enumerate((p0, p1, p2, p3)):
            columns = slice(index * lane, (index + 1) * lane)
            for part in range(3):
                at = slice(part * width + index * lane, part * width + (index + 1) * lane)
                weight_ref[:, at] = pack[part * width:(part + 1) * width, :]
            for part in range(width // lane):
                at = 3 * width + part * lane
                out_ref[columns, part * lane:(part + 1) * lane] = pack[at:at + lane, :]
            rows = pack[4 * width:4 * width + 16, :].astype(F32)
            bias_ref[0:1, columns] = rows[0:1] + rows[2:3] + rows[4:5]
            bias_ref[1:2, columns] = rows[1:2] + rows[3:4] + rows[5:6]
            for part in range(width // lane):
                hidden_ref[index:index + 1, part * lane:(part + 1) * lane] = rows[6 + part:7 + part]

    made = dot(x_ref[...], weight_ref[...])
    scale = HEAD_DIM ** (-0.5)
    queries = (made[:, :width] + bias_ref[0:1, :]).astype(BF16).astype(F32) * scale
    qkv_ref[:, :width] = queries.astype(BF16)
    qkv_ref[:, width:2 * width] = made[:, width:2 * width].astype(BF16)
    qkv_ref[:, 2 * width:] = (made[:, 2 * width:] + bias_ref[1:2, :]).astype(BF16)


def query_key_value(flag, stream, slots, packs):
    rows, width = stream.shape
    line = jax.ShapeDtypeStruct((1, rows), F32)
    bounds = jax.ShapeDtypeStruct((64,), jnp.int32)
    return pl.pallas_call(
        query_key_value_kernel,
        grid_spec=pltpu.PrefetchScalarGridSpec(
            num_scalar_prefetch=1,
            grid=(rows // TB,),
            in_specs=[tokens(width), fixed(slots.shape)] + [fixed(pack.shape) for pack in packs],
            out_specs=[tokens(3 * width), fixed((width, 3 * width)), fixed((width, width)), fixed((len(packs), width))]
            + [fixed(line.shape)] * 4
            + [pl.BlockSpec(memory_space=pltpu.SMEM)] * 2,
            scratch_shapes=[pltpu.VMEM((8, width), F32)],
        ),
        out_shape=[
            jax.ShapeDtypeStruct((rows, 3 * width), BF16),
            jax.ShapeDtypeStruct((width, 3 * width), BF16),
            jax.ShapeDtypeStruct((width, width), BF16),
            jax.ShapeDtypeStruct((len(packs), width), F32),
        ]
        + [line] * 4
        + [bounds] * 2,
        compiler_params=params(),
        cost_estimate=cost(6 * rows * width * width, 10 * rows * width),
        name="query_key_value",
    )(flag, stream, slots, *packs)


def cross_project_kernel(h_ref, memory_ref, query_ref, pair_ref, cvec_ref, made_ref):
    width = h_ref.shape[1]
    queries = (dot(h_ref[...], query_ref[...]) + cvec_ref[0:1, :]).astype(BF16).astype(F32)
    made_ref[:, :width] = (queries * HEAD_DIM ** (-0.5)).astype(BF16)
    made = dot(memory_ref[...], pair_ref[...])
    made_ref[:, width:2 * width] = made[:, :width].astype(BF16)
    made_ref[:, 2 * width:] = (made[:, width:] + cvec_ref[1:2, :]).astype(BF16)


def cross_project(h, memory, query, pair, cvec):
    rows, width = h.shape
    operands = (h, memory, query, pair, cvec)
    return pl.pallas_call(
        cross_project_kernel,
        grid=(rows // TB,),
        in_specs=[tokens(width)] * 2 + [fixed(v.shape) for v in operands[2:]],
        out_specs=tokens(3 * width),
        out_shape=jax.ShapeDtypeStruct((rows, 3 * width), BF16),
        compiler_params=params(),
        cost_estimate=cost(6 * rows * width * width, 12 * rows * width),
        name="cross_project",
    )(*operands)


def cross_unpack_kernel(place_ref, p0, p1, p2, p3, query_ref, pair_ref, out_ref, cvec_ref):
    lane = p0.shape[1]
    length = p0.shape[0] // 2
    half = (length - 16) // 4
    width = 2 * half
    count = width // lane
    for index, pack in enumerate((p0, p1, p2, p3)):
        columns = slice(index * lane, (index + 1) * lane)
        for side in range(2):
            rows = slice(side * half, (side + 1) * half)
            base = side * length
            query_ref[rows, columns] = pack[base:base + half, :]
            pair_ref[rows, columns] = pack[base + half:base + 2 * half, :]
            pair_ref[rows, width + index * lane:width + (index + 1) * lane] = pack[base + 2 * half:base + 3 * half, :]
            for part in range(half // lane):
                at = base + 3 * half + part * lane
                to = side * half + part * lane
                out_ref[columns, to:to + lane] = pack[at:at + lane, :]
    first = p0[4 * half:4 * half + 16, :].astype(F32)
    second = p0[length + 4 * half:length + 4 * half + 16, :].astype(F32)
    at_row = lax.broadcasted_iota(jnp.int32, (16, lane), 0)
    for index in range(count):
        columns = slice(index * lane, (index + 1) * lane)
        for which in range(2):
            wanted = which * count + (place_ref[0] ^ index)
            cvec_ref[which:which + 1, columns] = jnp.sum(jnp.where(at_row == wanted, first, 0.0), 0, keepdims=True)
        cvec_ref[2:3, columns] = second[index:index + 1]
        cvec_ref[4:5, columns] = second[count + index:count + index + 1]
        side, part = (first, index) if index < count // 2 else (second, index - count // 2)
        cvec_ref[3:4, columns] = side[2 * count + part:2 * count + part + 1]
    cvec_ref[5:8, :] = jnp.zeros((3, width), F32)


def cross_unpack(place, packs):
    length, lane = packs[0].shape
    width = (length // 2 - 16) // 2
    return pl.pallas_call(
        cross_unpack_kernel,
        grid_spec=pltpu.PrefetchScalarGridSpec(
            num_scalar_prefetch=1,
            grid=(1,),
            in_specs=[fixed(pack.shape) for pack in packs],
            out_specs=[fixed((width, width)), fixed((width, 2 * width)), fixed((width, width)), fixed((8, width))],
        ),
        out_shape=[
            jax.ShapeDtypeStruct((width, width), BF16),
            jax.ShapeDtypeStruct((width, 2 * width), BF16),
            jax.ShapeDtypeStruct((width, width), BF16),
            jax.ShapeDtypeStruct((8, width), F32),
        ],
        compiler_params=params(),
        cost_estimate=cost(0, 16 * width * width),
        name="cross_unpack",
    )(place, *packs)


def rows_of(vector, rows, at_row, base, order=None):
    lane = rows.shape[1]
    for index in range(vector.shape[1] // lane):
        to = base + (index if order is None else (order ^ index))
        rows = rows + jnp.where(at_row == to, vector[:, index * lane:(index + 1) * lane], 0.0)
    return rows


def attention_grads_kernel(
    is_cross, parts, place_ref, aq_ref, akv_ref, *refs
):
    width = aq_ref.shape[1]
    dq_refs, dk_refs, dv_refs = (refs[part * parts:(part + 1) * parts] for part in range(3))
    mixed_ref, da_ref, vgrad_ref, bgrad_ref, *packs, made_ref = refs[3 * parts:]
    lane = packs[0].shape[1]
    count = width // lane
    tail = packs[0].shape[0] - 4 * width
    akv = akv_ref if is_cross else aq_ref
    for part, (left, rights) in enumerate(((aq_ref, dq_refs), (akv, dk_refs), (akv, dv_refs))):
        for index, right in enumerate(rights):
            wide = width // parts
            made_ref[:, index * wide:(index + 1) * wide] = dot_tl(left[...], right[...]).astype(BF16)
        for index, pack in enumerate(packs):
            pack[part * width:(part + 1) * width, :] = made_ref[:, index * lane:(index + 1) * lane]
    made_ref[...] = dot_tl(mixed_ref[...], da_ref[...]).astype(BF16)
    for index, pack in enumerate(packs):
        for part in range(count):
            at = 3 * width + part * lane
            pack[at:at + lane, :] = made_ref[index * lane:(index + 1) * lane, part * lane:(part + 1) * lane]
    query_bias, value_bias = (
        jnp.concatenate([column_sum(ref[...]) for ref in some], 1) for some in (dq_refs, dv_refs)
    )
    at_row = lax.broadcasted_iota(jnp.int32, (tail, lane), 0)
    rows = jnp.zeros((tail, lane), F32)
    if is_cross:
        rows = rows_of(query_bias, rows, at_row, 0, place_ref[0])
        rows = rows_of(value_bias, rows, at_row, count, place_ref[0])
        for index in range(3):
            rows = rows_of(vgrad_ref[6 + index:7 + index, :], rows, at_row, (2 + index) * count)
    else:
        for index in range(6):
            rows = rows_of(vgrad_ref[index:index + 1, :], rows, at_row, 16 + index * count)
    for index, pack in enumerate(packs):
        own = rows
        if not is_cross:
            columns = slice(index * lane, (index + 1) * lane)
            own = own + jnp.where(at_row == 0, query_bias[:, columns], 0.0)
            own = own + jnp.where(at_row == 1, value_bias[:, columns], 0.0)
            own = rows_of(bgrad_ref[index:index + 1, :], own, at_row, 2)
        pack[4 * width:, :] = own.astype(BF16)


def attention_grads(is_cross, place, aq, akv, dqkv, mixed, da, vgrad, bgrad, lane):
    rows, width = aq.shape
    length = 4 * width + 64
    operands = (aq, akv, *dqkv, mixed, da, vgrad, bgrad)
    count = width // lane
    return pl.pallas_call(
        functools.partial(attention_grads_kernel, is_cross, len(dqkv) // 3),
        grid_spec=pltpu.PrefetchScalarGridSpec(
            num_scalar_prefetch=1,
            grid=(1,),
            in_specs=[fixed(v.shape) for v in operands],
            out_specs=[fixed((length, lane))] * count,
            scratch_shapes=[pltpu.VMEM((width, width), BF16)],
        ),
        out_shape=[jax.ShapeDtypeStruct((length, lane), BF16)] * count,
        compiler_params=params(),
        cost_estimate=cost(8 * rows * width * width, 14 * rows * width),
        name="cross_grads" if is_cross else "self_grads",
    )(place, *operands)


def feed_forward_grads_kernel(z_ref, du_ref, g_ref, df_ref, *packs):
    width = z_ref.shape[1]
    for index, pack in enumerate(packs):

        @pl.when(pl.program_id(0) == index)
        def _(pack=pack):
            pack[:width, :] = dot_tl(z_ref[...], du_ref[...]).astype(BF16)
            pack[width:, :] = dot_tl(g_ref[...], df_ref[...]).astype(BF16)


def feed_forward_grads(z, du, g, df, first, hidden):
    rows, width = z.shape
    quarter = pl.BlockSpec((rows, hidden), lambda i: (0, first - i))
    pack = (width + hidden, width)
    return pl.pallas_call(
        feed_forward_grads_kernel,
        grid=(2,),
        in_specs=[fixed(z.shape), quarter, quarter, fixed(df.shape)],
        out_specs=[fixed(pack)] * 2,
        out_shape=[jax.ShapeDtypeStruct(pack, BF16)] * 2,
        compiler_params=params(),
        cost_estimate=cost(8 * rows * width * hidden, 12 * rows * hidden),
        name="feed_forward_grads",
    )(z, du, g, df)


def tokens(width, section=None):
    if section is None:
        return pl.BlockSpec((TB, width), lambda i, *_: (i, 0))
    if section == 0:
        return pl.BlockSpec((TB, width), lambda i, flag: (i * (1 - flag[0]), 0))
    return pl.BlockSpec((TB, width), lambda i, flag: (i * flag[0], 0))


def anywhere():
    return pl.BlockSpec(memory_space=pl.ANY)


def ff_scratch(ff_packs):
    return [
        pltpu.VMEM((len(ff_packs),) + ff_packs[0].shape, BF16),
        pltpu.SemaphoreType.DMA((len(ff_packs),)),
    ]


def fetch_packs(packs, weights_ref, sems, wanted):
    started = (pl.program_id(0) == 0) & wanted

    @pl.when(started)
    def _():
        for index, pack in enumerate(packs):
            pltpu.make_async_copy(pack, weights_ref.at[index], sems.at[index]).start()

    def wait():
        @pl.when(started)
        def _():
            for index, pack in enumerate(packs):
                pltpu.make_async_copy(pack, weights_ref.at[index], sems.at[index]).wait()

    return wait


def over_pieces(hidden, first, then):
    piece = hidden // PIECES
    order = [(index, slice(at, at + piece)) for index in range(4) for at in range(0, hidden, piece)]
    made = first(*order[0])
    for here, ahead in zip(order, order[1:] + [None]):
        coming = None if ahead is None else first(*ahead)
        then(*here, made)
        made = coming


def piece_lanes(index, columns, hidden):
    return slice(index * hidden + columns.start, index * hidden + columns.stop)


def fixed(shape):
    return pl.BlockSpec(shape, lambda i, *_: (0,) * len(shape))


def encoder_forward_kernel(
    flag_ref, mixed_ref, x_ref, out_ref, vec_ref, ff0, ff1, ff2, ff3, bias_ref,
    *refs,
):
    sum1_ref, h_ref, g_ref, slope_ref, sum2_ref, memory_ref, weights_ref, sems = refs
    width = x_ref.shape[1]
    hidden = ff0.shape[1]
    is_enc = flag_ref[0] == 0
    wait = fetch_packs((ff0, ff1, ff2, ff3), weights_ref, sems, is_enc)
    stream = x_ref[...].astype(F32)
    summed = stream + (dot(mixed_ref[...], out_ref[...]) + vec_ref[0])
    sum1_ref[...] = summed
    first = normed_of(summed)[0] * vec_ref[2] + vec_ref[3]
    h_ref[...] = first.astype(BF16)
    wait()

    @pl.when(is_enc)
    def _():
        sum2_ref[...] = first + stream + vec_ref[1]

        def hidden_of(index, columns):
            return dot(h_ref[...], weights_ref[index, :width, columns]) + bias_ref[index:index + 1, columns]

        def quarter(index, columns, pre):
            value, slope = gelu_parts(pre)
            value = value.astype(BF16)
            lanes = piece_lanes(index, columns, hidden)
            g_ref[:, lanes] = value
            slope_ref[:, lanes] = slope.astype(BF16)
            below = slice(width + columns.start, width + columns.stop)
            sum2_ref[...] = sum2_ref[...] + dot(value, weights_ref[index, below, :])

        over_pieces(hidden, hidden_of, quarter)
        last = (normed_of(sum2_ref[...])[0] * vec_ref[4] + vec_ref[5]).astype(BF16)
        memory_ref[...] = last


def encoder_forward(flag, mixed, stream, out_weight, vectors, ff_packs, bias):
    rows, width = stream.shape
    hidden = 4 * ff_packs[0].shape[1]
    operands = (flag, mixed, stream, out_weight, vectors, *ff_packs, bias)
    return pl.pallas_call(
        encoder_forward_kernel,
        grid_spec=pltpu.PrefetchScalarGridSpec(
            num_scalar_prefetch=1,
            grid=(rows // TB,),
            in_specs=[tokens(width), tokens(width), fixed(out_weight.shape), fixed(vectors.shape)]
            + [anywhere()] * len(ff_packs)
            + [fixed(bias.shape)],
            out_specs=[
                tokens(width), tokens(width), tokens(hidden, 0), tokens(hidden, 0), tokens(width, 0), tokens(width, 0)
            ],
            scratch_shapes=ff_scratch(ff_packs),
        ),
        out_shape=[
            jax.ShapeDtypeStruct((rows, width), F32),
            jax.ShapeDtypeStruct((rows, width), BF16),
            jax.ShapeDtypeStruct((rows, hidden), BF16),
            jax.ShapeDtypeStruct((rows, hidden), BF16),
            jax.ShapeDtypeStruct((rows, width), F32),
            jax.ShapeDtypeStruct((rows, width), BF16),
        ],
        compiler_params=params(),
        cost_estimate=cost(2 * rows * width * (width + 2 * hidden), 20 * rows * width),
        name="encoder_forward",
    )(*operands)


def decoder_kernel(
    flag_ref, mixed_ref, sum1_ref, x_ref, cot_ref, g_in, h_in, memory_in,
    out_ref, vec_ref, cvec_ref, ff0, ff1, ff2, ff3, bias_ref,
    result_ref, g_ref, z_ref, du_ref, df_ref, dcross_ref, dmixed_ref, dh_ref, dlast_ref, vgrad_ref, bgrad_ref,
    weights_ref, sems, slope_ref, total_ref,
):
    width = x_ref.shape[1]
    hidden = ff0.shape[1]
    wait = fetch_packs((ff0, ff1, ff2, ff3), weights_ref, sems, flag_ref[0] == 1)

    @pl.when(pl.program_id(0) == 0)
    def _():
        vgrad_ref[...] = jnp.zeros(vgrad_ref.shape, F32)
        bgrad_ref[...] = jnp.zeros(bgrad_ref.shape, F32)

    @pl.when(flag_ref[0] == 0)
    def _():
        result_ref[...] = memory_in[...]
        g_ref[...] = g_in[...]
        z_ref[...] = h_in[...]

    @pl.when(flag_ref[0] == 1)
    def _():
        stream = x_ref[...].astype(F32)
        first = normed_of(sum1_ref[...])[0] * vec_ref[2] + vec_ref[3]
        mixed = mixed_ref[...]
        crossed = dot(mixed, out_ref[...]) + cvec_ref[2:3, :]
        normed_c, inverse_c = normed_of(first + crossed)
        second = normed_c * cvec_ref[3:4, :] + cvec_ref[4:5, :]
        second_low = second.astype(BF16)
        z_ref[...] = second_low
        total_ref[...] = second + stream + vec_ref[1]
        wait()

        def hidden_of(index, columns):
            return dot(z_ref[...], weights_ref[index, :width, columns]) + bias_ref[index:index + 1, columns]

        def quarter(index, columns, pre):
            value, slope = gelu_parts(pre)
            value = value.astype(BF16)
            lanes = piece_lanes(index, columns, hidden)
            g_ref[:, lanes] = value
            slope_ref[:, lanes] = slope.astype(BF16)
            below = slice(width + columns.start, width + columns.stop)
            total_ref[...] = total_ref[...] + dot(value, weights_ref[index, below, :])

        over_pieces(hidden, hidden_of, quarter)
        normed, inverse = normed_of(total_ref[...])
        result_ref[...] = (normed * vec_ref[4] + vec_ref[5]).astype(BF16)
        grad = cot_ref[...].astype(F32)
        grad_last = norm_back(grad, normed, inverse, vec_ref[4])
        dlast_ref[...] = grad_last
        grad_ffn = grad_last.astype(BF16)
        df_ref[...] = grad_ffn
        total_ref[...] = grad_last

        def value_grad_of(index, columns):
            return dot_t(df_ref[...], weights_ref[index, width + columns.start:width + columns.stop, :])

        def quarter_back(index, columns, grad_value):
            lanes = piece_lanes(index, columns, hidden)
            grad_pre = (grad_value * slope_ref[:, lanes].astype(F32)).astype(BF16)
            du_ref[:, lanes] = grad_pre
            bgrad_ref[index:index + 1, columns] += column_sum(grad_pre)
            total_ref[...] = total_ref[...] + dot_t(grad_pre, weights_ref[index, :width, columns])

        over_pieces(hidden, value_grad_of, quarter_back)
        grad_second = total_ref[...]
        grad_cross = norm_back(grad_second, normed_c, inverse_c, cvec_ref[3:4, :])
        dh_ref[...] = grad_cross
        cross_low = grad_cross.astype(BF16)
        dcross_ref[...] = cross_low
        dmixed_ref[...] = dot_t(cross_low, out_ref[...]).astype(BF16)
        vgrad_ref[1:2, :] += column_sum(grad_ffn)
        vgrad_ref[4:5, :] += column_sum(grad * normed)
        vgrad_ref[5:6, :] += column_sum(grad)
        vgrad_ref[6:7, :] += column_sum(cross_low)
        vgrad_ref[7:8, :] += column_sum(grad_second * normed_c)
        vgrad_ref[8:9, :] += column_sum(grad_second)


def decoder_step(flag, mixed, sum1, stream, cot, g_in, h_in, memory_in, out_weight, vectors, cvec, ff_packs, bias):
    rows, width = stream.shape
    hidden = g_in.shape[1]
    return pl.pallas_call(
        decoder_kernel,
        grid_spec=pltpu.PrefetchScalarGridSpec(
            num_scalar_prefetch=1,
            grid=(rows // TB,),
            in_specs=[
                tokens(width, 1), tokens(width, 1), tokens(width, 1), tokens(width, 1), tokens(hidden, 0),
                tokens(width, 0), tokens(width, 0), fixed(out_weight.shape), fixed(vectors.shape), fixed(cvec.shape),
            ]
            + [anywhere()] * len(ff_packs)
            + [fixed(bias.shape)],
            out_specs=[
                tokens(width), tokens(hidden), tokens(width), tokens(hidden, 1), tokens(width, 1), tokens(width, 1),
                tokens(width, 1), tokens(width, 1), tokens(width, 1), fixed((16, width)), fixed(bias.shape),
            ],
            scratch_shapes=ff_scratch(ff_packs) + [pltpu.VMEM((TB, hidden), BF16), pltpu.VMEM((TB, width), F32)],
        ),
        out_shape=[
            jax.ShapeDtypeStruct((rows, width), BF16),
            jax.ShapeDtypeStruct((rows, hidden), BF16),
            jax.ShapeDtypeStruct((rows, width), BF16),
            jax.ShapeDtypeStruct((rows, hidden), BF16),
            jax.ShapeDtypeStruct((rows, width), BF16),
            jax.ShapeDtypeStruct((rows, width), BF16),
            jax.ShapeDtypeStruct((rows, width), BF16),
            jax.ShapeDtypeStruct((rows, width), F32),
            jax.ShapeDtypeStruct((rows, width), F32),
            jax.ShapeDtypeStruct((16, width), F32),
            jax.ShapeDtypeStruct(bias.shape, F32),
        ],
        compiler_params=params(),
        cost_estimate=cost(2 * rows * width * (2 * width + 4 * hidden), 40 * rows * width),
        name="decoder_step",
    )(flag, mixed, sum1, stream, cot, g_in, h_in, memory_in, out_weight, vectors, cvec, *ff_packs, bias)


def backward_kernel(
    flag_ref, cot_ref, dmem_ref, sum1_ref, sum2_ref, slope_ref,
    dh_in, dq_in, dlast_in, du_in, df_in, vgrad_in, bgrad_in,
    out_ref, cross_ref, vec_ref, ff0, ff1, ff2, ff3,
    du_ref, df_ref, da_ref, dmixed_ref, dres_ref, vgrad_ref, bgrad_ref, dfirst_ref, weights_ref, sems,
):
    width = cot_ref.shape[1]
    hidden = ff0.shape[1]
    wait = fetch_packs((ff0, ff1, ff2, ff3), weights_ref, sems, flag_ref[0] == 0)
    at_start = pl.program_id(0) == 0
    is_dec = flag_ref[0] == 1

    @pl.when(at_start & is_dec)
    def _():
        vgrad_ref[...] = vgrad_in[...]
        bgrad_ref[...] = bgrad_in[...]

    @pl.when(at_start & jnp.logical_not(is_dec))
    def _():
        vgrad_ref[...] = jnp.zeros(vgrad_ref.shape, F32)
        bgrad_ref[...] = jnp.zeros(bgrad_ref.shape, F32)

    @pl.when(is_dec)
    def _():
        du_ref[...] = du_in[...]
        df_ref[...] = df_in[...]
        dres_ref[...] = dlast_in[...]
        dfirst_ref[...] = dh_in[...] + dot_t(dq_in[...], cross_ref[...])

    @pl.when(jnp.logical_not(is_dec))
    def _():
        grad = cot_ref[...].astype(F32) + dmem_ref[...].astype(F32)
        normed, inverse = normed_of(sum2_ref[...])
        grad_last = norm_back(grad, normed, inverse, vec_ref[4])
        dres_ref[...] = grad_last
        grad_ffn = grad_last.astype(BF16)
        df_ref[...] = grad_ffn
        dfirst_ref[...] = grad_last
        wait()

        def value_grad_of(index, columns):
            return dot_t(df_ref[...], weights_ref[index, width + columns.start:width + columns.stop, :])

        def quarter_back(index, columns, grad_value):
            lanes = piece_lanes(index, columns, hidden)
            grad_pre = (grad_value * slope_ref[:, lanes].astype(F32)).astype(BF16)
            du_ref[:, lanes] = grad_pre
            bgrad_ref[index:index + 1, columns] += column_sum(grad_pre)
            dfirst_ref[...] = dfirst_ref[...] + dot_t(grad_pre, weights_ref[index, :width, columns])

        over_pieces(hidden, value_grad_of, quarter_back)
        vgrad_ref[1:2, :] += column_sum(grad_ffn)
        vgrad_ref[4:5, :] += column_sum(grad * normed)
        vgrad_ref[5:6, :] += column_sum(grad)

    grad_first = dfirst_ref[...]
    normed, inverse = normed_of(sum1_ref[...])
    grad_in = norm_back(grad_first, normed, inverse, vec_ref[2])
    low = grad_in.astype(BF16)
    da_ref[...] = low
    dmixed_ref[...] = dot_t(low, out_ref[...]).astype(BF16)
    dres_ref[...] = dres_ref[...] + grad_in
    vgrad_ref[0:1, :] += column_sum(low)
    vgrad_ref[2:3, :] += column_sum(grad_first * normed)
    vgrad_ref[3:4, :] += column_sum(grad_first)


def backward_step(
    flag, cot, dmem, sum1, sum2, slope, dh, dq, dlast, du, df, vgrad, bgrad, out_weight, cross_query, vectors, ff_packs
):
    rows, width = cot.shape
    hidden = du.shape[1]
    return pl.pallas_call(
        backward_kernel,
        grid_spec=pltpu.PrefetchScalarGridSpec(
            num_scalar_prefetch=1,
            grid=(rows // TB,),
            in_specs=[
                tokens(width, 0), tokens(width, 0), tokens(width), tokens(width, 0), tokens(hidden, 0),
                tokens(width, 1), tokens(width, 1), tokens(width, 1), tokens(hidden, 1), tokens(width, 1),
                fixed(vgrad.shape), fixed(bgrad.shape),
                fixed(out_weight.shape), fixed(cross_query.shape), fixed(vectors.shape),
            ]
            + [anywhere()] * len(ff_packs),
            out_specs=[
                tokens(hidden), tokens(width), tokens(width), tokens(width), tokens(width),
                fixed(vgrad.shape), fixed(bgrad.shape),
            ],
            scratch_shapes=[pltpu.VMEM((TB, width), F32)] + ff_scratch(ff_packs),
        ),
        out_shape=[
            jax.ShapeDtypeStruct((rows, hidden), BF16),
            jax.ShapeDtypeStruct((rows, width), BF16),
            jax.ShapeDtypeStruct((rows, width), BF16),
            jax.ShapeDtypeStruct((rows, width), BF16),
            jax.ShapeDtypeStruct((rows, width), F32),
            jax.ShapeDtypeStruct(vgrad.shape, F32),
            jax.ShapeDtypeStruct(bgrad.shape, F32),
        ],
        compiler_params=params(),
        cost_estimate=cost(2 * rows * width * (width + 2 * hidden), 40 * rows * width),
        name="backward_step",
    )(
        flag, cot, dmem, sum1, sum2, slope, dh, dq, dlast, du, df, vgrad, bgrad,
        out_weight, cross_query, vectors, *ff_packs,
    )


def input_kernel(dres_ref, *refs):
    *parts, weight_ref, dx_ref = refs
    total = dres_ref[...]
    at = 0
    for part in parts:
        wide = part.shape[1]
        total = total + dot_t(part[...], weight_ref[:, at:at + wide])
        at += wide
    dx_ref[...] = total.astype(BF16)


def input_step(dres, parts, weight):
    rows, width = dres.shape
    block = 256
    spec = lambda v: pl.BlockSpec((block, v.shape[1]), lambda i: (i, 0))
    return pl.pallas_call(
        input_kernel,
        grid=(rows // block,),
        in_specs=[spec(v) for v in (dres, *parts)] + [fixed(weight.shape)],
        out_specs=spec(dres),
        out_shape=jax.ShapeDtypeStruct((rows, width), BF16),
        compiler_params=params(),
        cost_estimate=cost(6 * rows * width * width, 12 * rows * width),
        name="input_step",
    )(dres, *parts, weight)


def finish_kernel(attn_ref, qkv_ref, out_ref, bias_ref, hidden_ref, vectors_ref):
    width, lane = qkv_ref.shape[1:]
    for index in range(3):
        qkv_ref[index] = attn_ref[index * width:(index + 1) * width, :].astype(F32)
    for index in range(width // lane):
        at = 3 * width + index * lane
        out_ref[:, index * lane:(index + 1) * lane] = attn_ref[at:at + lane, :].astype(F32)
    rows = attn_ref[4 * width:, :].astype(F32)
    bias_ref[...] = rows[0:2]
    for index in range(hidden_ref.shape[1] // lane):
        hidden_ref[:, index * lane:(index + 1) * lane] = rows[2 + index:3 + index]
    count = width // lane
    for index in range(6):
        for part in range(count):
            row = 16 + index * count + part
            vectors_ref[index, :, part * lane:(part + 1) * lane] = rows[row:row + 1]


def finish_feed_forward_kernel(ff_ref, ffin_ref, ffout_ref):
    width = ffin_ref.shape[0]
    ffin_ref[...] = ff_ref[:width, :].astype(F32)
    ffout_ref[...] = ff_ref[width:, :].astype(F32)


def finish_feed_forward(ff_total, hidden):
    width = ff_total.shape[1]
    shapes = [(width, hidden), (hidden, width)]
    return pl.pallas_call(
        finish_feed_forward_kernel,
        grid=(1,),
        in_specs=[fixed(ff_total.shape)],
        out_specs=[fixed(shape) for shape in shapes],
        out_shape=[jax.ShapeDtypeStruct(shape, F32) for shape in shapes],
        compiler_params=params(),
        cost_estimate=cost(0, 20 * width * width),
        name="finish_feed_forward",
    )(ff_total)


def finish(attn_total, width, hidden):
    lane = attn_total.shape[1]
    shapes = [(3, width, lane), (lane, width), (2, lane), (1, hidden), (6, 1, width)]
    return pl.pallas_call(
        finish_kernel,
        grid=(1,),
        in_specs=[fixed(attn_total.shape)],
        out_specs=[fixed(shape) for shape in shapes],
        out_shape=[jax.ShapeDtypeStruct(shape, F32) for shape in shapes],
        compiler_params=params(),
        cost_estimate=cost(0, 20 * width * width),
        name="finish",
    )(attn_total)


def flipped(value, bits, section=None):
    count = lax.axis_size("tensor")
    if section is None:
        return lax.ppermute(value, "tensor", [(t, t ^ bits) for t in range(count)])
    base = section * count
    return lax.ppermute(value, ("pipe", "tensor"), [(base + t, base + (t ^ bits)) for t in range(count)])


def across(value, source, active):
    count = lax.axis_size("tensor")
    other = 1 - source
    pairs = [(source * count + t, other * count + t) for t in range(active)]
    return lax.ppermute(value, ("pipe", "tensor"), pairs)


def plus(own, received):
    return (own.astype(F32) + received.astype(F32)).astype(BF16)


def along_dp(part, level, section=None):
    count = lax.axis_size("dp")
    if section is None:
        return lax.ppermute(part, "dp", [(i, i ^ (1 << level)) for i in range(count)])
    base = section * count
    return lax.ppermute(part, ("pipe", "dp"), [(base + i, base + (i ^ (1 << level))) for i in range(count)])


def summed_whole(value, level, section=None, behind=()):
    return plus(after(value, *behind), along_dp(value, level, section))


def dp_bit(level):
    return lax.shift_right_logical(lax.axis_index("dp"), level) & 1


def halved(value, level, section=None, behind=()):
    rows = value.shape[0] // 2
    mine = dp_bit(level)
    got = along_dp(lax.dynamic_slice_in_dim(value, (1 - mine) * rows, rows, 0), level, section)
    return plus(lax.dynamic_slice_in_dim(after(value, *behind), mine * rows, rows, 0), got)


def doubled(value, level, section=None, behind=()):
    other = along_dp(value, level, section)
    upper = dp_bit(level) == 1
    value = after(value, *behind)
    return jnp.concatenate([jnp.where(upper, other, value), jnp.where(upper, value, other)], 0)


def after(value, *others):
    return lax.optimization_barrier((value, *others))[0]


def to_rows(shard):
    count = lax.axis_size("tensor")
    shard = jnp.pad(shard, ((0, count - shard.shape[0]), (0, 0), (0, 0)))
    out = lax.all_to_all(shard, "tensor", 0, 0, tiled=True)
    return out.reshape(count * shard.shape[1], shard.shape[2])


def from_rows(row, row_count):
    count = lax.axis_size("tensor")
    parts = row.reshape(count, row.shape[0] // count, row.shape[1])
    return lax.all_to_all(parts, "tensor", 0, 0, tiled=True)[:row_count]


def shards(
    inputs, cotangent, segments, pads, self_qkv, self_bias, self_out, ff_in, ff_bias, ff_out, vectors,
    cross_q, cross_kv, cross_out, cross_small, cross_gain,
):
    section = lax.axis_index("pipe").astype(jnp.int32)
    place = lax.axis_index("tensor").astype(jnp.int32)
    count = lax.axis_size("tensor")
    row_count = inputs.shape[1]
    decoder = section == 1
    flag, place_flag = section[None], place[None]
    width = inputs.shape[3]
    lane = self_qkv.shape[3]
    hidden = ff_in.shape[2]
    half = width // 2
    row = jnp.minimum(place, row_count - 1)

    attn_own, cross_half = first_packs(
        jnp.transpose(self_qkv[0], (1, 0, 2)), self_out[0], self_bias[0], ff_bias, cross_q,
        jnp.transpose(cross_kv, (1, 0, 2)), cross_out, cross_small, cross_gain[None],
    )
    attn_far, attn_near = flipped(attn_own, 2), flipped(attn_own, 1)
    stream = to_rows(after(inputs[0], attn_own))
    slots = jnp.concatenate(
        [
            lax.dynamic_index_in_dim(segments, row, 1, False),
            lax.dynamic_slice_in_dim(pads[0], row, 1, 0),
        ],
        0,
    )
    attn_packs = [attn_own, attn_near, attn_far, flipped(attn_far, 1)]
    other_half = across(cross_half, 0, count)
    ff_own = after(jnp.concatenate([ff_in[0], ff_out[0]], 0), stream, attn_far)
    ff_far, ff_near = flipped(ff_own, 2), flipped(ff_own, 1)
    vector_rows = jnp.transpose(vectors, (1, 0, 2))

    qkv, qkv_weight, out_weight, hidden_bias, own_code, key_code, target_code, source_code, self_bounds, cross_bounds = (
        query_key_value(flag, stream, slots, attn_packs)
    )
    parts = ((qkv, 0), (qkv, 1), (qkv, 2))
    self_codes, cross_codes = (own_code, key_code), (target_code, source_code)
    mixed, totals = attend_forward(self_bounds, self_codes, width, *parts)
    cross_own = jnp.concatenate([after(other_half, mixed), cross_half], 0)
    cross_far, cross_near = flipped(cross_own, 2, 1), flipped(cross_own, 1, 1)
    ff_packs = [ff_own, ff_near, ff_far, flipped(after(ff_far, cross_own), 1)]
    sum1, first_low, g_enc, slope, sum2, memory = encoder_forward(
        flag, mixed, stream, out_weight, vector_rows, ff_packs, hidden_bias
    )
    memory_in = across(memory, 0, row_count)
    cross_packs = [cross_own, cross_near, cross_far, flipped(after(cross_far, memory), 1, 1)]
    cot_row = to_rows(after(cotangent[0], memory))

    cross_query, cross_pair, cross_out_weight, cvec = cross_unpack(place_flag, cross_packs)
    cross_made = cross_project(first_low, memory_in, cross_query, cross_pair, cvec)
    cross_parts = ((cross_made, 0), (cross_made, 1), (cross_made, 2))
    cross_mixed, cross_totals = attend_forward(cross_bounds, cross_codes, width, *cross_parts)
    result, g_all, z_all, du_dec, df_dec, dcross, dcross_mixed, dh_dec, dlast_dec, vgrad_dec, bgrad_dec = decoder_step(
        flag, cross_mixed, sum1, stream, cot_row, g_enc, first_low, memory,
        cross_out_weight, vector_rows, cvec, ff_packs, hidden_bias,
    )
    dq_cross, dk_cross, dv_cross, dmemory = attend_backward(
        cross_bounds, cross_codes, *cross_parts, dcross_mixed, cross_totals, cross_pair
    )
    dmemory_in = across(dmemory, 1, row_count)
    cross_grads = attention_grads(
        True, place_flag, first_low, memory_in, (after(dq_cross, dmemory), dk_cross, dv_cross), cross_mixed, dcross,
        vgrad_dec, bgrad_dec, lane,
    )
    cross_far = plus(after(cross_grads[2], dmemory_in), flipped(cross_grads[3], 1, 1))
    cross_got = flipped(cross_grads[1], 1, 1)

    du_all, df_all, da, dmixed, dres, vgrad, bgrad = backward_step(
        flag, cot_row, dmemory_in, sum1, sum2, slope, dh_dec, after(dq_cross, cross_far, cross_grads[1]), dlast_dec,
        du_dec, df_dec, vgrad_dec, bgrad_dec, out_weight, cross_query, vector_rows, ff_packs,
    )
    cross_near = plus(after(cross_grads[0], da), cross_got)
    cross_part = plus(cross_near, flipped(cross_far, 2, 1))
    levels = range(lax.axis_size("dp").bit_length() - 1)
    ff_third, ff_second = feed_forward_grads(after(z_all, cross_part), du_all, g_all, df_all, 3, hidden)
    ff_first, ff_zeroth = feed_forward_grads(after(z_all, ff_second), du_all, g_all, df_all, 1, hidden)
    ff_far = plus(after(ff_second, ff_zeroth), flipped(ff_third, 1))
    ff_near = plus(after(ff_zeroth, ff_far), flipped(ff_first, 1))
    dqkv = attend_backward(self_bounds, self_codes, *parts, after(dmixed, ff_near), totals)
    cross_total = halved(cross_part, 0, 1, (dqkv[0],))
    ff_part = plus(after(ff_near, dqkv[0], cross_total), flipped(ff_far, 2))
    attn_grads = attention_grads(
        False, place_flag, stream, stream, (after(dqkv[0], ff_part), *dqkv[1:]), mixed, da, vgrad, bgrad, lane
    )
    ff_total = halved(ff_part, 0, behind=(attn_grads[3],))
    for level in levels[1:]:
        cross_total = halved(cross_total, level, 1, (ff_total,))
    attn_far = plus(after(attn_grads[2], ff_total, cross_total), flipped(attn_grads[3], 1))
    attn_near = plus(after(attn_grads[0], attn_far), flipped(attn_grads[1], 1))
    dx = input_step(after(dres, attn_near), dqkv, qkv_weight)
    section_out = from_rows(after(result, dx), row_count)[None]
    for level in levels[1:]:
        ff_total = halved(ff_total, level, behind=(dx,))
    cross_total = doubled(cross_total, levels[-1], 1, (ff_total,))
    attn_part = plus(after(attn_near, ff_total, cross_total), flipped(attn_far, 2))
    for level in reversed(levels[:-1]):
        cross_total = doubled(cross_total, level, 1, (attn_part,))
    cross_other = across(cross_total, 1, count)
    ff_total = doubled(ff_total, levels[-1], behind=(attn_part, section_out, cross_total))
    attn_total = halved(attn_part, 0, behind=(ff_total,))
    input_grad = from_rows(after(dx, attn_total), row_count).astype(F32)[None]
    for level in levels[1:]:
        attn_total = halved(attn_total, level, behind=(cross_total,))
    for level in reversed(levels[:-1]):
        ff_total = doubled(ff_total, level, behind=(attn_total,))
    attn_total = doubled(attn_total, levels[-1], behind=(ff_total, input_grad))
    cross_total, cross_other = after((cross_total, cross_other), attn_total)

    own, other = cross_total.astype(F32), cross_other.astype(F32)

    def halves(at):
        return jnp.where(decoder, own[at + half:at + 2 * half], other[at:at + half])

    cross_pair_grad = jnp.stack([halves(width), halves(2 * width)], 1)
    cross_out_grad = jnp.transpose(halves(3 * width).reshape(half // lane, lane, lane), (1, 0, 2)).reshape(lane, half)
    own_rows, other_rows = (v[4 * width:4 * width + 5 * count].reshape(5, width) for v in (own, other))
    small_grad = jnp.where(decoder, jnp.stack([own_rows[2], own_rows[4]]), other_rows[:2])
    gain_grad = jnp.where(decoder, own_rows[3, half:], other_rows[3, :half])
    cross_first, cross_last = halves(0), (cross_pair_grad, cross_out_grad, small_grad, gain_grad)
    ffin_grad, ffout_grad = finish_feed_forward(ff_total, hidden)
    for level in reversed(levels[:-1]):
        attn_total = doubled(attn_total, level, behind=(cross_first, *cross_last, ffin_grad))
    qkv_grad, out_grad, bias_grad, hidden_grad, vectors_grad = finish(attn_total, width, hidden)
    return (
        section_out,
        input_grad,
        jnp.transpose(qkv_grad, (1, 0, 2))[None],
        bias_grad[None],
        out_grad[None],
        ffin_grad[None],
        hidden_grad,
        ffout_grad[None],
        jnp.transpose(vectors_grad, (1, 0, 2)),
        cross_first,
        *cross_last,
    )


def solution(mesh):
    token_spec = P("pipe", "dp", "tensor", None)
    weights = (
        P("pipe", None, None, "tensor"),
        P("pipe", None, "tensor"),
        P("pipe", "tensor", None),
        P("pipe", None, "tensor"),
        P("pipe", "tensor"),
        P("pipe", "tensor", None),
        P("pipe", None, None),
        P("pipe", "tensor"),
        P("pipe", None, "tensor"),
        P("tensor", "pipe"),
        P("pipe", None),
        P("pipe"),
    )
    return jax.shard_map(
        shards,
        mesh=mesh,
        in_specs=(token_spec, token_spec, P(None, "dp", None), P("pipe", "dp", None)) + weights,
        out_specs=(token_spec, token_spec) + weights,
        check_vma=False,
    )
```

```python
import functools

import jax
import jax.numpy as jnp
from jax import lax
from jax.experimental import pallas as pl
from jax.experimental.pallas import tpu as pltpu
from jax.sharding import PartitionSpec as P

HEAD_DIM = 64
EPSILON = 1e-05
MASKED = -1e30
SEGS = 8
QF = 256
QB = 256
TB = 512
PIECES = 1
PAIR = 2 * HEAD_DIM
GELU_C = 0.7978845608028654
GELU_A = 0.044715
VMEM_LIMIT = 56 * 1024 * 1024
SMALL_LIMIT = 32 * 1024 * 1024
F32 = jnp.float32
BF16 = jnp.bfloat16


def dot(left, right):
    return jnp.dot(left, right, preferred_element_type=F32)


def dot_t(left, right):
    return lax.dot_general(left, right, (((1,), (1,)), ((), ())), preferred_element_type=F32)


def dot_tl(left, right):
    return lax.dot_general(left, right, (((0,), (0,)), ((), ())), preferred_element_type=F32)


def normed_of(values):
    center = values - jnp.mean(values, -1, keepdims=True)
    inverse = lax.rsqrt(jnp.mean(center * center, -1, keepdims=True) + EPSILON)
    return center * inverse, inverse


def norm_back(grad, normed, inverse, gain):
    scaled = grad * gain
    mean_scaled = jnp.mean(scaled, -1, keepdims=True)
    mean_both = jnp.mean(scaled * normed, -1, keepdims=True)
    return (scaled - mean_scaled - normed * mean_both) * inverse


def column_sum(values):
    return jnp.sum(values.astype(F32), 0, keepdims=True)


def gelu_parts(pre):
    squared = pre * pre
    half = 0.5 * jnp.tanh(pre * (GELU_C + (GELU_C * GELU_A) * squared)) + 0.5
    slope = half + (pre * (half - half * half)) * (2.0 * GELU_C + (6.0 * GELU_C * GELU_A) * squared)
    return pre * half, slope


def cost(flops, moved):
    return pl.CostEstimate(flops=int(flops) // 64, bytes_accessed=int(moved) // 64, transcendentals=0)


def params(limit=VMEM_LIMIT):
    return pltpu.CompilerParams(dimension_semantics=("arbitrary",), vmem_limit_bytes=limit)


def find_segments(section, slots_ref, own_ref, key_ref, target_ref, source_ref, self_ref, cross_ref):
    length = slots_ref.shape[1]
    source = slots_ref[0:1, :].astype(F32)
    target = slots_ref[1:2, :].astype(F32)
    own = jnp.where(section == 1, target, source)
    own_ref[...] = own
    key_ref[...] = jnp.where(slots_ref[2:3, :] == 0, own, -1.0)
    target_ref[...] = target
    source_ref[...] = source

    def starts(segments):
        found = [jnp.int32(0)]
        for index in range(1, SEGS):
            found.append(jnp.sum(jnp.where(segments < float(index), 1.0, 0.0)).astype(jnp.int32))
        return found + [jnp.int32(length)]

    source_starts, target_starts = starts(source), starts(target)
    for index in range(SEGS):
        own_start = jnp.where(section == 1, target_starts[index], source_starts[index])
        own_end = jnp.where(section == 1, target_starts[index + 1], source_starts[index + 1])
        self_ref[index] = own_start
        self_ref[16 + index] = own_start
        self_ref[32 + index] = own_end
        cross_ref[index] = target_starts[index]
        cross_ref[16 + index] = source_starts[index]
        cross_ref[32 + index] = source_starts[index + 1]
    self_ref[48] = jnp.int32(1)
    self_ref[49] = section
    self_ref[50] = jnp.int32(1)
    cross_ref[48] = jnp.int32(0)
    cross_ref[49] = jnp.int32(0)
    cross_ref[50] = section


def half_masked(values, side):
    lane = lax.broadcasted_iota(jnp.int32, values.shape, 1)
    return jnp.where((lane >= HEAD_DIM) == bool(side), values, jnp.zeros_like(values))


def key_window(bounds, block, block_rows):
    first = block * block_rows
    last = first + (block_rows - 1)
    low, high = jnp.int32(0), jnp.int32(0)
    for index in range(SEGS):
        low = jnp.where(bounds[index] <= first, bounds[16 + index], low)
        high = jnp.where(bounds[index] <= last, bounds[32 + index], high)
    high = jnp.where(bounds[49] == 1, jnp.minimum(high, last + 1), high)
    low_block = lax.shift_right_logical(low, 7)
    high_block = lax.shift_right_logical(high + 127, 7)
    return low_block, jnp.where(bounds[50] == 1, high_block - low_block, 0)


def by_size(bounds, block, block_rows, key_blocks, sizes, body):
    low_block, needed = key_window(bounds, block, block_rows)
    below = 0
    for size in sizes:
        size = min(size, key_blocks)
        if size == below:
            continue

        @pl.when((needed > below) & (needed <= size))
        def _(size=size):
            start = jnp.minimum(low_block, key_blocks - size) * 128
            body(size, pl.multiple_of(start, 128))

        below = size


def as_columns(row):
    parts = []
    for at in range(0, row.shape[1], 128):
        parts.append(jnp.broadcast_to(row[:, at:at + 128], (128, 128)).T)
    return jnp.concatenate(parts, 0)


def window_bias(bounds, block, block_rows, start, key_code, qcode_ref):
    key_at = start + lax.broadcasted_iota(jnp.int32, key_code.shape, 0)
    tiles = []
    for at in range(0, block_rows, 128):
        query_at = block * block_rows + at + lax.broadcasted_iota(jnp.int32, (1, 128), 1)
        limit = jnp.where(bounds[49] == 1, query_at, jnp.int32(1 << 30))
        same_at = jnp.where(bounds[48] == 1, query_at, -1)
        opened = (key_code == qcode_ref[:, at:at + 128]) & (key_at <= limit)
        tiles.append(jnp.where(opened | (key_at == same_at), 0.0, MASKED))
    return jnp.concatenate(tiles, 1)


def attend_forward_kernel(bounds, q_ref, k_ref, v_ref, qcode_ref, kcode_ref, mixed_ref, total_ref):
    block = pl.program_id(0)
    heads = q_ref.shape[1] // HEAD_DIM
    key_blocks = k_ref.shape[0] // 128
    own_code = as_columns(qcode_ref[...])
    query_at = block * QF + lax.broadcasted_iota(jnp.int32, (QF, 128), 0)
    limit = jnp.where(bounds[49] == 1, query_at, jnp.int32(1 << 30))
    same_at = jnp.where(bounds[48] == 1, query_at, -1)
    lane = lax.broadcasted_iota(jnp.int32, (QF, 128), 1)

    def body(size, start):
        window = pl.ds(start, size * 128)
        tiles = []
        for tile in range(size):
            at = start + tile * 128
            key_at = at + lane
            opened = (own_code == kcode_ref[:, pl.ds(pl.multiple_of(at, 128), 128)]) & (key_at <= limit)
            tiles.append(jnp.where(opened | (key_at == same_at), 0.0, MASKED))
        bias = jnp.concatenate(tiles, 1)

        def two_pairs(index, columns):
            lanes = [pl.ds(pl.multiple_of((2 * index + at) * PAIR, PAIR), PAIR) for at in range(2)]
            scores = []
            for at in range(2):
                queries, keys = q_ref[:, lanes[at]], k_ref[window, lanes[at]]
                scores.append([dot_t(half_masked(queries, side), keys) + bias for side in range(2)])
            for at in range(2):
                values = v_ref[window, lanes[at]]
                out = None
                for side in range(2):
                    top = jnp.max(scores[at][side], -1, keepdims=True)
                    weights = jnp.exp(scores[at][side] - top)
                    total = jnp.sum(weights, -1, keepdims=True)
                    part = dot(weights.astype(BF16), half_masked(values, side)) * (1.0 / total)
                    out = part if out is None else out + part
                    columns = jnp.where(lane == (2 * index + at) * 2 + side, top + jnp.log(total), columns)
                mixed_ref[:, lanes[at]] = out.astype(BF16)
            return columns

        columns = lax.fori_loop(0, heads // 4, two_pairs, jnp.zeros((QF, 128), F32))
        total_ref[...] = columns.T[:heads]

    by_size(bounds, block, QF, key_blocks, (2, 3, 4, 5, 6, 8), body)


def attend_forward(bounds, codes, width, queries, keys, values):
    (q_array, q_at), (k_array, k_at), (v_array, v_at) = queries, keys, values
    rows = q_array.shape[0]
    heads = width // HEAD_DIM
    whole = lambda at: (lambda i, *_: (0, at))
    return pl.pallas_call(
        attend_forward_kernel,
        grid_spec=pltpu.PrefetchScalarGridSpec(
            num_scalar_prefetch=1,
            grid=(rows // QF,),
            in_specs=[
                pl.BlockSpec((QF, width), lambda i, *_: (i, q_at)),
                pl.BlockSpec((rows, width), whole(k_at)),
                pl.BlockSpec((rows, width), whole(v_at)),
                pl.BlockSpec((1, QF), lambda i, *_: (0, i)),
                pl.BlockSpec((1, rows), whole(0)),
            ],
            out_specs=[
                pl.BlockSpec((QF, width), lambda i, *_: (i, 0)),
                pl.BlockSpec((heads, QF), lambda i, *_: (0, i)),
            ],
        ),
        out_shape=[
            jax.ShapeDtypeStruct((rows, width), BF16),
            jax.ShapeDtypeStruct((heads, rows), F32),
        ],
        compiler_params=params(SMALL_LIMIT),
        cost_estimate=cost(4 * rows * 512 * width * 2, 8 * rows * width),
        name="attend_forward",
    )(bounds, q_array, k_array, v_array, *codes)


def attend_backward_kernel(has_weight, first_head, bounds, q_ref, k_ref, v_ref, grad_ref, total_ref, qcode_ref, kcode_ref, *refs):
    if has_weight:
        weight_ref, dq_ref, dk_ref, dv_ref, dmem_ref, kcol_ref, dkacc_ref, dvacc_ref = refs
    else:
        dq_ref, dk_ref, dv_ref, kcol_ref, dkacc_ref, dvacc_ref = refs
    block = pl.program_id(0)
    width = q_ref.shape[1]
    heads = width // HEAD_DIM
    key_blocks = k_ref.shape[0] // 128

    @pl.when(block == 0)
    def _():
        dkacc_ref[...] = jnp.zeros(dkacc_ref.shape, F32)
        dvacc_ref[...] = jnp.zeros(dvacc_ref.shape, F32)
        kcol_ref[...] = as_columns(kcode_ref[...])

    def body(size, start):
        window = pl.ds(start, size * 128)
        bias = window_bias(bounds, block, QB, start, kcol_ref[window, :], qcode_ref)

        def two_pairs(index, carry):
            prepared = []
            for at in range(2):
                pair = 2 * index + at
                lanes = pl.ds(pl.multiple_of(pair * PAIR, PAIR), PAIR)
                queries, grads = q_ref[:, lanes], grad_ref[:, lanes]
                keys, values = k_ref[window, lanes], v_ref[window, lanes]
                query_halves = [half_masked(queries, side) for side in range(2)]
                grad_halves = [half_masked(grads, side) for side in range(2)]
                products = [
                    (dot_t(keys, query_halves[side]) + bias, dot_t(values, grad_halves[side])) for side in range(2)
                ]
                prepared.append((pair, lanes, keys, query_halves, grad_halves, products))
            for pair, lanes, keys, query_halves, grad_halves, products in prepared:
                dq = dk = dv = None
                for side in range(2):
                    scores, grad_weights = products[side]
                    weights = jnp.exp(scores - total_ref[pl.ds(first_head + pair * 2 + side, 1), :])
                    delta = jnp.sum(weights * grad_weights, 0, keepdims=True)
                    grad_scores = (weights * (grad_weights - delta)).astype(BF16)
                    made = (
                        dot_tl(grad_scores, half_masked(keys, side)),
                        dot(grad_scores, query_halves[side]),
                        dot(weights.astype(BF16), grad_halves[side]),
                    )
                    dq, dk, dv = made if dq is None else (dq + made[0], dk + made[1], dv + made[2])
                dkacc_ref[window, lanes] = dkacc_ref[window, lanes] + dk
                dvacc_ref[window, lanes] = dvacc_ref[window, lanes] + dv
                dq_ref[:, lanes] = (dq * HEAD_DIM ** (-0.5)).astype(BF16)
            return carry

        lax.fori_loop(0, heads // 4, two_pairs, 0)

    by_size(bounds, block, QB, key_blocks, (2, 3, 4, 5, 6, 8), body)

    @pl.when(block == pl.num_programs(0) - 1)
    def _():
        dk_ref[...] = dkacc_ref[...].astype(BF16)
        dv_ref[...] = dvacc_ref[...].astype(BF16)
        if has_weight:
            summed = dot_t(dk_ref[...], weight_ref[:, :width]) + dot_t(dv_ref[...], weight_ref[:, width:])
            dmem_ref[...] = summed.astype(BF16)


def attend_backward(bounds, codes, queries, keys, values, grad, totals, weight=None, part=(0, 1)):
    (q_array, q_at), (k_array, k_at), (v_array, v_at) = queries, keys, values
    index, count = part
    rows = grad.shape[0]
    heads = totals.shape[0]
    width = grad.shape[1] // count
    whole = lambda at: pl.BlockSpec((rows, width), lambda i, *_: (0, at * count + index))
    block = lambda at: pl.BlockSpec((QB, width), lambda i, *_: (i, at * count + index))
    extra = [] if weight is None else [weight]
    first = pl.BlockSpec((rows, width), lambda i, *_: (0, 0))
    return pl.pallas_call(
        functools.partial(attend_backward_kernel, weight is not None, index * heads // count),
        grid_spec=pltpu.PrefetchScalarGridSpec(
            num_scalar_prefetch=1,
            grid=(rows // QB,),
            in_specs=[
                block(q_at),
                whole(k_at),
                whole(v_at),
                block(0),
                pl.BlockSpec((heads, QB), lambda i, *_: (0, i)),
                pl.BlockSpec((1, QB), lambda i, *_: (0, i)),
                pl.BlockSpec((1, rows), lambda i, *_: (0, 0)),
            ]
            + [fixed(v.shape) for v in extra],
            out_specs=[pl.BlockSpec((QB, width), lambda i, *_: (i, 0))] + [first] * (2 + len(extra)),
            scratch_shapes=[
                pltpu.VMEM((rows, 128), F32),
                pltpu.VMEM((rows, width), F32),
                pltpu.VMEM((rows, width), F32),
            ],
        ),
        out_shape=[jax.ShapeDtypeStruct((rows, width), BF16)] * (3 + len(extra)),
        compiler_params=params(SMALL_LIMIT),
        cost_estimate=cost(10 * rows * 512 * width * 2, 16 * rows * width),
        name="attend_backward",
    )(bounds, q_array, k_array, v_array, grad, totals, *codes, *extra)


def first_packs_kernel(
    qkv_ref, out_ref, bias_ref, ffb_ref, query_ref, pair_ref, cout_ref, small_ref, gain_ref, pack_ref, half_ref
):
    width = qkv_ref.shape[1]
    lane = qkv_ref.shape[2]
    half = query_ref.shape[0]

    def columns(values):
        return [values[:, at:at + lane] for at in range(0, values.shape[1], lane)]

    def filled(rows):
        rest = jnp.zeros((16 - sum(part.shape[0] for part in rows), lane), F32)
        return jnp.concatenate([*rows, rest], 0).astype(BF16)

    for index in range(3):
        pack_ref[index * width:(index + 1) * width, :] = qkv_ref[index]
    for index, part in enumerate(columns(out_ref[...])):
        at = 3 * width + index * lane
        pack_ref[at:at + lane, :] = part
    bias = bias_ref[...]
    high = bias.astype(BF16).astype(F32)
    middle = (bias - high).astype(BF16).astype(F32)
    least = bias - high - middle
    pack_ref[4 * width:4 * width + 16, :] = filled([high, middle, least, *columns(ffb_ref[...].astype(F32))])
    half_ref[0:half, :] = query_ref[...]
    half_ref[half:2 * half, :] = pair_ref[0]
    half_ref[2 * half:3 * half, :] = pair_ref[1]
    for index, part in enumerate(columns(cout_ref[...])):
        at = 3 * half + index * lane
        half_ref[at:at + lane, :] = part
    small = small_ref[...].astype(F32)
    half_ref[4 * half:4 * half + 16, :] = filled(
        [*columns(small[0:1]), *columns(small[1:2]), *columns(gain_ref[...].astype(F32))]
    )


def first_packs(qkv, out_weight, bias, ff_bias, query, pair, cross_out, small, gain):
    width, lane = qkv.shape[1:]
    half = query.shape[0]
    operands = (qkv, out_weight, bias, ff_bias, query, pair, cross_out, small, gain)
    shapes = [(4 * width + 16, lane), (4 * half + 16, lane)]
    return pl.pallas_call(
        first_packs_kernel,
        grid=(1,),
        in_specs=[fixed(v.shape) for v in operands],
        out_specs=[fixed(shape) for shape in shapes],
        out_shape=[jax.ShapeDtypeStruct(shape, BF16) for shape in shapes],
        compiler_params=params(SMALL_LIMIT),
        cost_estimate=cost(0, 24 * width * lane),
        name="first_packs",
    )(*operands)


def query_key_value_kernel(
    flag_ref, x_ref, slots_ref, p0, p1, p2, p3, qkv_ref, weight_ref, out_ref, hidden_ref, *refs
):
    *found_refs, bias_ref = refs
    width = x_ref.shape[1]
    lane = p0.shape[1]

    @pl.when(pl.program_id(0) == 0)
    def _():
        find_segments(flag_ref[0], slots_ref, *found_refs)
        for index, pack in enumerate((p0, p1, p2, p3)):
            columns = slice(index * lane, (index + 1) * lane)
            for part in range(3):
                at = slice(part * width + index * lane, part * width + (index + 1) * lane)
                weight_ref[:, at] = pack[part * width:(part + 1) * width, :]
            for part in range(width // lane):
                at = 3 * width + part * lane
                out_ref[columns, part * lane:(part + 1) * lane] = pack[at:at + lane, :]
            rows = pack[4 * width:4 * width + 16, :].astype(F32)
            bias_ref[0:1, columns] = rows[0:1] + rows[2:3] + rows[4:5]
            bias_ref[1:2, columns] = rows[1:2] + rows[3:4] + rows[5:6]
            for part in range(width // lane):
                hidden_ref[index:index + 1, part * lane:(part + 1) * lane] = rows[6 + part:7 + part]

    made = dot(x_ref[...], weight_ref[...])
    scale = HEAD_DIM ** (-0.5)
    queries = (made[:, :width] + bias_ref[0:1, :]).astype(BF16).astype(F32) * scale
    qkv_ref[:, :width] = queries.astype(BF16)
    qkv_ref[:, width:2 * width] = made[:, width:2 * width].astype(BF16)
    qkv_ref[:, 2 * width:] = (made[:, 2 * width:] + bias_ref[1:2, :]).astype(BF16)


def query_key_value(flag, stream, slots, packs):
    rows, width = stream.shape
    line = jax.ShapeDtypeStruct((1, rows), F32)
    bounds = jax.ShapeDtypeStruct((64,), jnp.int32)
    return pl.pallas_call(
        query_key_value_kernel,
        grid_spec=pltpu.PrefetchScalarGridSpec(
            num_scalar_prefetch=1,
            grid=(rows // TB,),
            in_specs=[tokens(width), fixed(slots.shape)] + [fixed(pack.shape) for pack in packs],
            out_specs=[tokens(3 * width), fixed((width, 3 * width)), fixed((width, width)), fixed((len(packs), width))]
            + [fixed(line.shape)] * 4
            + [pl.BlockSpec(memory_space=pltpu.SMEM)] * 2,
            scratch_shapes=[pltpu.VMEM((8, width), F32)],
        ),
        out_shape=[
            jax.ShapeDtypeStruct((rows, 3 * width), BF16),
            jax.ShapeDtypeStruct((width, 3 * width), BF16),
            jax.ShapeDtypeStruct((width, width), BF16),
            jax.ShapeDtypeStruct((len(packs), width), F32),
        ]
        + [line] * 4
        + [bounds] * 2,
        compiler_params=params(SMALL_LIMIT),
        cost_estimate=cost(6 * rows * width * width, 10 * rows * width),
        name="query_key_value",
    )(flag, stream, slots, *packs)


def cross_project_kernel(h_ref, memory_ref, query_ref, pair_ref, cvec_ref, made_ref):
    width = h_ref.shape[1]
    queries = (dot(h_ref[...], query_ref[...]) + cvec_ref[0:1, :]).astype(BF16).astype(F32)
    made_ref[:, :width] = (queries * HEAD_DIM ** (-0.5)).astype(BF16)
    made = dot(memory_ref[...], pair_ref[...])
    made_ref[:, width:2 * width] = made[:, :width].astype(BF16)
    made_ref[:, 2 * width:] = (made[:, width:] + cvec_ref[1:2, :]).astype(BF16)


def cross_project(h, memory, query, pair, cvec):
    rows, width = h.shape
    operands = (h, memory, query, pair, cvec)
    return pl.pallas_call(
        cross_project_kernel,
        grid=(rows // TB,),
        in_specs=[tokens(width)] * 2 + [fixed(v.shape) for v in operands[2:]],
        out_specs=tokens(3 * width),
        out_shape=jax.ShapeDtypeStruct((rows, 3 * width), BF16),
        compiler_params=params(SMALL_LIMIT),
        cost_estimate=cost(6 * rows * width * width, 12 * rows * width),
        name="cross_project",
    )(*operands)


def cross_unpack_kernel(place_ref, p0, p1, p2, p3, query_ref, pair_ref, out_ref, cvec_ref):
    lane = p0.shape[1]
    length = p0.shape[0] // 2
    half = (length - 16) // 4
    width = 2 * half
    count = width // lane
    for index, pack in enumerate((p0, p1, p2, p3)):
        columns = slice(index * lane, (index + 1) * lane)
        for side in range(2):
            rows = slice(side * half, (side + 1) * half)
            base = side * length
            query_ref[rows, columns] = pack[base:base + half, :]
            pair_ref[rows, columns] = pack[base + half:base + 2 * half, :]
            pair_ref[rows, width + index * lane:width + (index + 1) * lane] = pack[base + 2 * half:base + 3 * half, :]
            for part in range(half // lane):
                at = base + 3 * half + part * lane
                to = side * half + part * lane
                out_ref[columns, to:to + lane] = pack[at:at + lane, :]
    first = p0[4 * half:4 * half + 16, :].astype(F32)
    second = p0[length + 4 * half:length + 4 * half + 16, :].astype(F32)
    at_row = lax.broadcasted_iota(jnp.int32, (16, lane), 0)
    for index in range(count):
        columns = slice(index * lane, (index + 1) * lane)
        for which in range(2):
            wanted = which * count + (place_ref[0] ^ index)
            cvec_ref[which:which + 1, columns] = jnp.sum(jnp.where(at_row == wanted, first, 0.0), 0, keepdims=True)
        cvec_ref[2:3, columns] = second[index:index + 1]
        cvec_ref[4:5, columns] = second[count + index:count + index + 1]
        side, part = (first, index) if index < count // 2 else (second, index - count // 2)
        cvec_ref[3:4, columns] = side[2 * count + part:2 * count + part + 1]
    cvec_ref[5:8, :] = jnp.zeros((3, width), F32)


def cross_unpack(place, packs):
    length, lane = packs[0].shape
    width = (length // 2 - 16) // 2
    return pl.pallas_call(
        cross_unpack_kernel,
        grid_spec=pltpu.PrefetchScalarGridSpec(
            num_scalar_prefetch=1,
            grid=(1,),
            in_specs=[fixed(pack.shape) for pack in packs],
            out_specs=[fixed((width, width)), fixed((width, 2 * width)), fixed((width, width)), fixed((8, width))],
        ),
        out_shape=[
            jax.ShapeDtypeStruct((width, width), BF16),
            jax.ShapeDtypeStruct((width, 2 * width), BF16),
            jax.ShapeDtypeStruct((width, width), BF16),
            jax.ShapeDtypeStruct((8, width), F32),
        ],
        compiler_params=params(SMALL_LIMIT),
        cost_estimate=cost(0, 16 * width * width),
        name="cross_unpack",
    )(place, *packs)


def rows_of(vector, rows, at_row, base, order=None):
    lane = rows.shape[1]
    for index in range(vector.shape[1] // lane):
        to = base + (index if order is None else (order ^ index))
        rows = rows + jnp.where(at_row == to, vector[:, index * lane:(index + 1) * lane], 0.0)
    return rows


def attention_grads_kernel(
    is_cross, parts, place_ref, aq_ref, akv_ref, *refs
):
    width = aq_ref.shape[1]
    dq_refs, dk_refs, dv_refs = (refs[part * parts:(part + 1) * parts] for part in range(3))
    mixed_ref, da_ref, vgrad_ref, bgrad_ref, *packs, made_ref = refs[3 * parts:]
    lane = packs[0].shape[1]
    count = width // lane
    tail = packs[0].shape[0] - 4 * width
    akv = akv_ref if is_cross else aq_ref
    for part, (left, rights) in enumerate(((aq_ref, dq_refs), (akv, dk_refs), (akv, dv_refs))):
        for index, right in enumerate(rights):
            wide = width // parts
            made_ref[:, index * wide:(index + 1) * wide] = dot_tl(left[...], right[...]).astype(BF16)
        for index, pack in enumerate(packs):
            pack[part * width:(part + 1) * width, :] = made_ref[:, index * lane:(index + 1) * lane]
    made_ref[...] = dot_tl(mixed_ref[...], da_ref[...]).astype(BF16)
    for index, pack in enumerate(packs):
        for part in range(count):
            at = 3 * width + part * lane
            pack[at:at + lane, :] = made_ref[index * lane:(index + 1) * lane, part * lane:(part + 1) * lane]
    query_bias, value_bias = (
        jnp.concatenate([column_sum(ref[...]) for ref in some], 1) for some in (dq_refs, dv_refs)
    )
    at_row = lax.broadcasted_iota(jnp.int32, (tail, lane), 0)
    rows = jnp.zeros((tail, lane), F32)
    if is_cross:
        rows = rows_of(query_bias, rows, at_row, 0, place_ref[0])
        rows = rows_of(value_bias, rows, at_row, count, place_ref[0])
        for index in range(3):
            rows = rows_of(vgrad_ref[6 + index:7 + index, :], rows, at_row, (2 + index) * count)
    else:
        for index in range(6):
            rows = rows_of(vgrad_ref[index:index + 1, :], rows, at_row, 16 + index * count)
    for index, pack in enumerate(packs):
        own = rows
        if not is_cross:
            columns = slice(index * lane, (index + 1) * lane)
            own = own + jnp.where(at_row == 0, query_bias[:, columns], 0.0)
            own = own + jnp.where(at_row == 1, value_bias[:, columns], 0.0)
            own = rows_of(bgrad_ref[index:index + 1, :], own, at_row, 2)
        pack[4 * width:, :] = own.astype(BF16)


def attention_grads(is_cross, place, aq, akv, dqkv, mixed, da, vgrad, bgrad, lane):
    rows, width = aq.shape
    length = 4 * width + 64
    operands = (aq, akv, *dqkv, mixed, da, vgrad, bgrad)
    count = width // lane
    return pl.pallas_call(
        functools.partial(attention_grads_kernel, is_cross, len(dqkv) // 3),
        grid_spec=pltpu.PrefetchScalarGridSpec(
            num_scalar_prefetch=1,
            grid=(1,),
            in_specs=[fixed(v.shape) for v in operands],
            out_specs=[fixed((length, lane))] * count,
            scratch_shapes=[pltpu.VMEM((width, width), BF16)],
        ),
        out_shape=[jax.ShapeDtypeStruct((length, lane), BF16)] * count,
        compiler_params=params(),
        cost_estimate=cost(8 * rows * width * width, 14 * rows * width),
        name="cross_grads" if is_cross else "self_grads",
    )(place, *operands)


def feed_forward_grads_kernel(z_ref, du_ref, g_ref, df_ref, *packs):
    width = z_ref.shape[1]
    for index, pack in enumerate(packs):

        @pl.when(pl.program_id(0) == index)
        def _(pack=pack):
            pack[:width, :] = dot_tl(z_ref[...], du_ref[...]).astype(BF16)
            pack[width:, :] = dot_tl(g_ref[...], df_ref[...]).astype(BF16)


def feed_forward_grads(z, du, g, df, first, hidden):
    rows, width = z.shape
    quarter = pl.BlockSpec((rows, hidden), lambda i: (0, first - i))
    pack = (width + hidden, width)
    return pl.pallas_call(
        feed_forward_grads_kernel,
        grid=(2,),
        in_specs=[fixed(z.shape), quarter, quarter, fixed(df.shape)],
        out_specs=[fixed(pack)] * 2,
        out_shape=[jax.ShapeDtypeStruct(pack, BF16)] * 2,
        compiler_params=params(SMALL_LIMIT),
        cost_estimate=cost(8 * rows * width * hidden, 12 * rows * hidden),
        name="feed_forward_grads",
    )(z, du, g, df)


def tokens(width, section=None):
    if section is None:
        return pl.BlockSpec((TB, width), lambda i, *_: (i, 0))
    if section == 0:
        return pl.BlockSpec((TB, width), lambda i, flag: (i * (1 - flag[0]), 0))
    return pl.BlockSpec((TB, width), lambda i, flag: (i * flag[0], 0))


def anywhere():
    return pl.BlockSpec(memory_space=pl.ANY)


def ff_scratch(ff_packs):
    return [
        pltpu.VMEM((len(ff_packs),) + ff_packs[0].shape, BF16),
        pltpu.SemaphoreType.DMA((len(ff_packs),)),
    ]


def fetch_packs(packs, weights_ref, sems, wanted):
    started = (pl.program_id(0) == 0) & wanted

    @pl.when(started)
    def _():
        for index, pack in enumerate(packs):
            pltpu.make_async_copy(pack, weights_ref.at[index], sems.at[index]).start()

    def wait():
        @pl.when(started)
        def _():
            for index, pack in enumerate(packs):
                pltpu.make_async_copy(pack, weights_ref.at[index], sems.at[index]).wait()

    return wait


def over_pieces(hidden, first, then):
    piece = hidden // PIECES
    order = [(index, slice(at, at + piece)) for index in range(4) for at in range(0, hidden, piece)]
    made = first(*order[0])
    for here, ahead in zip(order, order[1:] + [None]):
        coming = None if ahead is None else first(*ahead)
        then(*here, made)
        made = coming


def piece_lanes(index, columns, hidden):
    return slice(index * hidden + columns.start, index * hidden + columns.stop)


def fixed(shape):
    return pl.BlockSpec(shape, lambda i, *_: (0,) * len(shape))


def encoder_forward_kernel(
    flag_ref, mixed_ref, x_ref, out_ref, vec_ref, ff0, ff1, ff2, ff3, bias_ref,
    *refs,
):
    sum1_ref, h_ref, g_ref, slope_ref, sum2_ref, memory_ref, weights_ref, sems = refs
    width = x_ref.shape[1]
    hidden = ff0.shape[1]
    is_enc = flag_ref[0] == 0
    wait = fetch_packs((ff0, ff1, ff2, ff3), weights_ref, sems, is_enc)
    stream = x_ref[...].astype(F32)
    summed = stream + (dot(mixed_ref[...], out_ref[...]) + vec_ref[0])
    sum1_ref[...] = summed
    first = normed_of(summed)[0] * vec_ref[2] + vec_ref[3]
    h_ref[...] = first.astype(BF16)
    wait()

    @pl.when(is_enc)
    def _():
        sum2_ref[...] = first + stream + vec_ref[1]

        def hidden_of(index, columns):
            return dot(h_ref[...], weights_ref[index, :width, columns]) + bias_ref[index:index + 1, columns]

        def quarter(index, columns, pre):
            value, slope = gelu_parts(pre)
            value = value.astype(BF16)
            lanes = piece_lanes(index, columns, hidden)
            g_ref[:, lanes] = value
            slope_ref[:, lanes] = slope.astype(BF16)
            below = slice(width + columns.start, width + columns.stop)
            sum2_ref[...] = sum2_ref[...] + dot(value, weights_ref[index, below, :])

        over_pieces(hidden, hidden_of, quarter)
        last = (normed_of(sum2_ref[...])[0] * vec_ref[4] + vec_ref[5]).astype(BF16)
        memory_ref[...] = last


def encoder_forward(flag, mixed, stream, out_weight, vectors, ff_packs, bias):
    rows, width = stream.shape
    hidden = 4 * ff_packs[0].shape[1]
    operands = (flag, mixed, stream, out_weight, vectors, *ff_packs, bias)
    return pl.pallas_call(
        encoder_forward_kernel,
        grid_spec=pltpu.PrefetchScalarGridSpec(
            num_scalar_prefetch=1,
            grid=(rows // TB,),
            in_specs=[tokens(width), tokens(width), fixed(out_weight.shape), fixed(vectors.shape)]
            + [anywhere()] * len(ff_packs)
            + [fixed(bias.shape)],
            out_specs=[
                tokens(width), tokens(width), tokens(hidden, 0), tokens(hidden, 0), tokens(width, 0), tokens(width, 0)
            ],
            scratch_shapes=ff_scratch(ff_packs),
        ),
        out_shape=[
            jax.ShapeDtypeStruct((rows, width), F32),
            jax.ShapeDtypeStruct((rows, width), BF16),
            jax.ShapeDtypeStruct((rows, hidden), BF16),
            jax.ShapeDtypeStruct((rows, hidden), BF16),
            jax.ShapeDtypeStruct((rows, width), F32),
            jax.ShapeDtypeStruct((rows, width), BF16),
        ],
        compiler_params=params(),
        cost_estimate=cost(2 * rows * width * (width + 2 * hidden), 20 * rows * width),
        name="encoder_forward",
    )(*operands)


def decoder_kernel(
    flag_ref, mixed_ref, sum1_ref, x_ref, cot_ref, g_in, h_in, memory_in,
    out_ref, vec_ref, cvec_ref, ff0, ff1, ff2, ff3, bias_ref,
    result_ref, g_ref, z_ref, du_ref, df_ref, dcross_ref, dmixed_ref, dh_ref, dlast_ref, vgrad_ref, bgrad_ref,
    weights_ref, sems, slope_ref, total_ref,
):
    width = x_ref.shape[1]
    hidden = ff0.shape[1]
    wait = fetch_packs((ff0, ff1, ff2, ff3), weights_ref, sems, flag_ref[0] == 1)

    @pl.when(pl.program_id(0) == 0)
    def _():
        vgrad_ref[...] = jnp.zeros(vgrad_ref.shape, F32)
        bgrad_ref[...] = jnp.zeros(bgrad_ref.shape, F32)

    @pl.when(flag_ref[0] == 0)
    def _():
        result_ref[...] = memory_in[...]
        g_ref[...] = g_in[...]
        z_ref[...] = h_in[...]

    @pl.when(flag_ref[0] == 1)
    def _():
        stream = x_ref[...].astype(F32)
        first = normed_of(sum1_ref[...])[0] * vec_ref[2] + vec_ref[3]
        mixed = mixed_ref[...]
        crossed = dot(mixed, out_ref[...]) + cvec_ref[2:3, :]
        normed_c, inverse_c = normed_of(first + crossed)
        second = normed_c * cvec_ref[3:4, :] + cvec_ref[4:5, :]
        second_low = second.astype(BF16)
        z_ref[...] = second_low
        total_ref[...] = second + stream + vec_ref[1]
        wait()

        def hidden_of(index, columns):
            return dot(z_ref[...], weights_ref[index, :width, columns]) + bias_ref[index:index + 1, columns]

        def quarter(index, columns, pre):
            value, slope = gelu_parts(pre)
            value = value.astype(BF16)
            lanes = piece_lanes(index, columns, hidden)
            g_ref[:, lanes] = value
            slope_ref[:, lanes] = slope.astype(BF16)
            below = slice(width + columns.start, width + columns.stop)
            total_ref[...] = total_ref[...] + dot(value, weights_ref[index, below, :])

        over_pieces(hidden, hidden_of, quarter)
        normed, inverse = normed_of(total_ref[...])
        result_ref[...] = (normed * vec_ref[4] + vec_ref[5]).astype(BF16)
        grad = cot_ref[...].astype(F32)
        grad_last = norm_back(grad, normed, inverse, vec_ref[4])
        dlast_ref[...] = grad_last
        grad_ffn = grad_last.astype(BF16)
        df_ref[...] = grad_ffn
        total_ref[...] = grad_last

        def value_grad_of(index, columns):
            return dot_t(df_ref[...], weights_ref[index, width + columns.start:width + columns.stop, :])

        def quarter_back(index, columns, grad_value):
            lanes = piece_lanes(index, columns, hidden)
            grad_pre = (grad_value * slope_ref[:, lanes].astype(F32)).astype(BF16)
            du_ref[:, lanes] = grad_pre
            bgrad_ref[index:index + 1, columns] += column_sum(grad_pre)
            total_ref[...] = total_ref[...] + dot_t(grad_pre, weights_ref[index, :width, columns])

        over_pieces(hidden, value_grad_of, quarter_back)
        grad_second = total_ref[...]
        grad_cross = norm_back(grad_second, normed_c, inverse_c, cvec_ref[3:4, :])
        dh_ref[...] = grad_cross
        cross_low = grad_cross.astype(BF16)
        dcross_ref[...] = cross_low
        dmixed_ref[...] = dot_t(cross_low, out_ref[...]).astype(BF16)
        vgrad_ref[1:2, :] += column_sum(grad_ffn)
        vgrad_ref[4:5, :] += column_sum(grad * normed)
        vgrad_ref[5:6, :] += column_sum(grad)
        vgrad_ref[6:7, :] += column_sum(cross_low)
        vgrad_ref[7:8, :] += column_sum(grad_second * normed_c)
        vgrad_ref[8:9, :] += column_sum(grad_second)


def decoder_step(flag, mixed, sum1, stream, cot, g_in, h_in, memory_in, out_weight, vectors, cvec, ff_packs, bias):
    rows, width = stream.shape
    hidden = g_in.shape[1]
    return pl.pallas_call(
        decoder_kernel,
        grid_spec=pltpu.PrefetchScalarGridSpec(
            num_scalar_prefetch=1,
            grid=(rows // TB,),
            in_specs=[
                tokens(width, 1), tokens(width, 1), tokens(width, 1), tokens(width, 1), tokens(hidden, 0),
                tokens(width, 0), tokens(width, 0), fixed(out_weight.shape), fixed(vectors.shape), fixed(cvec.shape),
            ]
            + [anywhere()] * len(ff_packs)
            + [fixed(bias.shape)],
            out_specs=[
                tokens(width), tokens(hidden), tokens(width), tokens(hidden, 1), tokens(width, 1), tokens(width, 1),
                tokens(width, 1), tokens(width, 1), tokens(width, 1), fixed((16, width)), fixed(bias.shape),
            ],
            scratch_shapes=ff_scratch(ff_packs) + [pltpu.VMEM((TB, hidden), BF16), pltpu.VMEM((TB, width), F32)],
        ),
        out_shape=[
            jax.ShapeDtypeStruct((rows, width), BF16),
            jax.ShapeDtypeStruct((rows, hidden), BF16),
            jax.ShapeDtypeStruct((rows, width), BF16),
            jax.ShapeDtypeStruct((rows, hidden), BF16),
            jax.ShapeDtypeStruct((rows, width), BF16),
            jax.ShapeDtypeStruct((rows, width), BF16),
            jax.ShapeDtypeStruct((rows, width), BF16),
            jax.ShapeDtypeStruct((rows, width), F32),
            jax.ShapeDtypeStruct((rows, width), F32),
            jax.ShapeDtypeStruct((16, width), F32),
            jax.ShapeDtypeStruct(bias.shape, F32),
        ],
        compiler_params=params(),
        cost_estimate=cost(2 * rows * width * (2 * width + 4 * hidden), 40 * rows * width),
        name="decoder_step",
    )(flag, mixed, sum1, stream, cot, g_in, h_in, memory_in, out_weight, vectors, cvec, *ff_packs, bias)


def backward_kernel(
    flag_ref, cot_ref, dmem_ref, sum1_ref, sum2_ref, slope_ref,
    dh_in, dq_in, dlast_in, du_in, df_in, vgrad_in, bgrad_in,
    out_ref, cross_ref, vec_ref, ff0, ff1, ff2, ff3,
    du_ref, df_ref, da_ref, dmixed_ref, dres_ref, vgrad_ref, bgrad_ref, dfirst_ref, weights_ref, sems,
):
    width = cot_ref.shape[1]
    hidden = ff0.shape[1]
    wait = fetch_packs((ff0, ff1, ff2, ff3), weights_ref, sems, flag_ref[0] == 0)
    at_start = pl.program_id(0) == 0
    is_dec = flag_ref[0] == 1

    @pl.when(at_start & is_dec)
    def _():
        vgrad_ref[...] = vgrad_in[...]
        bgrad_ref[...] = bgrad_in[...]

    @pl.when(at_start & jnp.logical_not(is_dec))
    def _():
        vgrad_ref[...] = jnp.zeros(vgrad_ref.shape, F32)
        bgrad_ref[...] = jnp.zeros(bgrad_ref.shape, F32)

    @pl.when(is_dec)
    def _():
        du_ref[...] = du_in[...]
        df_ref[...] = df_in[...]
        dres_ref[...] = dlast_in[...]
        dfirst_ref[...] = dh_in[...] + dot_t(dq_in[...], cross_ref[...])

    @pl.when(jnp.logical_not(is_dec))
    def _():
        grad = cot_ref[...].astype(F32) + dmem_ref[...].astype(F32)
        normed, inverse = normed_of(sum2_ref[...])
        grad_last = norm_back(grad, normed, inverse, vec_ref[4])
        dres_ref[...] = grad_last
        grad_ffn = grad_last.astype(BF16)
        df_ref[...] = grad_ffn
        dfirst_ref[...] = grad_last
        wait()

        def value_grad_of(index, columns):
            return dot_t(df_ref[...], weights_ref[index, width + columns.start:width + columns.stop, :])

        def quarter_back(index, columns, grad_value):
            lanes = piece_lanes(index, columns, hidden)
            grad_pre = (grad_value * slope_ref[:, lanes].astype(F32)).astype(BF16)
            du_ref[:, lanes] = grad_pre
            bgrad_ref[index:index + 1, columns] += column_sum(grad_pre)
            dfirst_ref[...] = dfirst_ref[...] + dot_t(grad_pre, weights_ref[index, :width, columns])

        over_pieces(hidden, value_grad_of, quarter_back)
        vgrad_ref[1:2, :] += column_sum(grad_ffn)
        vgrad_ref[4:5, :] += column_sum(grad * normed)
        vgrad_ref[5:6, :] += column_sum(grad)

    grad_first = dfirst_ref[...]
    normed, inverse = normed_of(sum1_ref[...])
    grad_in = norm_back(grad_first, normed, inverse, vec_ref[2])
    low = grad_in.astype(BF16)
    da_ref[...] = low
    dmixed_ref[...] = dot_t(low, out_ref[...]).astype(BF16)
    dres_ref[...] = dres_ref[...] + grad_in
    vgrad_ref[0:1, :] += column_sum(low)
    vgrad_ref[2:3, :] += column_sum(grad_first * normed)
    vgrad_ref[3:4, :] += column_sum(grad_first)


def backward_step(
    flag, cot, dmem, sum1, sum2, slope, dh, dq, dlast, du, df, vgrad, bgrad, out_weight, cross_query, vectors, ff_packs
):
    rows, width = cot.shape
    hidden = du.shape[1]
    return pl.pallas_call(
        backward_kernel,
        grid_spec=pltpu.PrefetchScalarGridSpec(
            num_scalar_prefetch=1,
            grid=(rows // TB,),
            in_specs=[
                tokens(width, 0), tokens(width, 0), tokens(width), tokens(width, 0), tokens(hidden, 0),
                tokens(width, 1), tokens(width, 1), tokens(width, 1), tokens(hidden, 1), tokens(width, 1),
                fixed(vgrad.shape), fixed(bgrad.shape),
                fixed(out_weight.shape), fixed(cross_query.shape), fixed(vectors.shape),
            ]
            + [anywhere()] * len(ff_packs),
            out_specs=[
                tokens(hidden), tokens(width), tokens(width), tokens(width), tokens(width),
                fixed(vgrad.shape), fixed(bgrad.shape),
            ],
            scratch_shapes=[pltpu.VMEM((TB, width), F32)] + ff_scratch(ff_packs),
        ),
        out_shape=[
            jax.ShapeDtypeStruct((rows, hidden), BF16),
            jax.ShapeDtypeStruct((rows, width), BF16),
            jax.ShapeDtypeStruct((rows, width), BF16),
            jax.ShapeDtypeStruct((rows, width), BF16),
            jax.ShapeDtypeStruct((rows, width), F32),
            jax.ShapeDtypeStruct(vgrad.shape, F32),
            jax.ShapeDtypeStruct(bgrad.shape, F32),
        ],
        compiler_params=params(),
        cost_estimate=cost(2 * rows * width * (width + 2 * hidden), 40 * rows * width),
        name="backward_step",
    )(
        flag, cot, dmem, sum1, sum2, slope, dh, dq, dlast, du, df, vgrad, bgrad,
        out_weight, cross_query, vectors, *ff_packs,
    )


def input_kernel(dres_ref, *refs):
    *parts, weight_ref, dx_ref = refs
    total = dres_ref[...]
    at = 0
    for part in parts:
        wide = part.shape[1]
        total = total + dot_t(part[...], weight_ref[:, at:at + wide])
        at += wide
    dx_ref[...] = total.astype(BF16)


def input_step(dres, parts, weight):
    rows, width = dres.shape
    block = 256
    spec = lambda v: pl.BlockSpec((block, v.shape[1]), lambda i: (i, 0))
    return pl.pallas_call(
        input_kernel,
        grid=(rows // block,),
        in_specs=[spec(v) for v in (dres, *parts)] + [fixed(weight.shape)],
        out_specs=spec(dres),
        out_shape=jax.ShapeDtypeStruct((rows, width), BF16),
        compiler_params=params(SMALL_LIMIT),
        cost_estimate=cost(6 * rows * width * width, 12 * rows * width),
        name="input_step",
    )(dres, *parts, weight)


def finish_kernel(attn_ref, qkv_ref, out_ref, bias_ref, hidden_ref, vectors_ref):
    width, lane = qkv_ref.shape[1:]
    for index in range(3):
        qkv_ref[index] = attn_ref[index * width:(index + 1) * width, :].astype(F32)
    for index in range(width // lane):
        at = 3 * width + index * lane
        out_ref[:, index * lane:(index + 1) * lane] = attn_ref[at:at + lane, :].astype(F32)
    rows = attn_ref[4 * width:, :].astype(F32)
    bias_ref[...] = rows[0:2]
    for index in range(hidden_ref.shape[1] // lane):
        hidden_ref[:, index * lane:(index + 1) * lane] = rows[2 + index:3 + index]
    count = width // lane
    for index in range(6):
        for part in range(count):
            row = 16 + index * count + part
            vectors_ref[index, :, part * lane:(part + 1) * lane] = rows[row:row + 1]


def finish_feed_forward_kernel(ff_ref, ffin_ref, ffout_ref):
    width = ffin_ref.shape[0]
    ffin_ref[...] = ff_ref[:width, :].astype(F32)
    ffout_ref[...] = ff_ref[width:, :].astype(F32)


def finish_feed_forward(ff_total, hidden):
    width = ff_total.shape[1]
    shapes = [(width, hidden), (hidden, width)]
    return pl.pallas_call(
        finish_feed_forward_kernel,
        grid=(1,),
        in_specs=[fixed(ff_total.shape)],
        out_specs=[fixed(shape) for shape in shapes],
        out_shape=[jax.ShapeDtypeStruct(shape, F32) for shape in shapes],
        compiler_params=params(SMALL_LIMIT),
        cost_estimate=cost(0, 20 * width * width),
        name="finish_feed_forward",
    )(ff_total)


def finish(attn_total, width, hidden):
    lane = attn_total.shape[1]
    shapes = [(3, width, lane), (lane, width), (2, lane), (1, hidden), (6, 1, width)]
    return pl.pallas_call(
        finish_kernel,
        grid=(1,),
        in_specs=[fixed(attn_total.shape)],
        out_specs=[fixed(shape) for shape in shapes],
        out_shape=[jax.ShapeDtypeStruct(shape, F32) for shape in shapes],
        compiler_params=params(SMALL_LIMIT),
        cost_estimate=cost(0, 20 * width * width),
        name="finish",
    )(attn_total)


def flipped(value, bits, section=None):
    count = lax.axis_size("tensor")
    if section is None:
        return lax.ppermute(value, "tensor", [(t, t ^ bits) for t in range(count)])
    base = section * count
    return lax.ppermute(value, ("pipe", "tensor"), [(base + t, base + (t ^ bits)) for t in range(count)])


def across(value, source, active):
    count = lax.axis_size("tensor")
    other = 1 - source
    pairs = [(source * count + t, other * count + t) for t in range(active)]
    return lax.ppermute(value, ("pipe", "tensor"), pairs)


def plus(own, received):
    return (own.astype(F32) + received.astype(F32)).astype(BF16)


def along_dp(part, level, section=None):
    count = lax.axis_size("dp")
    if section is None:
        return lax.ppermute(part, "dp", [(i, i ^ (1 << level)) for i in range(count)])
    base = section * count
    return lax.ppermute(part, ("pipe", "dp"), [(base + i, base + (i ^ (1 << level))) for i in range(count)])


def summed_whole(value, level, section=None, behind=()):
    return plus(after(value, *behind), along_dp(value, level, section))


def dp_bit(level):
    return lax.shift_right_logical(lax.axis_index("dp"), level) & 1


def halved(value, level, section=None, behind=()):
    rows = value.shape[0] // 2
    mine = dp_bit(level)
    got = along_dp(lax.dynamic_slice_in_dim(value, (1 - mine) * rows, rows, 0), level, section)
    return plus(lax.dynamic_slice_in_dim(after(value, *behind), mine * rows, rows, 0), got)


def doubled(value, level, section=None, behind=()):
    other = along_dp(value, level, section)
    upper = dp_bit(level) == 1
    value = after(value, *behind)
    return jnp.concatenate([jnp.where(upper, other, value), jnp.where(upper, value, other)], 0)


def after(value, *others):
    return lax.optimization_barrier((value, *others))[0]


def to_rows(shard):
    count = lax.axis_size("tensor")
    shard = jnp.pad(shard, ((0, count - shard.shape[0]), (0, 0), (0, 0)))
    out = lax.all_to_all(shard, "tensor", 0, 0, tiled=True)
    return out.reshape(count * shard.shape[1], shard.shape[2])


def from_rows(row, row_count):
    count = lax.axis_size("tensor")
    parts = row.reshape(count, row.shape[0] // count, row.shape[1])
    return lax.all_to_all(parts, "tensor", 0, 0, tiled=True)[:row_count]


def shards(
    inputs, cotangent, segments, pads, self_qkv, self_bias, self_out, ff_in, ff_bias, ff_out, vectors,
    cross_q, cross_kv, cross_out, cross_small, cross_gain,
):
    section = lax.axis_index("pipe").astype(jnp.int32)
    place = lax.axis_index("tensor").astype(jnp.int32)
    count = lax.axis_size("tensor")
    row_count = inputs.shape[1]
    decoder = section == 1
    flag, place_flag = section[None], place[None]
    width = inputs.shape[3]
    lane = self_qkv.shape[3]
    hidden = ff_in.shape[2]
    half = width // 2
    row = jnp.minimum(place, row_count - 1)

    attn_own, cross_half = first_packs(
        jnp.transpose(self_qkv[0], (1, 0, 2)), self_out[0], self_bias[0], ff_bias, cross_q,
        jnp.transpose(cross_kv, (1, 0, 2)), cross_out, cross_small, cross_gain[None],
    )
    attn_far, attn_near = flipped(attn_own, 2), flipped(attn_own, 1)
    stream = to_rows(after(inputs[0], attn_own))
    slots = jnp.concatenate(
        [
            lax.dynamic_index_in_dim(segments, row, 1, False),
            lax.dynamic_slice_in_dim(pads[0], row, 1, 0),
        ],
        0,
    )
    attn_packs = [attn_own, attn_near, attn_far, flipped(attn_far, 1)]
    other_half = across(cross_half, 0, count)
    ff_own = after(jnp.concatenate([ff_in[0], ff_out[0]], 0), stream, attn_far)
    ff_far, ff_near = flipped(ff_own, 2), flipped(ff_own, 1)
    vector_rows = jnp.transpose(vectors, (1, 0, 2))

    qkv, qkv_weight, out_weight, hidden_bias, own_code, key_code, target_code, source_code, self_bounds, cross_bounds = (
        query_key_value(flag, stream, slots, attn_packs)
    )
    parts = ((qkv, 0), (qkv, 1), (qkv, 2))
    self_codes, cross_codes = (own_code, key_code), (target_code, source_code)
    mixed, totals = attend_forward(self_bounds, self_codes, width, *parts)
    cross_own = jnp.concatenate([after(other_half, mixed), cross_half], 0)
    cross_far, cross_near = flipped(cross_own, 2, 1), flipped(cross_own, 1, 1)
    ff_packs = [ff_own, ff_near, ff_far, flipped(after(ff_far, cross_own), 1)]
    sum1, first_low, g_enc, slope, sum2, memory = encoder_forward(
        flag, mixed, stream, out_weight, vector_rows, ff_packs, hidden_bias
    )
    memory_in = across(memory, 0, row_count)
    cross_packs = [cross_own, cross_near, cross_far, flipped(after(cross_far, memory), 1, 1)]
    cot_row = to_rows(after(cotangent[0], memory))

    cross_query, cross_pair, cross_out_weight, cvec = cross_unpack(place_flag, cross_packs)
    cross_made = cross_project(first_low, memory_in, cross_query, cross_pair, cvec)
    cross_parts = ((cross_made, 0), (cross_made, 1), (cross_made, 2))
    cross_mixed, cross_totals = attend_forward(cross_bounds, cross_codes, width, *cross_parts)
    result, g_all, z_all, du_dec, df_dec, dcross, dcross_mixed, dh_dec, dlast_dec, vgrad_dec, bgrad_dec = decoder_step(
        flag, cross_mixed, sum1, stream, cot_row, g_enc, first_low, memory,
        cross_out_weight, vector_rows, cvec, ff_packs, hidden_bias,
    )
    dq_cross, dk_cross, dv_cross, dmemory = attend_backward(
        cross_bounds, cross_codes, *cross_parts, dcross_mixed, cross_totals, cross_pair
    )
    dmemory_in = across(dmemory, 1, row_count)
    cross_grads = attention_grads(
        True, place_flag, first_low, memory_in, (after(dq_cross, dmemory), dk_cross, dv_cross), cross_mixed, dcross,
        vgrad_dec, bgrad_dec, lane,
    )
    cross_far = plus(after(cross_grads[2], dmemory_in), flipped(cross_grads[3], 1, 1))
    cross_got = flipped(cross_grads[1], 1, 1)

    du_all, df_all, da, dmixed, dres, vgrad, bgrad = backward_step(
        flag, cot_row, dmemory_in, sum1, sum2, slope, dh_dec, after(dq_cross, cross_far, cross_grads[1]), dlast_dec,
        du_dec, df_dec, vgrad_dec, bgrad_dec, out_weight, cross_query, vector_rows, ff_packs,
    )
    cross_near = plus(after(cross_grads[0], da), cross_got)
    cross_part = plus(cross_near, flipped(cross_far, 2, 1))
    levels = range(lax.axis_size("dp").bit_length() - 1)
    ff_third, ff_second = feed_forward_grads(after(z_all, cross_part), du_all, g_all, df_all, 3, hidden)
    ff_first, ff_zeroth = feed_forward_grads(after(z_all, ff_second), du_all, g_all, df_all, 1, hidden)
    ff_far = plus(after(ff_second, ff_zeroth), flipped(ff_third, 1))
    ff_near = plus(after(ff_zeroth, ff_far), flipped(ff_first, 1))
    dqkv = attend_backward(self_bounds, self_codes, *parts, after(dmixed, ff_near), totals)
    cross_total = halved(cross_part, 0, 1, (dqkv[0],))
    ff_part = plus(after(ff_near, dqkv[0], cross_total), flipped(ff_far, 2))
    attn_grads = attention_grads(
        False, place_flag, stream, stream, (after(dqkv[0], ff_part), *dqkv[1:]), mixed, da, vgrad, bgrad, lane
    )
    ff_total = halved(ff_part, 0, behind=(attn_grads[3],))
    for level in levels[1:]:
        cross_total = halved(cross_total, level, 1, (ff_total,))
    attn_far = plus(after(attn_grads[2], ff_total, cross_total), flipped(attn_grads[3], 1))
    attn_near = plus(after(attn_grads[0], attn_far), flipped(attn_grads[1], 1))
    dx = input_step(after(dres, attn_near), dqkv, qkv_weight)
    section_out = from_rows(after(result, dx), row_count)[None]
    for level in levels[1:]:
        ff_total = halved(ff_total, level, behind=(dx,))
    cross_total = doubled(cross_total, levels[-1], 1, (ff_total,))
    attn_part = plus(after(attn_near, ff_total, cross_total), flipped(attn_far, 2))
    for level in reversed(levels[:-1]):
        cross_total = doubled(cross_total, level, 1, (attn_part,))
    cross_other = across(cross_total, 1, count)
    ff_total = doubled(ff_total, levels[-1], behind=(attn_part, section_out, cross_total))
    attn_total = halved(attn_part, 0, behind=(ff_total,))
    input_grad = from_rows(after(dx, attn_total), row_count).astype(F32)[None]
    for level in levels[1:]:
        attn_total = halved(attn_total, level, behind=(cross_total,))
    for level in reversed(levels[:-1]):
        ff_total = doubled(ff_total, level, behind=(attn_total,))
    attn_total = doubled(attn_total, levels[-1], behind=(ff_total, input_grad))
    cross_total, cross_other = after((cross_total, cross_other), attn_total)

    own, other = cross_total.astype(F32), cross_other.astype(F32)

    def halves(at):
        return jnp.where(decoder, own[at + half:at + 2 * half], other[at:at + half])

    cross_pair_grad = jnp.stack([halves(width), halves(2 * width)], 1)
    cross_out_grad = jnp.transpose(halves(3 * width).reshape(half // lane, lane, lane), (1, 0, 2)).reshape(lane, half)
    own_rows, other_rows = (v[4 * width:4 * width + 5 * count].reshape(5, width) for v in (own, other))
    small_grad = jnp.where(decoder, jnp.stack([own_rows[2], own_rows[4]]), other_rows[:2])
    gain_grad = jnp.where(decoder, own_rows[3, half:], other_rows[3, :half])
    cross_first, cross_last = halves(0), (cross_pair_grad, cross_out_grad, small_grad, gain_grad)
    ffin_grad, ffout_grad = finish_feed_forward(ff_total, hidden)
    for level in reversed(levels[:-1]):
        attn_total = doubled(attn_total, level, behind=(cross_first, *cross_last, ffin_grad))
    qkv_grad, out_grad, bias_grad, hidden_grad, vectors_grad = finish(attn_total, width, hidden)
    return (
        section_out,
        input_grad,
        jnp.transpose(qkv_grad, (1, 0, 2))[None],
        bias_grad[None],
        out_grad[None],
        ffin_grad[None],
        hidden_grad,
        ffout_grad[None],
        jnp.transpose(vectors_grad, (1, 0, 2)),
        cross_first,
        *cross_last,
    )


def solution(mesh):
    token_spec = P("pipe", "dp", "tensor", None)
    weights = (
        P("pipe", None, None, "tensor"),
        P("pipe", None, "tensor"),
        P("pipe", "tensor", None),
        P("pipe", None, "tensor"),
        P("pipe", "tensor"),
        P("pipe", "tensor", None),
        P("pipe", None, None),
        P("pipe", "tensor"),
        P("pipe", None, "tensor"),
        P("tensor", "pipe"),
        P("pipe", None),
        P("pipe"),
    )
    return jax.shard_map(
        shards,
        mesh=mesh,
        in_specs=(token_spec, token_spec, P(None, "dp", None), P("pipe", "dp", None)) + weights,
        out_specs=(token_spec, token_spec) + weights,
        check_vma=False,
    )
```
